256 devices in a mesh: layer: 8 (over x, core), gx: 8 (over z), gy: 4 (over y).
Axes of the slice: x: 4, y: 4, z: 8, core: 2. Of those that a mesh axis runs over, the one named last changes fastest.
Arguments:
- pressure: float32 [64, 512, 1024], P('layer', 'gx', 'gy'), may hold values from -6 to 6
- source: float32 [64, 512, 1024], P('layer', 'gx', 'gy'), may hold values from -6 to 6
- perm_x: float32 [64, 512, 1024], P('layer', 'gx', 'gy'), may hold values from 0.05 to 0.5
- perm_y: float32 [64, 512, 1024], P('layer', 'gx', 'gy'), may hold values from 0.05 to 0.5
- line_inverse: float32 [8, 8, 8, 512, 1024], P('layer', None, None, 'gx', 'gy'), may hold values from -0.98 to 1.2
- robin_below: float32 [8, 512, 1024], P('layer', 'gx', 'gy'), may hold values from -6 to 6
- tile_count: int32 [8, 32], P('layer', ('gx', 'gy')), may hold values from 1 to 48, 512 in all within a row
- perf_owner: int32 [8, 1536, 1], P('layer', ('gx', 'gy')), may hold values from 0 to 31; in each aligned block of 48 rows (0 to 47, 48 to 95, ..., all dimensions but the last counted through in order) at most 2 rows name the same one
- perf_well: int32 [8, 1536], P('layer', ('gx', 'gy')), may hold values from 0 to 7
- perf_column: int32 [8, 1536], P('layer', ('gx', 'gy')), may hold values from 0 to 16383
- perf_index: float32 [8, 1536, 8], P('layer', ('gx', 'gy')), may hold values from 0.2 to 2
- well_rate: float32 [8, 256], P('layer', ('gx', 'gy')), may hold values from -8 to 8
Outputs:
- pressure_out: float32 [64, 512, 1024], P('layer', 'gx', 'gy')
- perf_flow: float32 [8, 1536, 8], P('layer', ('gx', 'gy'))
The draws below stay inside these ranges and needn't reach their ends.
Inputs may be any that keep to these rules, and one draw needn't show every extreme that they name: `tile_count`: live slots of a tile are its first ones; some tile of every group has all 48 live. `perf_owner`: among the 48 slots of one tile at most 2 name one owner.
All inputs are finite; a program needn't handle non-finite values.
Results may differ from the reference program's by a relative error of at most 0.00018.
Values sent between devices are 32-bit elements; how exact they have to be, the bound alone decides.
No kernel may reach another device: no remote copies, remote signals or barrier semaphores. Data moves between devices by JAX's collectives and lax.ppermute only.
A program may use at most 64 MiB of HBM per device.

```python
import math
import jax
import jax.numpy as jnp
import numpy as np
from jax import lax

LZ = 8
CX = 64
CY = 256
ITERS = 2
SLOTS = 48
WO = 8
GROUPS = 8
TILES = 32
CAP = 2
NZ = 64
NX = 512
NY = 1024
N_GY = 4


def draw_line_inverse(key, part):
    keys = jax.random.split(key, 9)
    shape = (GROUPS, LZ, LZ, NX, NY)
    layer_sheet = (GROUPS, NX, NY)
    spread = jax.random.uniform(keys[0], shape, jnp.float32, -0.25, 0.25)
    diag_vals = jnp.exp(jax.random.uniform(keys[1], (GROUPS, LZ, NX, NY), jnp.float32, jnp.log(0.3), jnp.log(1.2)))
    eye_mask = (jnp.arange(LZ)[:, None] == jnp.arange(LZ)[None, :]).astype(jnp.float32)[None, :, :, None, None]
    matrix = spread * (1.0 - eye_mask) + eye_mask * diag_vals[:, :, None, :, :]
    slow_low = 0.2 ** (1.0 / max(GROUPS - 1, 1))
    slow_share = 0.5
    corners = []
    for which in range(2):
        gradual_indicator = jax.random.bernoulli(keys[2 + 3 * which], slow_share, layer_sheet)
        subset_part = jax.random.split(keys[3 + 3 * which], 3)
        gradual_amplitude = jax.random.uniform(subset_part[0], layer_sheet, jnp.float32, slow_low, 0.98)
        rapid_amplitude = jax.random.uniform(subset_part[1], layer_sheet, jnp.float32, 0.15, 0.45)
        spike_indicator = jax.random.bernoulli(subset_part[2], 0.15, layer_sheet)
        sign_flag = jax.random.bernoulli(keys[4 + 3 * which], 0.8, layer_sheet)
        amplitude_level = jnp.where(gradual_indicator, gradual_amplitude, rapid_amplitude) * jnp.where(spike_indicator, 0.5, 1.0)
        corners.append(amplitude_level * jnp.where(sign_flag, 1.0, -1.0))
    matrix = matrix.at[:, LZ - 1, 0].set(corners[0])
    matrix = matrix.at[:, 0, LZ - 1].set(corners[1])
    return matrix.astype(jnp.float32)


def plant(values, rng, smallest, top_value):
    extent = values.shape
    spot = [jax.random.randint(jax.random.fold_in(rng, axis), (), 0, extent[axis]) for axis in range(len(extent))]
    values = values.at[tuple(spot)].set(smallest)
    longest = extent.index(max(extent))
    spot[longest] = (spot[longest] + 1) % extent[longest]
    return values.at[tuple(spot)].set(top_value)


def levels(own_key, dims, shards, smallest, high):
    def one(position, blocks):
        steps = jax.random.uniform(jax.random.fold_in(jax.random.fold_in(own_key, 6), position), (blocks,), jnp.float32, smallest / len(shards), high / len(shards))
        return jnp.repeat(jnp.exp(steps), dims[position] // blocks).reshape((-1,) + (1,) * (len(dims) - position - 1))

    factor_of = one(*shards[0])
    for cut in shards[1:]:
        factor_of = factor_of * one(*cut)
    return factor_of


def length_profile(count, total, most, slope):
    portions = [(1 << 20) // math.isqrt(standing ** slope) + 1 for standing in range(2, count + 1)]
    rest, given = total - most - (count - 1), [1] * (count - 1)
    while rest > 0:
        free = [i for i in range(count - 1) if given[i] < most]
        mass, budget = sum([portions[i] for i in free]), rest
        for i in free:
            addition = min(most - given[i], max(1, budget * portions[i] // mass), rest)
            given[i] = given[i] + addition
            rest = rest - addition
    return np.array([most] + given)


def ragged_sizes(key, count, total, reach, slope):
    if count == 2:
        one = jax.random.randint(key, (), max(1, total - reach), min(reach, total - 1) + 1)
        return jnp.stack([one, total - one])
    sizes = jnp.asarray(length_profile(count, total, reach, slope), jnp.int32)
    twos = (count - 1) // 2
    giver, taker = sizes[1:1 + 2 * twos:2], sizes[2:2 + 2 * twos:2]
    room = jnp.minimum(giver - 1, reach - taker)
    moved = jax.random.randint(jax.random.fold_in(key, 1), (twos,), 0, 1 << 20) % (room + 1)
    sizes = sizes.at[1:1 + 2 * twos:2].set(giver - moved).at[2:2 + 2 * twos:2].set(taker + moved)
    return sizes[jax.random.permutation(jax.random.fold_in(key, 2), count)]


def assign_block(rng, own, number, rows, amount, top, bound, lean):
    order = jax.random.permutation(rng, amount)
    heavy_load, usual = portions_of(amount, rows * top, bound, lean, True), portions_of(amount, rows * top, bound, lean, False)
    places = jnp.arange(amount)

    def named(sizes, offset_by):
        used = int((sizes > 0).sum())
        fixed = max(1, used // 4)
        moved = fixed + (places - fixed + offset_by * (used - fixed)) % max(1, amount - fixed)
        return jnp.zeros((amount,), jnp.int32).at[order[jnp.where(places < fixed, places, moved)]].set(jnp.asarray(sizes, jnp.int32))

    sizes = jnp.where(number % 4 == 0, named(heavy_load, number // 4), named(usual, number - number // 4 - 1))
    mixed = jax.random.permutation(jax.random.fold_in(own, 3), amount)
    giver, sink = mixed[0:amount // 2 * 2:2], mixed[1:amount // 2 * 2:2]
    slack = jnp.minimum(sizes[giver] - 1, bound - sizes[sink]) // 2
    slack = jnp.where((giver == order[0]) | (sink == order[0]) | (sizes[sink] == 0), 0, jnp.maximum(slack, 0))
    moved = jax.random.randint(jax.random.fold_in(own, 4), (amount // 2,), 0, 1 << 20) % (slack + 1)
    sizes = sizes.at[giver].add(-moved).at[sink].add(moved)
    labels = jnp.searchsorted(jnp.cumsum(sizes), jnp.arange(rows * top), side="right").astype(jnp.int32)
    grid = labels.reshape(top, rows).T
    grid = grid[jax.random.permutation(jax.random.fold_in(own, 1), rows)]
    offset_by = jax.random.randint(jax.random.fold_in(own, 2), (rows, 1), 0, top)
    return jnp.take_along_axis(grid, (jnp.arange(top)[None, :] + offset_by) % top, axis=1)


def portions_of(count, total, most, skew, full):
    loads = [(1 << 20) // math.isqrt(standing ** skew) + 1 for standing in range(1, count + 1)]
    largest = most if full else min(most, max(-(-total // count), total * loads[0] // sum(loads)))
    least = 1 if total - largest >= count - 1 else 0
    given, spare = [largest] + [least] * (count - 1), total - largest - least * (count - 1)
    while spare > 0:
        movable = [i for i in range(1, count) if given[i] < largest] or [i for i in range(1, count) if given[i] < most]
        pool, remaining = sum([loads[i] for i in movable]), spare
        for i in movable:
            addition = min(most - given[i], max(1, remaining * loads[i] // pool), spare)
            given[i] = given[i] + addition
            spare = spare - addition
    return np.array(given)


def centred(stream_key, shape, width, limit, shards=(), kind=jnp.bfloat16):
    entries = width * jax.random.normal(stream_key, shape, jnp.float32)
    if shards:
        entries = entries * levels(stream_key, shape, shards, -0.22, 0.18)
    return jnp.clip(entries, -limit, limit).astype(kind)


def setup_inputs(seed: int = 0) -> dict:
    key_list = jax.random.split(jax.random.key(seed), 13)
    pressure = centred(key_list[0], (NZ, NX, NY), 1.0, 6.0, ((0, 8), (1, 8), (2, 4)), jnp.float32)
    source = centred(key_list[1], (NZ, NX, NY), 1.0, 6.0, ((0, 8), (1, 8), (2, 4)), jnp.float32)
    perm_x = jnp.clip(jnp.exp(math.log(0.5) - 2.3025851 * jax.random.uniform(key_list[2], (NZ, NX, NY), jnp.float32) ** levels(key_list[2], (NZ, NX, NY), ((0, 8), (1, 8), (2, 4)), -0.2, 0.2)), 0.05, 0.5)
    perm_y = jnp.clip(jnp.exp(math.log(0.5) - 2.3025851 * jax.random.uniform(key_list[3], (NZ, NX, NY), jnp.float32) ** levels(key_list[3], (NZ, NX, NY), ((0, 8), (1, 8), (2, 4)), -0.2, 0.2)), 0.05, 0.5)
    line_inverse = draw_line_inverse(jax.random.fold_in(key_list[12], 71), 0)
    robin_below = centred(key_list[5], (GROUPS, NX, NY), 1.0, 6.0, ((0, 8), (1, 8), (2, 4)), jnp.float32)
    tile_count = jax.vmap(lambda own: ragged_sizes(own, TILES, TILES * SLOTS // 3, SLOTS, 2))(jax.random.split(key_list[6], GROUPS)).reshape((GROUPS, TILES)).astype(jnp.int32)
    perf_owner_keys = jax.random.split(jax.random.fold_in(key_list[7], 1), GROUPS * (TILES * SLOTS) // SLOTS)
    perf_owner_turns = jax.random.permutation(jax.random.fold_in(key_list[7], 3), GROUPS * (TILES * SLOTS) // SLOTS)
    perf_owner = jax.vmap(lambda own, number: assign_block(jax.random.fold_in(key_list[7], 2), own, number, SLOTS, TILES, 1, CAP, 2))(perf_owner_keys, perf_owner_turns).reshape((GROUPS, TILES * SLOTS, 1))
    perf_well = plant(jax.random.randint(key_list[8], (GROUPS, TILES * SLOTS), 0, WO), jax.random.fold_in(key_list[8], 1), 0, WO - 1).astype(jnp.int32)
    perf_column = plant(jax.random.randint(key_list[9], (GROUPS, TILES * SLOTS), 0, CX * CY), jax.random.fold_in(key_list[9], 1), 0, (CX * CY) - 1).astype(jnp.int32)
    perf_index = jnp.clip(jnp.exp(math.log(2.0) - 2.3025851 * jax.random.uniform(key_list[10], (GROUPS, TILES * SLOTS, LZ), jnp.float32) ** levels(key_list[10], (GROUPS, TILES * SLOTS, LZ), ((0, 8), (1, 32)), -0.2, 0.2)), 0.2, 2.0)
    well_rate = centred(key_list[11], (GROUPS, TILES * WO), 2.0, 8.0, ((0, 8), (1, 32)), jnp.float32)
    return {"pressure": pressure, "source": source, "perm_x": perm_x, "perm_y": perm_y, "line_inverse": line_inverse, "robin_below": robin_below, "tile_count": tile_count, "perf_owner": perf_owner, "perf_well": perf_well, "perf_column": perf_column, "perf_index": perf_index, "well_rate": well_rate}


HIGHEST_PRECISION = lax.Precision.HIGHEST


def neighbours(padded_field, rock_x, rock_y, perm_x, perm_y):
    east_term = 0.5 * (perm_x + rock_x[:, 2:, 1:-1]) * padded_field[:, 2:, 1:-1]
    west_term = 0.5 * (perm_x + rock_x[:, :-2, 1:-1]) * padded_field[:, :-2, 1:-1]
    north_term = 0.5 * (perm_y + rock_y[:, 1:-1, 2:]) * padded_field[:, 1:-1, 2:]
    south_term = 0.5 * (perm_y + rock_y[:, 1:-1, :-2]) * padded_field[:, 1:-1, :-2]
    return (east_term + west_term) + (north_term + south_term)


def reference(pressure, source, perm_x, perm_y, line_inverse, robin_below, tile_count, perf_owner, perf_well, perf_column, perf_index, well_rate):
    group_total = GROUPS
    tile_total = TILES
    border = ((0, 0), (1, 1), (1, 1))
    rock_x = jnp.pad(perm_x, border)
    rock_y = jnp.pad(perm_y, border)
    live_slot = (jnp.arange(SLOTS).astype(jnp.int32)[None, None, :] < tile_count[:, :, None]).astype(jnp.float32)[..., None]
    tile_ids = jnp.arange(tile_total).astype(jnp.int32)
    column = perf_column.reshape(group_total, tile_total, SLOTS)
    cell_x = (tile_ids // N_GY)[None, :, None] * CX + column // CY
    cell_y = (tile_ids % N_GY)[None, :, None] * CY + column % CY
    full_shape = (group_total, tile_total, SLOTS, LZ)
    layer_ids = jnp.broadcast_to((jnp.arange(group_total)[:, None, None, None] * LZ + jnp.arange(LZ)[None, None, None, :]).astype(jnp.int32), full_shape)
    cell_x4 = jnp.broadcast_to(cell_x[..., None], full_shape)
    cell_y4 = jnp.broadcast_to(cell_y[..., None], full_shape)
    index_rows = perf_index.reshape(full_shape)
    well_ids = perf_owner.reshape(group_total, tile_total, SLOTS) * WO + perf_well.reshape(group_total, tile_total, SLOTS)
    group_ids = jnp.broadcast_to(jnp.arange(group_total).astype(jnp.int32)[:, None, None], well_ids.shape)
    field_now = pressure
    lower_data = robin_below
    slot_flow = jnp.zeros(full_shape, jnp.float32)
    for sweep_step in range(ITERS):
        lateral = neighbours(jnp.pad(field_now, border), rock_x, rock_y, perm_x, perm_y)
        at_slots = field_now[layer_ids, cell_x4, cell_y4]
        index_sum = jnp.zeros((group_total, tile_total * WO), jnp.float32).at[group_ids, well_ids].add(jnp.sum(index_rows * live_slot, axis=-1))
        weighted_sum = jnp.zeros((group_total, tile_total * WO), jnp.float32).at[group_ids, well_ids].add(jnp.sum(index_rows * at_slots * live_slot, axis=-1))
        bottom_hole = (well_rate + weighted_sum) / (index_sum + 1.0)
        slot_flow = index_rows * (bottom_hole[group_ids, well_ids][..., None] - at_slots) * live_slot
        well_term = jnp.zeros_like(field_now).at[layer_ids, cell_x4, cell_y4].add(slot_flow)
        rhs = (source + lateral) + well_term
        blocks = rhs.reshape(group_total, LZ, NX, NY)
        solved = jnp.einsum('gijxy,gjxy->gixy', line_inverse, blocks, precision=HIGHEST_PRECISION)
        upper_trace = jnp.zeros((NX, NY), jnp.float32)
        upper_list = [upper_trace]
        for group_id in range(group_total - 1):
            carried = (solved[group_id, LZ - 1] + line_inverse[group_id, LZ - 1, LZ - 1] * lower_data[group_id]) - lower_data[group_id]
            upper_trace = line_inverse[group_id, LZ - 1, 0] * upper_trace + carried
            upper_list.append(upper_trace)
        upper_all = jnp.stack(upper_list)
        lower_trace = jnp.zeros((NX, NY), jnp.float32)
        lower_list = [lower_trace for group_id in range(group_total)]
        for group_id in range(group_total - 1, 0, -1):
            carried = (solved[group_id, 0] + line_inverse[group_id, 0, 0] * upper_all[group_id]) - upper_all[group_id]
            lower_trace = line_inverse[group_id, 0, LZ - 1] * lower_trace + carried
            lower_list[group_id - 1] = lower_trace
        lower_data = jnp.stack(lower_list)
        updated = solved + line_inverse[:, :, 0] * upper_all[:, None] + line_inverse[:, :, LZ - 1] * lower_data[:, None]
        field_now = updated.reshape(NZ, NX, NY)
    return field_now, slot_flow.reshape(group_total, tile_total * SLOTS, LZ)
```

```python
import functools

import jax
import jax.numpy as jnp
from jax import lax
from jax.experimental import pallas as pl
from jax.experimental.pallas import tpu as pltpu
from jax.sharding import PartitionSpec as P

ITERS = 2
LZ = 8
CX = 64
CY = 256
SLOTS = 48
WELLS = 256
TILES = 32
GROUPS = 8
F32 = jnp.float32
VMEM = pl.BlockSpec(memory_space=pltpu.VMEM)
SMEM = pl.BlockSpec(memory_space=pltpu.SMEM)
ANY = pl.BlockSpec(memory_space=pl.ANY)


def shape(*dims):
    return jax.ShapeDtypeStruct(dims, F32)


def lane_ids(rows, lanes):
    return lax.broadcasted_iota(jnp.int32, (rows, lanes), 1)


def x_edges(ref, row, out, first):
    for l in range(LZ):
        out[first + l : first + l + 1, :] = ref[l * CX + row : l * CX + row + 1, :]


def y_edges(pieces):
    lanes = lane_ids(2 * CX, 128)
    packed = jnp.zeros((2 * CX, 128), F32)
    row = 0
    for ref, column in pieces:
        start = (column // 128) * 128
        for r in range(LZ // 2):
            block = ref[r * 2 * CX : (r + 1) * 2 * CX, start : start + 128]
            value = block[:, column - start : column - start + 1]
            packed = jnp.where(lanes == row, value, packed)
            row += 1
    return packed.T


def gather_slots(split_ref, column_ref):
    lanes = lane_ids(LZ, 128)
    found = jnp.zeros((LZ, 128), F32)
    for s in range(SLOTS):
        column = column_ref[0, s]
        x = column // CY
        y = column % CY
        half = y // 128
        lane = y % 128
        block = split_ref.at[half][pl.ds(x, LZ, stride=CX), :]
        value = jnp.sum(jnp.where(lanes == lane, block, 0.0), axis=1, keepdims=True)
        found = jnp.where(lanes == s, value, found)
    return found


def well_columns(rows):
    block = jnp.concatenate(rows + [jnp.zeros((8 - len(rows), 128), F32)], axis=0)
    turned = block.T
    return [turned[:, i : i + 1] for i in range(len(rows))]


def pad_lanes(value):
    return jnp.concatenate([value, jnp.zeros((value.shape[0], 128 - value.shape[1]), value.dtype)], axis=1)


def send_partials(out, values):
    for t in range(TILES):
        out[t] = values


def live_index(index_ref, count_ref):
    index = pad_lanes(index_ref[...])
    return jnp.where(lane_ids(LZ, 128) < count_ref[0, 0], index, 0.0)


def well_row(owner_ref, well_ref):
    return pad_lanes((owner_ref[...] * 8 + well_ref[...]).astype(F32))


def totals_by_well(column, well_column):
    ids = well_column[:SLOTS].astype(jnp.int32)
    halves = []
    for half in range(2):
        hit = ids == lane_ids(SLOTS, 128) + half * 128
        halves.append(jnp.sum(jnp.where(hit, column[:SLOTS], 0.0), axis=0, keepdims=True))
    return jnp.concatenate(halves, axis=0)


def own_rates(rate_ref):
    tile = lax.axis_index("gx") * 4 + lax.axis_index("gy")
    rate = rate_ref[...]
    tiled = jnp.concatenate([rate] * 16, axis=1)
    lanes = lane_ids(1, 128)
    halves = [jnp.where((lanes + half * 128) // 8 == tile, tiled, 0.0) for half in range(2)]
    return jnp.concatenate(halves, axis=0)


def open_kernel(
    field, kx_lo, kx_hi, ky, index, owner, well, rate, column, count, xlo, xhi, ylo, yhi, partials, at_slots, split
):
    for half in range(2):
        split[half] = field[:, half * 128 : half * 128 + 128]
    x_edges(field, 0, xlo, 0)
    x_edges(field, CX - 1, xhi, 0)
    for l in range(LZ):
        xlo[LZ + l : LZ + l + 1, :] = kx_lo[l, 0:1, :]
        xhi[LZ + l : LZ + l + 1, :] = kx_hi[l, 7:8, :]
    turned = y_edges([(field, 0), (ky, 0), (field, CY - 1), (ky, CY - 1)])
    ylo[...] = turned[0:8]
    yhi[...] = turned[8:16]
    at = gather_slots(split, column)
    at_slots[...] = at
    live = live_index(index, count)
    weighted = jnp.sum(live * at, axis=0, keepdims=True)
    total = jnp.sum(live, axis=0, keepdims=True)
    weighted_c, total_c, wells_c = well_columns([weighted, total, well_row(owner, well)])
    values = jnp.concatenate(
        [totals_by_well(weighted_c, wells_c) + own_rates(rate), totals_by_well(total_c, wells_c)], axis=0
    )
    send_partials(partials, values)


def solve_kernel(
    first,
    field,
    source,
    kx,
    ky,
    inverse,
    lower,
    from_xlo,
    from_xhi,
    from_ylo,
    from_yhi,
    kx_edges_lo,
    kx_edges_hi,
    ky_edges_lo,
    ky_edges_hi,
    partials,
    sums,
    index,
    owner,
    well,
    at_slots,
    column,
    count,
    solved,
    carried,
    sums_out,
    flow_out,
    rhs,
):
    gx, gy = lax.axis_index("gx"), lax.axis_index("gy")
    total = partials[0]
    for t in range(1, TILES):
        total = total + partials[t]
    if first:
        numerator, index_sum = total[0:2], total[2:4]
        sums_out[...] = index_sum
    else:
        numerator, index_sum = total[0:2], sums[...]
    bottom_hole = numerator / (index_sum + 1.0)
    (wells_c,) = well_columns([well_row(owner, well)])
    ids = wells_c[:SLOTS].astype(jnp.int32)
    held = jnp.zeros((SLOTS, 128), F32)
    for half in range(2):
        hit = ids == lane_ids(SLOTS, 128) + half * 128
        held = held + jnp.where(hit, bottom_hole[half : half + 1], 0.0)
    hole = jnp.sum(held, axis=1, keepdims=True)
    hole = jnp.broadcast_to(hole, (SLOTS, 128))
    hole = jnp.concatenate([hole, jnp.zeros((128 - SLOTS, 128), F32)], axis=0).T[0:1]
    flow = live_index(index, count) * (hole - at_slots[...])
    flow_out[...] = flow

    rows = lax.broadcasted_iota(jnp.int32, (CX, CY), 0)
    lanes = lane_ids(CX, CY)
    ylo_c = from_ylo[...].T
    yhi_c = from_yhi[...].T
    kylo_c = ky_edges_lo[...].T
    kyhi_c = ky_edges_hi[...].T
    k_row = 4 if first else 4

    def y_column(turned, base, l):
        s = (l % 2) * CX
        return turned[s : s + CX, base + l // 2 : base + l // 2 + 1]

    for l in range(LZ):
        span = slice(l * CX, (l + 1) * CX)
        f = field[span, :]
        k = kx[span, :]
        f_after = jnp.where(gx < 7, from_xhi[l : l + 1, :], 0.0)
        k_after = kx_edges_hi[LZ + l : LZ + l + 1, :]
        f_before = jnp.where(gx > 0, from_xlo[l : l + 1, :], 0.0)
        k_before = kx_edges_lo[LZ + l : LZ + l + 1, :]
        f_east = jnp.where(rows == CX - 1, f_after, pltpu.roll(f, CX - 1, 0))
        k_east = jnp.where(rows == CX - 1, k_after, pltpu.roll(k, CX - 1, 0))
        face = k + k_east
        west_first = (k[0:1, :] + k_before) * f_before
        lateral = face * f_east + jnp.where(rows == 0, west_first, pltpu.roll(face * f, 1, 0))
        k = ky[span, :]
        f_after = jnp.where(gy < 3, y_column(yhi_c, 0, l), 0.0)
        k_after = y_column(kyhi_c, k_row, l)
        f_before = jnp.where(gy > 0, y_column(ylo_c, 0, l), 0.0)
        k_before = y_column(kylo_c, k_row, l)
        f_north = jnp.where(lanes == CY - 1, f_after, pltpu.roll(f, CY - 1, 1))
        k_north = jnp.where(lanes == CY - 1, k_after, pltpu.roll(k, CY - 1, 1))
        face = k + k_north
        south_first = (k[:, 0:1] + k_before) * f_before
        lateral = lateral + face * f_north + jnp.where(lanes == 0, south_first, pltpu.roll(face * f, 1, 1))
        value = source[span, :] + 0.5 * lateral
        rhs[0, span, :] = value[:, :128]
        rhs[1, span, :] = value[:, 128:]

    lanes8 = lane_ids(LZ, 128)
    for s in range(SLOTS):
        place = column[0, s]
        x = place // CY
        y = place % CY
        half = y // 128
        lane = y % 128
        part = rhs.at[half]
        where = (pl.ds(x, LZ, stride=CX), slice(None))
        part[where] = part[where] + jnp.where(lanes8 == lane, flow[:, s : s + 1], 0.0)

    def block(b, carry):
        at = pl.multiple_of(b * 8, 8)
        right = [
            jnp.concatenate([rhs[half, pl.ds(j * CX + at, 8), :] for half in range(2)], axis=1) for j in range(LZ)
        ]
        here = pl.ds(at, 8)
        for i in range(LZ):
            total = inverse[i, 0, here, :] * right[0]
            for j in range(1, LZ):
                total = total + inverse[i, j, here, :] * right[j]
            solved[pl.ds(i * CX + at, 8), :] = total
            if i == 0:
                carried[1, here, :] = total
            if i == LZ - 1:
                low = lower[here, :]
                carried[0, here, :] = total + inverse[i, i, here, :] * low - low
        return carry

    lax.fori_loop(0, CX // 8, block, 0)


def sweep_kernel(last, *refs):
    cds, refs = refs[:8], refs[8:]
    fixed, refs = refs[:8], refs[8:]
    solved, first_column, last_column, *refs = refs
    if last:
        field, cd_all, fixed_all, sem = refs
    else:
        (index, owner, well, rate, column, count, field, lower, xlo, xhi, ylo, yhi, partials, at_slots, cd_all, fixed_all, sem, split) = refs
    me = lax.axis_index("layer")
    copies = []
    for n in range(8):
        distance, other = n % 4, n // 4
        core = me % 2
        core = jnp.where(other == 1, 1 - core, core)
        group = ((me // 2 + 4 - distance) % 4) * 2 + core
        copies.append(pltpu.make_async_copy(cds[n], cd_all.at[group], sem.at[0]))
        copies.append(pltpu.make_async_copy(fixed[n], fixed_all.at[group], sem.at[0]))
    for copy in copies:
        copy.start()
    for copy in copies:
        copy.wait()

    def block(b, carry):
        here = pl.ds(pl.multiple_of(b * 8, 8), 8)
        upper = jnp.zeros((8, CY), F32)
        uppers = [upper]
        for g in range(GROUPS - 1):
            upper = fixed_all[g, 0, here, :] * upper + cd_all[g, 0, here, :]
            uppers.append(upper)
        low = jnp.zeros((8, CY), F32)
        own_low, own_upper = low, uppers[0]
        for g in range(GROUPS - 1, 0, -1):
            own_upper = jnp.where(me == g, uppers[g], own_upper)
            step = cd_all[g, 1, here, :] + fixed_all[g, 2, here, :] * uppers[g] - uppers[g]
            low = fixed_all[g, 1, here, :] * low + step
            own_low = jnp.where(me == g - 1, low, own_low)
        for i in range(LZ):
            span = pl.ds(pl.multiple_of(i * CX + b * 8, 8), 8)
            value = (
                solved[span, :]
                + first_column[i, 0, here, :] * own_upper
                + last_column[i, 0, here, :] * own_low
            )
            field[span, :] = value
            if not last:
                split[0, span, :] = value[:, :128]
                split[1, span, :] = value[:, 128:]
        if not last:
            lower[here, :] = own_low
        return carry

    lax.fori_loop(0, CX // 8, block, 0)
    if last:
        return
    x_edges(field, 0, xlo, 0)
    x_edges(field, CX - 1, xhi, 0)
    turned = y_edges([(field, 0), (field, CY - 1)])
    ylo[...] = turned[0:8]
    yhi[...] = jnp.concatenate([turned[4:8], turned[0:4]], axis=0)
    at = gather_slots(split, column)
    at_slots[...] = at
    live = live_index(index, count)
    weighted = jnp.sum(live * at, axis=0, keepdims=True)
    weighted_c, wells_c = well_columns([weighted, well_row(owner, well)])
    send_partials(partials, totals_by_well(weighted_c, wells_c) + own_rates(rate))


def params():
    return pltpu.CompilerParams(vmem_limit_bytes=40 * 1024 * 1024)


def around(n, step):
    return [(i, (i + step) % n) for i in range(n)]


def from_sides(xlo, xhi, ylo, yhi):
    return (
        lax.ppermute(xhi, "gx", around(8, 1)),
        lax.ppermute(xlo, "gx", around(8, -1)),
        lax.ppermute(yhi, "gy", around(4, 1)),
        lax.ppermute(ylo, "gy", around(4, -1)),
    )


def all_groups(value):
    own = [value] + [lax.ppermute(value, "layer", around(8, 2 * d)) for d in range(1, 4)]
    swap = [(i, i ^ 1) for i in range(8)]
    return own + [lax.ppermute(v, "layer", swap) for v in own]


def shards(
    pressure,
    source,
    perm_x,
    perm_y,
    line_inverse,
    robin_below,
    tile_count,
    perf_owner,
    perf_well,
    perf_column,
    perf_index,
    well_rate,
):
    rows = LZ * CX
    field = pressure.reshape(rows, CY)
    source = source.reshape(rows, CY)
    kx = perm_x.reshape(rows, CY)
    ky = perm_y.reshape(rows, CY)
    inverse = line_inverse[0]
    lower = robin_below[0]
    index = perf_index[0].T
    owner = perf_owner[0].T
    well = perf_well
    column = perf_column
    count = tile_count

    fixed = all_groups(jnp.stack([inverse[LZ - 1, 0], inverse[0, LZ - 1], inverse[0, 0]]))

    edge_x = pl.BlockSpec((LZ, 8, CY), lambda n: (0, 0, 0))
    edge_x_hi = pl.BlockSpec((LZ, 8, CY), lambda n: (0, CX // 8 - 1, 0))
    *edges, partials, at_slots = pl.pallas_call(
        open_kernel,
        out_shape=(
            shape(16, CY),
            shape(16, CY),
            shape(8, 128),
            shape(8, 128),
            shape(TILES, 4, 128),
            shape(LZ, 128),
        ),
        grid=(1,),
        in_specs=[VMEM, edge_x, edge_x_hi] + [VMEM] * 5 + [SMEM] * 2,
        out_specs=(VMEM,) * 6,
        scratch_shapes=[pltpu.VMEM((2, rows, 128), F32)],
        compiler_params=params(),
        name="open_edges",
    )(field, perm_x, perm_x, ky, index, owner, well, well_rate, column, count)
    k_sides = None
    sums = jnp.zeros((2, 128), F32)
    for sweep_step in range(ITERS):
        first, last = sweep_step == 0, sweep_step == ITERS - 1
        sides = from_sides(*edges)
        if first:
            k_sides = sides
        spread = lax.all_to_all(partials, ("gx", "gy"), split_axis=0, concat_axis=0, tiled=True)
        solved, carried, new_sums, flow = pl.pallas_call(
            functools.partial(solve_kernel, first),
            out_shape=(shape(rows, CY), shape(2, CX, CY), shape(2, 128), shape(LZ, 128)),
            in_specs=[VMEM] * 20 + [SMEM] * 2,
            out_specs=(VMEM,) * 4,
            scratch_shapes=[pltpu.VMEM((2, rows, 128), F32)],
            compiler_params=params(),
            name="solve_lines",
        )(
            field,
            source,
            kx,
            ky,
            inverse,
            lower,
            *sides,
            *k_sides,
            spread,
            sums,
            index,
            owner,
            well,
            at_slots,
            column,
            count,
        )
        if first:
            sums = new_sums
        groups = all_groups(carried)
        column_first = pl.BlockSpec((LZ, 1, CX, CY), lambda n: (0, 0, 0, 0))
        column_last = pl.BlockSpec((LZ, 1, CX, CY), lambda n: (0, LZ - 1, 0, 0))
        specs = [ANY] * 16 + [VMEM, column_first, column_last]
        scratch = [
            pltpu.VMEM((GROUPS, 2, CX, CY), F32),
            pltpu.VMEM((GROUPS, 3, CX, CY), F32),
            pltpu.SemaphoreType.DMA((1,)),
        ]
        if last:
            (field,) = pl.pallas_call(
                functools.partial(sweep_kernel, True),
                out_shape=(shape(rows, CY),),
                grid=(1,),
                in_specs=specs,
                out_specs=(VMEM,),
                scratch_shapes=scratch,
                compiler_params=params(),
                name="sweep_last",
            )(*groups, *fixed, solved, inverse, inverse)
        else:
            field, lower, *edges, partials, at_slots = pl.pallas_call(
                functools.partial(sweep_kernel, False),
                out_shape=(
                    shape(rows, CY),
                    shape(CX, CY),
                    shape(8, CY),
                    shape(8, CY),
                    shape(8, 128),
                    shape(8, 128),
                    shape(TILES, 2, 128),
                    shape(LZ, 128),
                ),
                grid=(1,),
                in_specs=specs + [VMEM] * 4 + [SMEM] * 2,
                out_specs=(VMEM,) * 8,
                scratch_shapes=scratch + [pltpu.VMEM((2, rows, 128), F32)],
                compiler_params=params(),
                name="sweep_mid",
            )(*groups, *fixed, solved, inverse, inverse, index, owner, well, well_rate, column, count)
    return (field.reshape(LZ, CX, CY), flow[:, :SLOTS].T[None])


def solution(mesh):
    placed = (
        P("layer", "gx", "gy"),
        P("layer", "gx", "gy"),
        P("layer", "gx", "gy"),
        P("layer", "gx", "gy"),
        P("layer", None, None, "gx", "gy"),
        P("layer", "gx", "gy"),
        P("layer", ("gx", "gy")),
        P("layer", ("gx", "gy"), None),
        P("layer", ("gx", "gy")),
        P("layer", ("gx", "gy")),
        P("layer", ("gx", "gy"), None),
        P("layer", ("gx", "gy")),
    )
    return jax.shard_map(
        shards,
        mesh=mesh,
        in_specs=placed,
        out_specs=(P("layer", "gx", "gy"), P("layer", ("gx", "gy"), None)),
        check_vma=False,
    )
```

```python
import functools

import jax
import jax.numpy as jnp
from jax import lax
from jax.experimental import pallas as pl
from jax.experimental.pallas import tpu as pltpu
from jax.sharding import PartitionSpec as P

ITERS = 2
EDGE_MIB = 60
WELLS_MIB = 8
LZ = 8
CX = 64
CY = 256
SLOTS = 48
WELLS = 256
TILES = 32
GROUPS = 8
F32 = jnp.float32
VMEM = pl.BlockSpec(memory_space=pltpu.VMEM)
SMEM = pl.BlockSpec(memory_space=pltpu.SMEM)
ANY = pl.BlockSpec(memory_space=pltpu.HBM)


def shape(*dims):
    return jax.ShapeDtypeStruct(dims, F32)


def lane_ids(rows, lanes):
    return lax.broadcasted_iota(jnp.int32, (rows, lanes), 1)


def x_edges(ref, row, out, first):
    for l in range(LZ):
        out[first + l : first + l + 1, :] = ref[l * CX + row : l * CX + row + 1, :]


def y_edges(pieces):
    lanes = lane_ids(2 * CX, 128)
    packed = jnp.zeros((2 * CX, 128), F32)
    row = 0
    for ref, column in pieces:
        start = (column // 128) * 128
        for r in range(LZ // 2):
            block = ref[r * 2 * CX : (r + 1) * 2 * CX, start : start + 128]
            value = block[:, column - start : column - start + 1]
            packed = jnp.where(lanes == row, value, packed)
            row += 1
    return packed.T


def gather_slots(split_ref, column_ref):
    lanes = lane_ids(LZ, 128)
    found = jnp.zeros((LZ, 128), F32)
    for s in range(SLOTS):
        column = column_ref[0, s]
        x = column // CY
        y = column % CY
        half = y // 128
        lane = y % 128
        block = split_ref.at[half][pl.ds(x, LZ, stride=CX), :]
        value = jnp.sum(jnp.where(lanes == lane, block, 0.0), axis=1, keepdims=True)
        found = jnp.where(lanes == s, value, found)
    return found


def well_columns(rows):
    block = jnp.concatenate(rows + [jnp.zeros((8 - len(rows), 128), F32)], axis=0)
    turned = block.T
    return [turned[:, i : i + 1] for i in range(len(rows))]


def pad_lanes(value):
    return jnp.concatenate([value, jnp.zeros((value.shape[0], 128 - value.shape[1]), value.dtype)], axis=1)


def send_partials(out, values):
    for t in range(TILES):
        out[t] = values


def live_index(index_ref, count_ref):
    index = pad_lanes(index_ref[...])
    return jnp.where(lane_ids(LZ, 128) < count_ref[0, 0], index, 0.0)


def well_row(owner_ref, well_ref):
    return pad_lanes((owner_ref[...] * 8 + well_ref[...]).astype(F32))


def totals_by_well(column, well_column):
    ids = well_column[:SLOTS].astype(jnp.int32)
    halves = []
    for half in range(2):
        hit = ids == lane_ids(SLOTS, 128) + half * 128
        halves.append(jnp.sum(jnp.where(hit, column[:SLOTS], 0.0), axis=0, keepdims=True))
    return jnp.concatenate(halves, axis=0)


def own_rates(rate_ref):
    tile = lax.axis_index("gx") * 4 + lax.axis_index("gy")
    rate = rate_ref[...]
    tiled = jnp.concatenate([rate] * 16, axis=1)
    lanes = lane_ids(1, 128)
    halves = [jnp.where((lanes + half * 128) // 8 == tile, tiled, 0.0) for half in range(2)]
    return jnp.concatenate(halves, axis=0)


def load(copies, sem):
    started = [pltpu.make_async_copy(source, target, sem.at[n]) for n, (source, target) in enumerate(copies)]
    for copy in started:
        copy.start()
    return started


def halves_of(split, span):
    return jnp.concatenate([split[0, span, :], split[1, span, :]], axis=1)


def edges_kernel(pressure, perm_x, perm_y, inverse, xlo, xhi, ylo, yhi, fixed, split, kx_lo, kx_hi, ky, sem):
    copies = load(
        [(pressure.at[:, half * 128 : half * 128 + 128], split.at[half]) for half in range(2)]
        + [(perm_x.at[:, 0:8], kx_lo), (perm_x.at[:, CX - 8 : CX], kx_hi), (perm_y, ky)]
        + [(inverse.at[LZ - 1, 0], fixed.at[0]), (inverse.at[0, LZ - 1], fixed.at[1]), (inverse.at[0, 0], fixed.at[2])],
        sem,
    )
    for copy in copies[:5]:
        copy.wait()
    split_x_edges(split, xlo, xhi)
    for l in range(LZ):
        xlo[LZ + l : LZ + l + 1, :] = kx_lo[l, 0:1, :]
        xhi[LZ + l : LZ + l + 1, :] = kx_hi[l, 7:8, :]
    turned = y_edges([(split.at[0], 0), (ky, 0), (split.at[1], 127), (ky, CY - 1)])
    ylo[...] = turned[0:8]
    yhi[...] = turned[8:16]
    for copy in copies[5:]:
        copy.wait()


def split_x_edges(split, xlo, xhi):
    for l in range(LZ):
        for half in range(2):
            lanes = slice(half * 128, half * 128 + 128)
            xlo[l : l + 1, lanes] = split[half, l * CX : l * CX + 1, :]
            xhi[l : l + 1, lanes] = split[half, l * CX + CX - 1 : l * CX + CX, :]


def wells_first_kernel(
    pressure,
    index,
    owner,
    well,
    rate,
    column,
    count,
    partials,
    at_slots,
    live_out,
    wells_out,
    split,
    index_v,
    owner_v,
    well_v,
    rate_v,
    column_s,
    count_s,
    sem,
):
    copies = load(
        [(pressure.at[:, half * 128 : half * 128 + 128], split.at[half]) for half in range(2)]
        + [
            (column, column_s),
            (count, count_s),
            (index, index_v),
            (owner, owner_v),
            (well, well_v),
            (rate, rate_v),
        ],
        sem,
    )
    for copy in copies:
        copy.wait()
    at = gather_slots(split, column_s)
    at_slots[...] = at
    live = live_index(index_v, count_s)
    live_out[...] = live
    weighted = jnp.sum(live * at, axis=0, keepdims=True)
    total = jnp.sum(live, axis=0, keepdims=True)
    wells = well_row(owner_v, well_v)
    wells_out[...] = wells
    weighted_c, total_c, wells_c = well_columns([weighted, total, wells])
    values = jnp.concatenate(
        [totals_by_well(weighted_c, wells_c) + own_rates(rate_v), totals_by_well(total_c, wells_c)], axis=0
    )
    send_partials(partials, values)


def wells_next_kernel(split, live, wells, rate, column, partials, at_slots, rate_v, column_s, sem):
    copies = load([(column, column_s), (rate, rate_v)], sem)
    for copy in copies:
        copy.wait()
    at = gather_slots(split, column_s)
    at_slots[...] = at
    weighted = jnp.sum(live[...] * at, axis=0, keepdims=True)
    weighted_c, wells_c = well_columns([weighted, wells[...]])
    send_partials(partials, totals_by_well(weighted_c, wells_c) + own_rates(rate_v))


def solve_kernel(first, *refs):
    if first:
        (split, source, kx, ky, inverse, lower, from_xlo, from_xhi, from_ylo, from_yhi, partials, *refs) = refs
        kx_lo, kx_hi, ky_lo, ky_hi = from_xlo, from_xhi, from_ylo, from_yhi
        (live, wells, at_slots, column, solved, carried, sums_out, rhs, column_s, sem) = refs
    else:
        (split, source, kx, ky, inverse, lower, from_xlo, from_xhi, from_ylo, from_yhi, partials, *refs) = refs
        (kx_lo, kx_hi, ky_lo, ky_hi, sums, *refs) = refs
        (live, wells, at_slots, column, solved, carried, flow_out, rhs, column_s, sem) = refs
    copies = load([(column, column_s)], sem)
    gx, gy = lax.axis_index("gx"), lax.axis_index("gy")
    total = partials[0]
    for t in range(1, TILES):
        total = total + partials[t]
    if first:
        numerator, index_sum = total[0:2], total[2:4]
        sums_out[...] = index_sum
    else:
        numerator, index_sum = total, sums[...]
    bottom_hole = numerator / (index_sum + 1.0)
    (wells_c,) = well_columns([wells[...]])
    ids = wells_c[:SLOTS].astype(jnp.int32)
    held = jnp.zeros((SLOTS, 128), F32)
    for half in range(2):
        hit = ids == lane_ids(SLOTS, 128) + half * 128
        held = held + jnp.where(hit, bottom_hole[half : half + 1], 0.0)
    hole = jnp.sum(held, axis=1, keepdims=True)
    hole = jnp.broadcast_to(hole, (SLOTS, 128))
    hole = jnp.concatenate([hole, jnp.zeros((128 - SLOTS, 128), F32)], axis=0).T[0:1]
    flow = live[...] * (hole - at_slots[...])
    if not first:
        flow_out[...] = flow[:, :SLOTS]

    rows = lax.broadcasted_iota(jnp.int32, (CX, CY), 0)
    lanes = lane_ids(CX, CY)
    ylo_c = from_ylo[...].T
    yhi_c = from_yhi[...].T
    kylo_c = ky_lo[...].T
    kyhi_c = ky_hi[...].T

    def y_column(turned, base, l):
        s = (l % 2) * CX
        return turned[s : s + CX, base + l // 2 : base + l // 2 + 1]

    for l in range(LZ):
        span = slice(l * CX, (l + 1) * CX)
        f = halves_of(split, span)
        k = kx[span, :]
        f_after = jnp.where(gx < 7, from_xhi[l : l + 1, :], 0.0)
        k_after = kx_hi[LZ + l : LZ + l + 1, :]
        f_before = jnp.where(gx > 0, from_xlo[l : l + 1, :], 0.0)
        k_before = kx_lo[LZ + l : LZ + l + 1, :]
        f_east = jnp.where(rows == CX - 1, f_after, pltpu.roll(f, CX - 1, 0))
        k_east = jnp.where(rows == CX - 1, k_after, pltpu.roll(k, CX - 1, 0))
        face = k + k_east
        west_first = (k[0:1, :] + k_before) * f_before
        lateral = face * f_east + jnp.where(rows == 0, west_first, pltpu.roll(face * f, 1, 0))
        k = ky[span, :]
        f_after = jnp.where(gy < 3, y_column(yhi_c, 0, l), 0.0)
        k_after = y_column(kyhi_c, 4, l)
        f_before = jnp.where(gy > 0, y_column(ylo_c, 0, l), 0.0)
        k_before = y_column(kylo_c, 4, l)
        f_north = jnp.where(lanes == CY - 1, f_after, pltpu.roll(f, CY - 1, 1))
        k_north = jnp.where(lanes == CY - 1, k_after, pltpu.roll(k, CY - 1, 1))
        face = k + k_north
        south_first = (k[:, 0:1] + k_before) * f_before
        lateral = lateral + face * f_north + jnp.where(lanes == 0, south_first, pltpu.roll(face * f, 1, 1))
        value = source[span, :] + 0.5 * lateral
        rhs[0, span, :] = value[:, :128]
        rhs[1, span, :] = value[:, 128:]

    for copy in copies:
        copy.wait()
    lanes8 = lane_ids(LZ, 128)
    for s in range(SLOTS):
        place = column_s[0, s]
        x = place // CY
        y = place % CY
        half = y // 128
        lane = y % 128
        part = rhs.at[half]
        where = (pl.ds(x, LZ, stride=CX), slice(None))
        part[where] = part[where] + jnp.where(lanes8 == lane, flow[:, s : s + 1], 0.0)

    def block(b, carry):
        at = pl.multiple_of(b * 8, 8)
        right = [halves_of(rhs, pl.ds(j * CX + at, 8)) for j in range(LZ)]
        here = pl.ds(at, 8)
        for i in range(LZ):
            total = inverse[i, 0, here, :] * right[0]
            for j in range(1, LZ):
                total = total + inverse[i, j, here, :] * right[j]
            solved[pl.ds(i * CX + at, 8), :] = total
            if i == 0:
                carried[1, here, :] = total
            if i == LZ - 1:
                low = lower[here, :]
                carried[0, here, :] = total + inverse[i, i, here, :] * low - low
        return carry

    lax.fori_loop(0, CX // 8, block, 0)


def sweep_kernel(last, *refs):
    cds, fixed, refs = refs[:8], refs[8:16], refs[16:]
    if last:
        solved, inverse, field = refs
    else:
        solved, inverse, split, lower, xlo, xhi, ylo, yhi = refs
    me = lax.axis_index("layer")

    def position(own):
        def of(planes, g):
            distance = (own // 2 - g // 2) % 4
            return planes[distance + 4 * ((own ^ g) & 1)]

        def block(b, carry):
            here = pl.ds(pl.multiple_of(b * 8, 8), 8)
            upper = jnp.zeros((8, CY), F32)
            uppers = [upper]
            for g in range(GROUPS - 1):
                upper = of(fixed, g)[0, here, :] * upper + of(cds, g)[0, here, :]
                uppers.append(upper)
            low = jnp.zeros((8, CY), F32)
            for g in range(GROUPS - 1, own, -1):
                step = of(cds, g)[1, here, :] + of(fixed, g)[2, here, :] * uppers[g] - uppers[g]
                low = of(fixed, g)[1, here, :] * low + step
            for i in range(LZ):
                span = pl.ds(pl.multiple_of(i * CX + b * 8, 8), 8)
                value = solved[span, :] + inverse[i, 0, here, :] * uppers[own] + inverse[i, LZ - 1, here, :] * low
                if last:
                    field[span, :] = value
                else:
                    split[0, span, :] = value[:, :128]
                    split[1, span, :] = value[:, 128:]
            if not last:
                lower[here, :] = low
            return carry

        @pl.when(me == own)
        def _():
            lax.fori_loop(0, CX // 8, block, 0)

    for own in range(GROUPS):
        position(own)
    if last:
        return
    split_x_edges(split, xlo, xhi)
    turned = y_edges([(split.at[0], 0), (split.at[1], 127)])
    ylo[...] = turned[0:8]
    yhi[...] = jnp.concatenate([turned[4:8], turned[0:4]], axis=0)


def params(mib=8):
    return pltpu.CompilerParams(vmem_limit_bytes=mib * 1024 * 1024)


def around(n, step):
    return [(i, (i + step) % n) for i in range(n)]


def from_sides(xlo, xhi, ylo, yhi):
    return (
        lax.ppermute(xhi, "gx", around(8, 1)),
        lax.ppermute(xlo, "gx", around(8, -1)),
        lax.ppermute(yhi, "gy", around(4, 1)),
        lax.ppermute(ylo, "gy", around(4, -1)),
    )


def all_groups(value):
    own = [value] + [lax.ppermute(value, "layer", around(8, 2 * d)) for d in range(1, 4)]
    swap = [(i, i ^ 1) for i in range(8)]
    return own + [lax.ppermute(v, "layer", swap) for v in own]


def shards(
    pressure,
    source,
    perm_x,
    perm_y,
    line_inverse,
    robin_below,
    tile_count,
    perf_owner,
    perf_well,
    perf_column,
    perf_index,
    well_rate,
):
    rows = LZ * CX
    pressure = pressure.reshape(rows, CY)
    source = source.reshape(rows, CY)
    inverse = line_inverse[0]
    lower = robin_below[0]
    owner = perf_owner[0].T
    index = perf_index[0].T

    kx = perm_x.reshape(rows, CY)
    ky = perm_y.reshape(rows, CY)
    *edges, fixed = pl.pallas_call(
        edges_kernel,
        out_shape=(shape(16, CY), shape(16, CY), shape(8, 128), shape(8, 128), shape(3, CX, CY)),
        in_specs=[ANY] * 4,
        out_specs=(VMEM,) * 5,
        scratch_shapes=[
            pltpu.VMEM((2, rows, 128), F32),
            pltpu.VMEM((LZ, 8, CY), F32),
            pltpu.VMEM((LZ, 8, CY), F32),
            pltpu.VMEM((rows, CY), F32),
            pltpu.SemaphoreType.DMA((8,)),
        ],
        compiler_params=params(EDGE_MIB),
        name="first_edges",
    )(pressure, perm_x, ky, inverse)
    k_sides = sides = from_sides(*edges)
    fixed = all_groups(fixed)
    partials, at_slots, live, wells, field = pl.pallas_call(
        wells_first_kernel,
        out_shape=(
            shape(TILES, 4, 128),
            shape(LZ, 128),
            shape(LZ, 128),
            shape(1, 128),
            shape(2, rows, 128),
        ),
        in_specs=[ANY] * 7,
        out_specs=(VMEM,) * 5,
        scratch_shapes=[
            pltpu.VMEM((LZ, SLOTS), F32),
            pltpu.VMEM((1, SLOTS), jnp.int32),
            pltpu.VMEM((1, SLOTS), jnp.int32),
            pltpu.VMEM((1, 8), F32),
            pltpu.SMEM((1, SLOTS), jnp.int32),
            pltpu.SMEM((1, 1), jnp.int32),
            pltpu.SemaphoreType.DMA((8,)),
        ],
        compiler_params=params(WELLS_MIB),
        name="first_wells",
    )(pressure, index, owner, perf_well, well_rate, perf_column, tile_count)
    sums = None
    for sweep_step in range(ITERS):
        first, last = sweep_step == 0, sweep_step == ITERS - 1
        tied = lax.optimization_barrier((partials, *sides))
        partials, sides = tied[0], tied[1:]
        if first:
            k_sides = sides
        spread = lax.all_to_all(partials, ("gx", "gy"), split_axis=0, concat_axis=0, tiled=True)
        extra = () if first else (*k_sides, sums)
        solved, carried, small = pl.pallas_call(
            functools.partial(solve_kernel, first),
            out_shape=(shape(rows, CY), shape(2, CX, CY), shape(2, 128) if first else shape(LZ, SLOTS)),
            in_specs=[VMEM] * (14 + len(extra)) + [ANY],
            out_specs=(VMEM,) * 3,
            scratch_shapes=[
                pltpu.VMEM((2, rows, 128), F32),
                pltpu.SMEM((1, SLOTS), jnp.int32),
                pltpu.SemaphoreType.DMA((1,)),
            ],
            compiler_params=params(),
            name="solve_lines",
        )(field, source, kx, ky, inverse, lower, *sides, spread, *extra, live, wells, at_slots, perf_column)
        groups = all_groups(carried)
        if last:
            flow = small
            (field,) = pl.pallas_call(
                functools.partial(sweep_kernel, True),
                out_shape=(shape(rows, CY),),
                in_specs=[VMEM] * 18,
                out_specs=(VMEM,),
                compiler_params=params(),
                name="sweep_last",
            )(*groups, *fixed, solved, inverse)
            break
        sums = small
        field, lower, *edges = pl.pallas_call(
            functools.partial(sweep_kernel, False),
            out_shape=(
                shape(2, rows, 128),
                shape(CX, CY),
                shape(8, CY),
                shape(8, CY),
                shape(8, 128),
                shape(8, 128),
            ),
            in_specs=[VMEM] * 18,
            out_specs=(VMEM,) * 6,
            compiler_params=params(),
            name="sweep_mid",
        )(*groups, *fixed, solved, inverse)
        sides = from_sides(*edges)
        partials, at_slots = pl.pallas_call(
            wells_next_kernel,
            out_shape=(shape(TILES, 2, 128), shape(LZ, 128)),
            in_specs=[VMEM] * 3 + [ANY] * 2,
            out_specs=(VMEM,) * 2,
            scratch_shapes=[
                pltpu.VMEM((1, 8), F32),
                pltpu.SMEM((1, SLOTS), jnp.int32),
                pltpu.SemaphoreType.DMA((2,)),
            ],
            compiler_params=params(),
            name="next_wells",
        )(field, live, wells, well_rate, perf_column)
    return (field.reshape(LZ, CX, CY), flow.T[None])


def solution(mesh):
    placed = (
        P("layer", "gx", "gy"),
        P("layer", "gx", "gy"),
        P("layer", "gx", "gy"),
        P("layer", "gx", "gy"),
        P("layer", None, None, "gx", "gy"),
        P("layer", "gx", "gy"),
        P("layer", ("gx", "gy")),
        P("layer", ("gx", "gy"), None),
        P("layer", ("gx", "gy")),
        P("layer", ("gx", "gy")),
        P("layer", ("gx", "gy"), None),
        P("layer", ("gx", "gy")),
    )
    return jax.shard_map(
        shards,
        mesh=mesh,
        in_specs=placed,
        out_specs=(P("layer", "gx", "gy"), P("layer", ("gx", "gy"), None)),
        check_vma=False,
    )
```

```python
import functools

import jax
import jax.numpy as jnp
from jax import lax
from jax.experimental import pallas as pl
from jax.experimental.pallas import tpu as pltpu
from jax.sharding import PartitionSpec as P

ITERS = 2
EDGE_MIB = 54
WELLS_MIB = 8
LZ = 8
CX = 64
CY = 256
SLOTS = 48
WELLS = 256
TILES = 32
GROUPS = 8
F32 = jnp.float32
VMEM = pl.BlockSpec(memory_space=pltpu.VMEM)
SMEM = pl.BlockSpec(memory_space=pltpu.SMEM)
ANY = pl.BlockSpec(memory_space=pltpu.HBM)


def shape(*dims):
    return jax.ShapeDtypeStruct(dims, F32)


def lane_ids(rows, lanes):
    return lax.broadcasted_iota(jnp.int32, (rows, lanes), 1)


def x_edges(ref, row, out, first):
    for l in range(LZ):
        out[first + l : first + l + 1, :] = ref[l * CX + row : l * CX + row + 1, :]


def y_edges(pieces):
    lanes = lane_ids(2 * CX, 128)
    packed = jnp.zeros((2 * CX, 128), F32)
    row = 0
    for ref, column in pieces:
        start = (column // 128) * 128
        for r in range(LZ // 2):
            block = ref[r * 2 * CX : (r + 1) * 2 * CX, start : start + 128]
            value = block[:, column - start : column - start + 1]
            packed = jnp.where(lanes == row, value, packed)
            row += 1
    return packed.T


def gather_slots(split_ref, column_ref):
    lanes = lane_ids(LZ, 128)
    found = jnp.zeros((LZ, 128), F32)
    for s in range(SLOTS):
        column = column_ref[0, s]
        x = column // CY
        y = column % CY
        half = y // 128
        lane = y % 128
        block = split_ref.at[half][pl.ds(x, LZ, stride=CX), :]
        value = jnp.sum(jnp.where(lanes == lane, block, 0.0), axis=1, keepdims=True)
        found = jnp.where(lanes == s, value, found)
    return found


def well_columns(rows):
    block = jnp.concatenate(rows + [jnp.zeros((8 - len(rows), 128), F32)], axis=0)
    turned = block.T
    return [turned[:, i : i + 1] for i in range(len(rows))]


def pad_lanes(value):
    return jnp.concatenate([value, jnp.zeros((value.shape[0], 128 - value.shape[1]), value.dtype)], axis=1)


def own_tile():
    return lax.axis_index("gx") * 4 + lax.axis_index("gy")


def tile_at(step):
    return lax.rem(own_tile() + step + TILES, TILES)


def send_wells(out, wells):
    count = out.shape[0] // TILES
    for t in range(TILES):
        out[t * count] = wells


def send_y(out, lower_edge, upper_edge):
    count, rows, _ = out.shape
    count = count // TILES
    for step, edge in ((1, upper_edge), (-1, lower_edge)):
        first = tile_at(step) * count + 1
        for n in range(edge.shape[0] // rows):
            out[first + n] = edge[n * rows : (n + 1) * rows]


def send_x(out, split):
    count = out.shape[0] // TILES
    for step, row in ((4, CX - 1), (-4, 0)):
        first = tile_at(step) * count + 1
        for l in range(LZ):
            for half in range(2):
                out[first + l, half : half + 1, :] = split[half, l * CX + row : l * CX + row + 1, :]


def from_y(spread, blocks):
    count = spread.shape[0] // TILES
    result = []
    for step in (-1, 1):
        first = tile_at(step) * count + 1
        result.append(jnp.concatenate([spread[first + n] for n in range(blocks)], axis=0))
    return result


def from_x(spread, step, l):
    count = spread.shape[0] // TILES
    block = spread[tile_at(step) * count + 1 + l]
    return jnp.concatenate([block[0:1], block[1:2]], axis=1)


def live_index(index_ref, count_ref):
    index = pad_lanes(index_ref[...])
    return jnp.where(lane_ids(LZ, 128) < count_ref[0, 0], index, 0.0)


def well_row(owner_ref, well_ref):
    return pad_lanes((owner_ref[...] * 8 + well_ref[...]).astype(F32))


def totals_by_well(column, well_column):
    ids = well_column[:SLOTS].astype(jnp.int32)
    halves = []
    for half in range(2):
        hit = ids == lane_ids(SLOTS, 128) + half * 128
        halves.append(jnp.sum(jnp.where(hit, column[:SLOTS], 0.0), axis=0, keepdims=True))
    return jnp.concatenate(halves, axis=0)


def own_rates(rate_ref):
    tile = own_tile()
    rate = rate_ref[...]
    tiled = jnp.concatenate([rate] * 16, axis=1)
    lanes = lane_ids(1, 128)
    halves = [jnp.where((lanes + half * 128) // 8 == tile, tiled, 0.0) for half in range(2)]
    return jnp.concatenate(halves, axis=0)


def load(copies, sem):
    started = [pltpu.make_async_copy(source, target, sem.at[n]) for n, (source, target) in enumerate(copies)]
    for copy in started:
        copy.start()
    return started


def halves_of(split, span):
    return jnp.concatenate([split[0, span, :], split[1, span, :]], axis=1)


def edges_kernel(pressure, perm_x, perm_y, inverse, xlo, xhi, y_edge, fixed, split, kx_lo, kx_hi, ky, sem):
    copies = load(
        [(pressure.at[:, half * 128 : half * 128 + 128], split.at[half]) for half in range(2)]
        + [(perm_x.at[:, 0:8], kx_lo), (perm_x.at[:, CX - 8 : CX], kx_hi), (perm_y, ky)]
        + [(inverse.at[LZ - 1, 0], fixed.at[0]), (inverse.at[0, LZ - 1], fixed.at[1]), (inverse.at[0, 0], fixed.at[2])],
        sem,
    )
    for copy in copies[:5]:
        copy.wait()
    split_x_edges(split, xlo, xhi)
    for l in range(LZ):
        xlo[LZ + l : LZ + l + 1, :] = kx_lo[l, 0:1, :]
        xhi[LZ + l : LZ + l + 1, :] = kx_hi[l, 7:8, :]
    y_edge[...] = y_edges([(split.at[0], 0), (ky, 0), (split.at[1], 127), (ky, CY - 1)])[0:16]
    for copy in copies[5:]:
        copy.wait()


def split_x_edges(split, xlo, xhi):
    for l in range(LZ):
        for half in range(2):
            lanes = slice(half * 128, half * 128 + 128)
            xlo[l : l + 1, lanes] = split[half, l * CX : l * CX + 1, :]
            xhi[l : l + 1, lanes] = split[half, l * CX + CX - 1 : l * CX + CX, :]


def wells_first_kernel(
    y_edge,
    pressure,
    index,
    owner,
    well,
    rate,
    column,
    count,
    partials,
    at_slots,
    live_out,
    wells_out,
    split,
    index_v,
    owner_v,
    well_v,
    rate_v,
    column_s,
    count_s,
    sem,
):
    copies = load(
        [(pressure.at[:, half * 128 : half * 128 + 128], split.at[half]) for half in range(2)]
        + [
            (column, column_s),
            (count, count_s),
            (index, index_v),
            (owner, owner_v),
            (well, well_v),
            (rate, rate_v),
        ],
        sem,
    )
    for copy in copies:
        copy.wait()
    at = gather_slots(split, column_s)
    at_slots[...] = at
    live = live_index(index_v, count_s)
    live_out[...] = live
    weighted = jnp.sum(live * at, axis=0, keepdims=True)
    total = jnp.sum(live, axis=0, keepdims=True)
    wells = well_row(owner_v, well_v)
    wells_out[...] = wells
    weighted_c, total_c, wells_c = well_columns([weighted, total, wells])
    values = jnp.concatenate(
        [totals_by_well(weighted_c, wells_c) + own_rates(rate_v), totals_by_well(total_c, wells_c)], axis=0
    )
    send_wells(partials, values)
    send_y(partials, y_edge[0:8], y_edge[8:16])


def wells_next_kernel(split, live, wells, rate, column, partials, at_slots, rate_v, column_s, sem):
    copies = load([(column, column_s), (rate, rate_v)], sem)
    for copy in copies:
        copy.wait()
    at = gather_slots(split, column_s)
    at_slots[...] = at
    weighted = jnp.sum(live[...] * at, axis=0, keepdims=True)
    weighted_c, wells_c = well_columns([weighted, wells[...]])
    send_wells(partials, totals_by_well(weighted_c, wells_c) + own_rates(rate_v))
    turned = y_edges([(split.at[0], 0), (split.at[1], 127)])
    send_y(partials, turned[0:4], turned[4:8])
    send_x(partials, split)


def solve_kernel(first, *refs):
    (split, source, kx, ky, inverse, lower, kx_lo, kx_hi, partials, *refs) = refs
    if first:
        (live, wells, at_slots, column, solved, carried, sums_out, kylo_out, kyhi_out, rhs, column_s, sem) = refs
    else:
        (ky_lo, ky_hi, sums, *refs) = refs
        (live, wells, at_slots, column, solved, carried, flow_out, rhs, column_s, sem) = refs
    copies = load([(column, column_s)], sem)
    gx, gy = lax.axis_index("gx"), lax.axis_index("gy")
    total = partials[0]
    for t in range(1, TILES):
        total = total + partials[partials.shape[0] // TILES * t]
    if first:
        numerator, index_sum = total[0:2], total[2:4]
        sums_out[...] = index_sum
    else:
        numerator, index_sum = total, sums[...]
    bottom_hole = numerator / (index_sum + 1.0)
    (wells_c,) = well_columns([wells[...]])
    ids = wells_c[:SLOTS].astype(jnp.int32)
    held = jnp.zeros((SLOTS, 128), F32)
    for half in range(2):
        hit = ids == lane_ids(SLOTS, 128) + half * 128
        held = held + jnp.where(hit, bottom_hole[half : half + 1], 0.0)
    hole = jnp.sum(held, axis=1, keepdims=True)
    hole = jnp.broadcast_to(hole, (SLOTS, 128))
    hole = jnp.concatenate([hole, jnp.zeros((128 - SLOTS, 128), F32)], axis=0).T[0:1]
    flow = live[...] * (hole - at_slots[...])
    if not first:
        flow_out[...] = flow[:, :SLOTS]

    rows = lax.broadcasted_iota(jnp.int32, (CX, CY), 0)
    lanes = lane_ids(CX, CY)
    from_ylo, from_yhi = from_y(partials, 2)
    if first:
        kylo_out[...] = from_ylo
        kyhi_out[...] = from_yhi
        ylo_c = kylo_c = from_ylo.T
        yhi_c = kyhi_c = from_yhi.T
    else:
        spare = jnp.zeros((4, 128), F32)
        ylo_c = jnp.concatenate([from_ylo, spare], axis=0).T
        yhi_c = jnp.concatenate([from_yhi, spare], axis=0).T
        kylo_c = ky_lo[...].T
        kyhi_c = ky_hi[...].T

    def y_column(turned, base, l):
        s = (l % 2) * CX
        return turned[s : s + CX, base + l // 2 : base + l // 2 + 1]

    for l in range(LZ):
        span = slice(l * CX, (l + 1) * CX)
        f = halves_of(split, span)
        k = kx[span, :]
        f_after = kx_hi[l : l + 1, :] if first else from_x(partials, 4, l)
        f_after = jnp.where(gx < 7, f_after, 0.0)
        k_after = kx_hi[LZ + l : LZ + l + 1, :]
        f_before = kx_lo[l : l + 1, :] if first else from_x(partials, -4, l)
        f_before = jnp.where(gx > 0, f_before, 0.0)
        k_before = kx_lo[LZ + l : LZ + l + 1, :]
        f_east = jnp.where(rows == CX - 1, f_after, pltpu.roll(f, CX - 1, 0))
        k_east = jnp.where(rows == CX - 1, k_after, pltpu.roll(k, CX - 1, 0))
        face = k + k_east
        west_first = (k[0:1, :] + k_before) * f_before
        lateral = face * f_east + jnp.where(rows == 0, west_first, pltpu.roll(face * f, 1, 0))
        k = ky[span, :]
        f_after = jnp.where(gy < 3, y_column(yhi_c, 0, l), 0.0)
        k_after = y_column(kyhi_c, 4, l)
        f_before = jnp.where(gy > 0, y_column(ylo_c, 0, l), 0.0)
        k_before = y_column(kylo_c, 4, l)
        f_north = jnp.where(lanes == CY - 1, f_after, pltpu.roll(f, CY - 1, 1))
        k_north = jnp.where(lanes == CY - 1, k_after, pltpu.roll(k, CY - 1, 1))
        face = k + k_north
        south_first = (k[:, 0:1] + k_before) * f_before
        lateral = lateral + face * f_north + jnp.where(lanes == 0, south_first, pltpu.roll(face * f, 1, 1))
        value = source[span, :] + 0.5 * lateral
        rhs[0, span, :] = value[:, :128]
        rhs[1, span, :] = value[:, 128:]

    for copy in copies:
        copy.wait()
    lanes8 = lane_ids(LZ, 128)
    for s in range(SLOTS):
        place = column_s[0, s]
        x = place // CY
        y = place % CY
        half = y // 128
        lane = y % 128
        part = rhs.at[half]
        where = (pl.ds(x, LZ, stride=CX), slice(None))
        part[where] = part[where] + jnp.where(lanes8 == lane, flow[:, s : s + 1], 0.0)

    def block(b, carry):
        at = pl.multiple_of(b * 8, 8)
        right = [halves_of(rhs, pl.ds(j * CX + at, 8)) for j in range(LZ)]
        here = pl.ds(at, 8)
        for i in range(LZ):
            total = inverse[i, 0, here, :] * right[0]
            for j in range(1, LZ):
                total = total + inverse[i, j, here, :] * right[j]
            solved[pl.ds(i * CX + at, 8), :] = total
            if i == 0:
                carried[1, here, :] = total
            if i == LZ - 1:
                low = lower[here, :]
                carried[0, here, :] = total + inverse[i, i, here, :] * low - low
        return carry

    lax.fori_loop(0, CX // 8, block, 0)


def sweep_kernel(last, *refs):
    cds, fixed, refs = refs[:8], refs[8:16], refs[16:]
    if last:
        solved, inverse, field = refs
    else:
        solved, inverse, split, lower = refs
    me = lax.axis_index("layer")

    def position(own):
        def of(planes, g):
            distance = (own // 2 - g // 2) % 4
            return planes[distance + 4 * ((own ^ g) & 1)]

        def block(b, carry):
            here = pl.ds(pl.multiple_of(b * 8, 8), 8)
            upper = jnp.zeros((8, CY), F32)
            uppers = [upper]
            for g in range(GROUPS - 1):
                upper = of(fixed, g)[0, here, :] * upper + of(cds, g)[0, here, :]
                uppers.append(upper)
            low = jnp.zeros((8, CY), F32)
            for g in range(GROUPS - 1, own, -1):
                step = of(cds, g)[1, here, :] + of(fixed, g)[2, here, :] * uppers[g] - uppers[g]
                low = of(fixed, g)[1, here, :] * low + step
            for i in range(LZ):
                span = pl.ds(pl.multiple_of(i * CX + b * 8, 8), 8)
                value = solved[span, :] + inverse[i, 0, here, :] * uppers[own] + inverse[i, LZ - 1, here, :] * low
                if last:
                    field[span, :] = value
                else:
                    split[0, span, :] = value[:, :128]
                    split[1, span, :] = value[:, 128:]
            if not last:
                lower[here, :] = low
            return carry

        @pl.when(me == own)
        def _():
            lax.fori_loop(0, CX // 8, block, 0)

    for own in range(GROUPS):
        position(own)


def params(mib=8):
    return pltpu.CompilerParams(vmem_limit_bytes=mib * 1024 * 1024)


def around(n, step):
    return [(i, (i + step) % n) for i in range(n)]


def from_sides(xlo, xhi):
    return (lax.ppermute(xhi, "gx", around(8, 1)), lax.ppermute(xlo, "gx", around(8, -1)))


def all_groups(value):
    own = [value] + [lax.ppermute(value, "layer", around(8, 2 * d)) for d in range(1, 4)]
    swap = [(i, i ^ 1) for i in range(8)]
    return own + [lax.ppermute(v, "layer", swap) for v in own]


def shards(
    pressure,
    source,
    perm_x,
    perm_y,
    line_inverse,
    robin_below,
    tile_count,
    perf_owner,
    perf_well,
    perf_column,
    perf_index,
    well_rate,
):
    rows = LZ * CX
    pressure = pressure.reshape(rows, CY)
    source = source.reshape(rows, CY)
    inverse = line_inverse[0]
    lower = robin_below[0]
    owner = perf_owner[0].T
    index = perf_index[0].T

    kx = perm_x.reshape(rows, CY)
    ky = perm_y.reshape(rows, CY)
    *edges, y_edge, fixed = pl.pallas_call(
        edges_kernel,
        out_shape=(shape(16, CY), shape(16, CY), shape(16, 128), shape(3, CX, CY)),
        in_specs=[ANY] * 4,
        out_specs=(VMEM,) * 4,
        scratch_shapes=[
            pltpu.VMEM((2, rows, 128), F32),
            pltpu.VMEM((LZ, 8, CY), F32),
            pltpu.VMEM((LZ, 8, CY), F32),
            pltpu.VMEM((rows, CY), F32),
            pltpu.SemaphoreType.DMA((8,)),
        ],
        compiler_params=params(EDGE_MIB),
        name="first_edges",
    )(pressure, perm_x, ky, inverse)
    sides = from_sides(*edges)
    fixed = all_groups(fixed)
    partials, at_slots, live, wells, field = pl.pallas_call(
        wells_first_kernel,
        out_shape=(
            shape(3 * TILES, 4, 128),
            shape(LZ, 128),
            shape(LZ, 128),
            shape(1, 128),
            shape(2, rows, 128),
        ),
        in_specs=[VMEM] + [ANY] * 7,
        out_specs=(VMEM,) * 5,
        scratch_shapes=[
            pltpu.VMEM((LZ, SLOTS), F32),
            pltpu.VMEM((1, SLOTS), jnp.int32),
            pltpu.VMEM((1, SLOTS), jnp.int32),
            pltpu.VMEM((1, 8), F32),
            pltpu.SMEM((1, SLOTS), jnp.int32),
            pltpu.SMEM((1, 1), jnp.int32),
            pltpu.SemaphoreType.DMA((8,)),
        ],
        compiler_params=params(WELLS_MIB),
        name="first_wells",
    )(y_edge, pressure, index, owner, perf_well, well_rate, perf_column, tile_count)
    sums = None
    for sweep_step in range(ITERS):
        first, last = sweep_step == 0, sweep_step == ITERS - 1
        if first:
            partials, *sides = lax.optimization_barrier((partials, *sides))
        spread = lax.all_to_all(partials, ("gx", "gy"), split_axis=0, concat_axis=0, tiled=True)
        extra = () if first else (*ky_sides, sums)
        solved, carried, small, *ky_out = pl.pallas_call(
            functools.partial(solve_kernel, first),
            out_shape=(shape(rows, CY), shape(2, CX, CY))
            + ((shape(2, 128), shape(8, 128), shape(8, 128)) if first else (shape(LZ, SLOTS),)),
            in_specs=[VMEM] * (12 + len(extra)) + [ANY],
            out_specs=(VMEM,) * (5 if first else 3),
            scratch_shapes=[
                pltpu.VMEM((2, rows, 128), F32),
                pltpu.SMEM((1, SLOTS), jnp.int32),
                pltpu.SemaphoreType.DMA((1,)),
            ],
            compiler_params=params(),
            name="solve_lines",
        )(field, source, kx, ky, inverse, lower, *sides, spread, *extra, live, wells, at_slots, perf_column)
        groups = all_groups(carried)
        if last:
            flow = small
            (field,) = pl.pallas_call(
                functools.partial(sweep_kernel, True),
                out_shape=(shape(rows, CY),),
                in_specs=[VMEM] * 18,
                out_specs=(VMEM,),
                compiler_params=params(),
                name="sweep_last",
            )(*groups, *fixed, solved, inverse)
            break
        sums, ky_sides = small, ky_out
        field, lower = pl.pallas_call(
            functools.partial(sweep_kernel, False),
            out_shape=(
                shape(2, rows, 128),
                shape(CX, CY),
            ),
            in_specs=[VMEM] * 18,
            out_specs=(VMEM,) * 2,
            compiler_params=params(),
            name="sweep_mid",
        )(*groups, *fixed, solved, inverse)
        partials, at_slots = pl.pallas_call(
            wells_next_kernel,
            out_shape=(shape(9 * TILES, 2, 128), shape(LZ, 128)),
            in_specs=[VMEM] * 3 + [ANY] * 2,
            out_specs=(VMEM,) * 2,
            scratch_shapes=[
                pltpu.VMEM((1, 8), F32),
                pltpu.SMEM((1, SLOTS), jnp.int32),
                pltpu.SemaphoreType.DMA((2,)),
            ],
            compiler_params=params(),
            name="next_wells",
        )(field, live, wells, well_rate, perf_column)
    return (field.reshape(LZ, CX, CY), flow.T[None])


def solution(mesh):
    placed = (
        P("layer", "gx", "gy"),
        P("layer", "gx", "gy"),
        P("layer", "gx", "gy"),
        P("layer", "gx", "gy"),
        P("layer", None, None, "gx", "gy"),
        P("layer", "gx", "gy"),
        P("layer", ("gx", "gy")),
        P("layer", ("gx", "gy"), None),
        P("layer", ("gx", "gy")),
        P("layer", ("gx", "gy")),
        P("layer", ("gx", "gy"), None),
        P("layer", ("gx", "gy")),
    )
    return jax.shard_map(
        shards,
        mesh=mesh,
        in_specs=placed,
        out_specs=(P("layer", "gx", "gy"), P("layer", ("gx", "gy"), None)),
        check_vma=False,
    )
```

```python
import functools

import jax
import jax.numpy as jnp
from jax import lax
from jax.experimental import pallas as pl
from jax.experimental.pallas import tpu as pltpu
from jax.sharding import PartitionSpec as P

ITERS = 2
EDGE_MIB = 53.0
WELLS_MIB = 52.0
SOLVE_MIB = 52.0
LZ = 8
CX = 64
CY = 256
SLOTS = 48
WELLS = 256
TILES = 32
GROUPS = 8
F32 = jnp.float32
VMEM = pl.BlockSpec(memory_space=pltpu.VMEM)
SMEM = pl.BlockSpec(memory_space=pltpu.SMEM)
ANY = pl.BlockSpec(memory_space=pltpu.HBM)


def shape(*dims):
    return jax.ShapeDtypeStruct(dims, F32)


def lane_ids(rows, lanes):
    return lax.broadcasted_iota(jnp.int32, (rows, lanes), 1)


def x_edges(ref, row, out, first):
    for l in range(LZ):
        out[first + l : first + l + 1, :] = ref[l * CX + row : l * CX + row + 1, :]


def y_edges(pieces):
    lanes = lane_ids(2 * CX, 128)
    packed = jnp.zeros((2 * CX, 128), F32)
    row = 0
    for ref, column in pieces:
        start = (column // 128) * 128
        for r in range(LZ // 2):
            block = ref[r * 2 * CX : (r + 1) * 2 * CX, start : start + 128]
            value = block[:, column - start : column - start + 1]
            packed = jnp.where(lanes == row, value, packed)
            row += 1
    return packed.T


def gather_slots(split_ref, column_ref):
    lanes = lane_ids(LZ, 128)
    found = jnp.zeros((LZ, 128), F32)
    for s in range(SLOTS):
        column = column_ref[0, s]
        x = column // CY
        y = column % CY
        half = y // 128
        lane = y % 128
        block = split_ref.at[half][pl.ds(x, LZ, stride=CX), :]
        value = jnp.sum(jnp.where(lanes == lane, block, 0.0), axis=1, keepdims=True)
        found = jnp.where(lanes == s, value, found)
    return found


def well_columns(rows):
    block = jnp.concatenate(rows + [jnp.zeros((8 - len(rows), 128), F32)], axis=0)
    turned = block.T
    return [turned[:, i : i + 1] for i in range(len(rows))]


def pad_lanes(value):
    return jnp.concatenate([value, jnp.zeros((value.shape[0], 128 - value.shape[1]), value.dtype)], axis=1)


def own_tile():
    return lax.axis_index("gx") * 4 + lax.axis_index("gy")


def tile_at(step):
    return lax.rem(own_tile() + step + TILES, TILES)


def send_wells(out, wells):
    count = out.shape[0] // TILES
    for t in range(TILES):
        out[t * count] = wells


def send_y(out, lower_edge, upper_edge):
    count, rows, _ = out.shape
    count = count // TILES
    for step, edge in ((1, upper_edge), (-1, lower_edge)):
        first = tile_at(step) * count + 1
        for n in range(edge.shape[0] // rows):
            out[first + n] = edge[n * rows : (n + 1) * rows]


def from_y(spread, blocks):
    count = spread.shape[0] // TILES
    result = []
    for step in (-1, 1):
        first = tile_at(step) * count + 1
        result.append(jnp.concatenate([spread[first + n] for n in range(blocks)], axis=0))
    return result


def live_index(index_ref, count_ref):
    index = pad_lanes(index_ref[...])
    return jnp.where(lane_ids(LZ, 128) < count_ref[0, 0], index, 0.0)


def well_row(owner_ref, well_ref):
    return pad_lanes((owner_ref[...] * 8 + well_ref[...]).astype(F32))


def totals_by_well(column, well_column):
    ids = well_column[:SLOTS].astype(jnp.int32)
    halves = []
    for half in range(2):
        hit = ids == lane_ids(SLOTS, 128) + half * 128
        halves.append(jnp.sum(jnp.where(hit, column[:SLOTS], 0.0), axis=0, keepdims=True))
    return jnp.concatenate(halves, axis=0)


def own_rates(rate_ref):
    tile = own_tile()
    rate = rate_ref[...]
    tiled = jnp.concatenate([rate] * 16, axis=1)
    lanes = lane_ids(1, 128)
    halves = [jnp.where((lanes + half * 128) // 8 == tile, tiled, 0.0) for half in range(2)]
    return jnp.concatenate(halves, axis=0)


def load(copies, sem):
    started = [pltpu.make_async_copy(source, target, sem.at[n]) for n, (source, target) in enumerate(copies)]
    for copy in started:
        copy.start()
    return started


def halves_of(split, span):
    return jnp.concatenate([split[0, span, :], split[1, span, :]], axis=1)


def edges_kernel(pressure, perm_x, perm_y, inverse, xlo, xhi, y_edge, fixed, split, kx_lo, kx_hi, ky, sem):
    copies = load(
        [(pressure.at[:, half * 128 : half * 128 + 128], split.at[half]) for half in range(2)]
        + [(perm_x.at[:, 0:8], kx_lo), (perm_x.at[:, CX - 8 : CX], kx_hi), (perm_y, ky)]
        + [(inverse.at[LZ - 1, 0], fixed.at[0]), (inverse.at[0, LZ - 1], fixed.at[1]), (inverse.at[0, 0], fixed.at[2])],
        sem,
    )
    for copy in copies[:5]:
        copy.wait()
    split_x_edges(split, xlo, xhi)
    for l in range(LZ):
        xlo[LZ + l : LZ + l + 1, :] = kx_lo[l, 0:1, :]
        xhi[LZ + l : LZ + l + 1, :] = kx_hi[l, 7:8, :]
    y_edge[...] = y_edges([(split.at[0], 0), (ky, 0), (split.at[1], 127), (ky, CY - 1)])[0:16]
    for copy in copies[5:]:
        copy.wait()


def split_x_edges(split, xlo, xhi):
    for l in range(LZ):
        for half in range(2):
            lanes = slice(half * 128, half * 128 + 128)
            xlo[l : l + 1, lanes] = split[half, l * CX : l * CX + 1, :]
            xhi[l : l + 1, lanes] = split[half, l * CX + CX - 1 : l * CX + CX, :]


def wells_first_kernel(*refs):
    (y_edge, pressure, index, owner, well, rate, column, count, *refs) = refs
    (partials, at_slots, live_out, wells_out, *refs) = refs
    (split, y_edge_v, index_v, owner_v, well_v, rate_v, column_s, count_s, sem) = refs
    copies = load(
        [(pressure.at[:, half * 128 : half * 128 + 128], split.at[half]) for half in range(2)]
        + [
            (y_edge, y_edge_v),
            (column, column_s),
            (count, count_s),
            (index, index_v),
            (owner, owner_v),
            (well, well_v),
            (rate, rate_v),
        ],
        sem,
    )
    for copy in copies:
        copy.wait()
    at = gather_slots(split, column_s)
    at_slots[...] = at
    live = live_index(index_v, count_s)
    live_out[...] = live
    weighted = jnp.sum(live * at, axis=0, keepdims=True)
    total = jnp.sum(live, axis=0, keepdims=True)
    wells = well_row(owner_v, well_v)
    wells_out[...] = wells
    weighted_c, total_c, wells_c = well_columns([weighted, total, wells])
    values = jnp.concatenate(
        [totals_by_well(weighted_c, wells_c) + own_rates(rate_v), totals_by_well(total_c, wells_c)], axis=0
    )
    send_wells(partials, values)
    send_y(partials, y_edge_v[0:8], y_edge_v[8:16])


def wells_next_kernel(split, live, wells, rate, column, partials, at_slots, live_v, wells_v, rate_v, column_s, sem):
    copies = load([(column, column_s), (rate, rate_v), (live, live_v), (wells, wells_v)], sem)
    for copy in copies:
        copy.wait()
    at = gather_slots(split, column_s)
    at_slots[...] = at
    weighted = jnp.sum(live_v[...] * at, axis=0, keepdims=True)
    weighted_c, wells_c = well_columns([weighted, wells_v[...]])
    send_wells(partials, totals_by_well(weighted_c, wells_c) + own_rates(rate_v))
    turned = y_edges([(split.at[0], 0), (split.at[1], 127)])
    send_y(partials, turned[0:4], turned[4:8])


def solve_kernel(first, inputs, *refs):
    away, refs = refs[:inputs], refs[inputs:]
    if first:
        (solved, carried, sums_out, kylo_out, kyhi_out, rims, *refs) = refs
    else:
        (solved, carried, flow_out, *refs) = refs
    held, (rhs, column_s, sem) = refs[:inputs], refs[inputs:]
    (column, partials, live, wells, at_slots, *small, field, kx, ky, source, lower, inverse) = held
    held = dict(zip(range(inputs), held))
    wanted = [(away[0], column_s)] + [(away[n], held[n]) for n in range(1, inputs - 6)]
    if first:
        wanted += [(away[inputs - 6].at[:, half * 128 : half * 128 + 128], field.at[half]) for half in range(2)]
    else:
        wanted += [(away[inputs - 6].at[half], field.at[half]) for half in range(2)]
    wanted += [(away[n], held[n]) for n in range(inputs - 5, inputs)]
    copies = load(wanted, sem)
    for copy in copies[: inputs - 6]:
        copy.wait()
    gx, gy = lax.axis_index("gx"), lax.axis_index("gy")
    block = partials.shape[0] // TILES
    total = partials[0]
    for t in range(1, TILES):
        total = total + partials[block * t]
    if first:
        x_lo, x_hi = small
        kx_lo, kx_hi = x_lo, x_hi
        numerator, index_sum = total[0:2], total[2:4]
        sums_out[...] = index_sum
    else:
        x_lo, x_hi, kx_lo, kx_hi, ky_lo, ky_hi, sums = small
        numerator, index_sum = total, sums[...]
    bottom_hole = numerator / (index_sum + 1.0)
    (wells_c,) = well_columns([wells[...]])
    ids = wells_c[:SLOTS].astype(jnp.int32)
    hole = jnp.zeros((SLOTS, 128), F32)
    for half in range(2):
        hit = ids == lane_ids(SLOTS, 128) + half * 128
        hole = hole + jnp.where(hit, bottom_hole[half : half + 1], 0.0)
    hole = jnp.sum(hole, axis=1, keepdims=True)
    hole = jnp.broadcast_to(hole, (SLOTS, 128))
    hole = jnp.concatenate([hole, jnp.zeros((128 - SLOTS, 128), F32)], axis=0).T[0:1]
    flow = live[...] * (hole - at_slots[...])
    if not first:
        flow_out[...] = flow[:, :SLOTS]

    rows = lax.broadcasted_iota(jnp.int32, (CX, CY), 0)
    lanes = lane_ids(CX, CY)
    from_ylo, from_yhi = from_y(partials, 2)
    if first:
        kylo_out[...] = from_ylo
        kyhi_out[...] = from_yhi
        ylo_c = kylo_c = from_ylo.T
        yhi_c = kyhi_c = from_yhi.T
    else:
        spare = jnp.zeros((4, 128), F32)
        ylo_c = jnp.concatenate([from_ylo, spare], axis=0).T
        yhi_c = jnp.concatenate([from_yhi, spare], axis=0).T
        kylo_c = ky_lo[...].T
        kyhi_c = ky_hi[...].T

    def y_column(turned, base, l):
        s = (l % 2) * CX
        return turned[s : s + CX, base + l // 2 : base + l // 2 + 1]

    for copy in copies[inputs - 6 : inputs - 1]:
        copy.wait()
    for l in range(LZ):
        span = slice(l * CX, (l + 1) * CX)
        f = halves_of(field, span)
        k = kx[span, :]
        f_after = jnp.where(gx < 7, x_hi[l : l + 1, :], 0.0)
        k_after = kx_hi[LZ + l : LZ + l + 1, :]
        f_before = jnp.where(gx > 0, x_lo[l : l + 1, :], 0.0)
        k_before = kx_lo[LZ + l : LZ + l + 1, :]
        f_east = jnp.where(rows == CX - 1, f_after, pltpu.roll(f, CX - 1, 0))
        k_east = jnp.where(rows == CX - 1, k_after, pltpu.roll(k, CX - 1, 0))
        face = k + k_east
        west_first = (k[0:1, :] + k_before) * f_before
        lateral = face * f_east + jnp.where(rows == 0, west_first, pltpu.roll(face * f, 1, 0))
        k = ky[span, :]
        f_after = jnp.where(gy < 3, y_column(yhi_c, 0, l), 0.0)
        k_after = y_column(kyhi_c, 4, l)
        f_before = jnp.where(gy > 0, y_column(ylo_c, 0, l), 0.0)
        k_before = y_column(kylo_c, 4, l)
        f_north = jnp.where(lanes == CY - 1, f_after, pltpu.roll(f, CY - 1, 1))
        k_north = jnp.where(lanes == CY - 1, k_after, pltpu.roll(k, CY - 1, 1))
        face = k + k_north
        south_first = (k[:, 0:1] + k_before) * f_before
        lateral = lateral + face * f_north + jnp.where(lanes == 0, south_first, pltpu.roll(face * f, 1, 1))
        value = source[span, :] + 0.5 * lateral
        rhs[0, span, :] = value[:, :128]
        rhs[1, span, :] = value[:, 128:]

    lanes8 = lane_ids(LZ, 128)
    for s in range(SLOTS):
        place = column_s[0, s]
        x = place // CY
        y = place % CY
        half = y // 128
        lane = y % 128
        part = rhs.at[half]
        where = (pl.ds(x, LZ, stride=CX), slice(None))
        part[where] = part[where] + jnp.where(lanes8 == lane, flow[:, s : s + 1], 0.0)

    for copy in copies[inputs - 1 :]:
        copy.wait()

    def solve_block(b, carry):
        at = pl.multiple_of(b * 8, 8)
        right = [halves_of(rhs, pl.ds(j * CX + at, 8)) for j in range(LZ)]
        here = pl.ds(at, 8)
        for i in range(LZ):
            if first:
                rims[0, i, here, :] = inverse[i, 0, here, :]
                rims[1, i, here, :] = inverse[i, LZ - 1, here, :]
            total = inverse[i, 0, here, :] * right[0]
            for j in range(1, LZ):
                total = total + inverse[i, j, here, :] * right[j]
            solved[pl.ds(i * CX + at, 8), :] = total
            if i == 0:
                carried[1, here, :] = total
            if i == LZ - 1:
                low = lower[here, :]
                carried[0, here, :] = total + inverse[i, i, here, :] * low - low
        return carry

    lax.fori_loop(0, CX // 8, solve_block, 0)


def by_core(body):
    core = lax.axis_index("layer") % 2
    for own in range(2):
        pl.when(core == own)(functools.partial(body, own))


def pair_fixed_kernel(mine, other, out):
    def body(own):
        top, low = (mine, other) if own == 0 else (other, mine)
        out[0] = low[0] * top[0]
        out[1] = top[1] * low[1]
        out[2] = top[2] + top[1] * (low[2] - 1.0) * top[0]

    by_core(body)


def pair_kernel(mine, other, fixed_mine, fixed_other, out):
    def body(own):
        top, low = (mine, other) if own == 0 else (other, mine)
        fixed_top, fixed_low = (fixed_mine, fixed_other) if own == 0 else (fixed_other, fixed_mine)
        out[0] = fixed_low[0] * top[0] + low[0]
        out[1] = top[1] + fixed_top[1] * (low[1] + fixed_low[2] * top[0] - top[0])

    by_core(body)


def sweep_kernel(last, *refs):
    cds, fixed, refs = refs[:4], refs[4:8], refs[8:]
    cd_mine, cd_other, fixed_mine, fixed_other, solved, rims, *refs = refs
    if last:
        (field,) = refs
    else:
        split, lower, xlo, xhi = refs
    me = lax.axis_index("layer")

    def position(own):
        chip = own // 2

        def block(b, carry):
            here = pl.ds(pl.multiple_of(b * 8, 8), 8)
            upper = jnp.zeros((8, CY), F32)
            uppers = [upper]
            for c in range(3):
                d = (chip - c) % 4
                upper = fixed[d][0, here, :] * upper + cds[d][0, here, :]
                uppers.append(upper)
            low = jnp.zeros((8, CY), F32)
            for c in range(3, chip, -1):
                d = (chip - c) % 4
                step = cds[d][1, here, :] + fixed[d][2, here, :] * uppers[c] - uppers[c]
                low = fixed[d][1, here, :] * low + step
            upper = uppers[chip]
            if own % 2 == 0:
                below = fixed_mine[0, here, :] * upper + cd_mine[0, here, :]
                step = cd_other[1, here, :] + fixed_other[2, here, :] * below - below
                low = fixed_other[1, here, :] * low + step
            else:
                upper = fixed_other[0, here, :] * upper + cd_other[0, here, :]
            for i in range(LZ):
                span = pl.ds(pl.multiple_of(i * CX + b * 8, 8), 8)
                value = solved[span, :] + rims[0, i, here, :] * upper + rims[1, i, here, :] * low
                if last:
                    field[span, :] = value
                else:
                    split[0, span, :] = value[:, :128]
                    split[1, span, :] = value[:, 128:]
            if not last:
                lower[here, :] = low
            return carry

        @pl.when(me == own)
        def _():
            lax.fori_loop(0, CX // 8, block, 0)

    for own in range(GROUPS):
        position(own)
    if not last:
        split_x_edges(split, xlo, xhi)


def params(mib=8.0):
    return pltpu.CompilerParams(vmem_limit_bytes=int(mib * 1024) * 1024)


def around(n, step):
    return [(i, (i + step) % n) for i in range(n)]


def from_sides(xlo, xhi):
    return (lax.ppermute(xhi, "gx", around(8, 1)), lax.ppermute(xlo, "gx", around(8, -1)))


def swapped(value):
    return lax.ppermute(value, "layer", [(i, i ^ 1) for i in range(GROUPS)])


def all_chips(value):
    return [value] + [lax.ppermute(value, "layer", around(GROUPS, 2 * d)) for d in range(1, 4)]


def whole(kernel, name, out_shape, *operands):
    return pl.pallas_call(
        kernel,
        out_shape=out_shape,
        in_specs=[VMEM] * len(operands),
        out_specs=jax.tree.map(lambda _: VMEM, out_shape),
        compiler_params=params(),
        name=name,
    )(*operands)


def shards(
    pressure,
    source,
    perm_x,
    perm_y,
    line_inverse,
    robin_below,
    tile_count,
    perf_owner,
    perf_well,
    perf_column,
    perf_index,
    well_rate,
):
    rows = LZ * CX
    pressure = pressure.reshape(rows, CY)
    source = source.reshape(rows, CY)
    inverse = line_inverse[0]
    lower = robin_below[0]
    owner = perf_owner[0].T
    index = perf_index[0].T

    kx = perm_x.reshape(rows, CY)
    ky = perm_y.reshape(rows, CY)
    *edges, y_edge, fixed = pl.pallas_call(
        edges_kernel,
        out_shape=(shape(16, CY), shape(16, CY), shape(16, 128), shape(3, CX, CY)),
        in_specs=[ANY] * 4,
        out_specs=(VMEM,) * 4,
        scratch_shapes=[
            pltpu.VMEM((2, rows, 128), F32),
            pltpu.VMEM((LZ, 8, CY), F32),
            pltpu.VMEM((LZ, 8, CY), F32),
            pltpu.VMEM((rows, CY), F32),
            pltpu.SemaphoreType.DMA((8,)),
        ],
        compiler_params=params(EDGE_MIB),
        name="first_edges",
    )(pressure, perm_x, ky, inverse)
    sides = from_sides(*edges)
    fixed_other = swapped(fixed)
    fixed_pair = whole(pair_fixed_kernel, "pair_fixed", shape(3, CX, CY), fixed, fixed_other)
    fixed_chips = all_chips(fixed_pair)
    partials, at_slots, live, wells = pl.pallas_call(
        wells_first_kernel,
        out_shape=(shape(3 * TILES, 4, 128), shape(LZ, 128), shape(LZ, 128), shape(1, 128)),
        in_specs=[ANY] * 8,
        out_specs=(VMEM,) * 4,
        scratch_shapes=[
            pltpu.VMEM((2, rows, 128), F32),
            pltpu.VMEM((16, 128), F32),
            pltpu.VMEM((LZ, SLOTS), F32),
            pltpu.VMEM((1, SLOTS), jnp.int32),
            pltpu.VMEM((1, SLOTS), jnp.int32),
            pltpu.VMEM((1, 8), F32),
            pltpu.SMEM((1, SLOTS), jnp.int32),
            pltpu.SMEM((1, 1), jnp.int32),
            pltpu.SemaphoreType.DMA((9,)),
        ],
        compiler_params=params(WELLS_MIB),
        name="first_wells",
    )(y_edge, pressure, index, owner, perf_well, well_rate, perf_column, tile_count)
    field = pressure
    k_sides = sides
    ky_sides = sums = None
    for sweep_step in range(ITERS):
        first, last = sweep_step == 0, sweep_step == ITERS - 1
        if first:
            partials, fixed_pair = lax.optimization_barrier((partials, fixed_pair))
        spread = lax.all_to_all(partials, ("gx", "gy"), split_axis=0, concat_axis=0, tiled=True)
        if first:
            spread, *fixed_chips = lax.optimization_barrier((spread, *fixed_chips))
        small = sides if first else (*sides, *k_sides, *ky_sides, sums)
        operands = (perf_column, spread, live, wells, at_slots, *small, field, kx, ky, source, lower, inverse)
        held = [pltpu.VMEM(value.shape, value.dtype) for value in operands]
        held[len(operands) - 6] = pltpu.VMEM((2, rows, 128), F32)
        solved, carried, *small = pl.pallas_call(
            functools.partial(solve_kernel, first, len(operands)),
            out_shape=(shape(rows, CY), shape(2, CX, CY))
            + ((shape(2, 128), shape(8, 128), shape(8, 128), shape(2, LZ, CX, CY)) if first else (shape(LZ, SLOTS),)),
            in_specs=[ANY] * len(operands),
            out_specs=(VMEM,) * (6 if first else 3),
            scratch_shapes=held
            + [
                pltpu.VMEM((2, rows, 128), F32),
                pltpu.SMEM((1, SLOTS), jnp.int32),
                pltpu.SemaphoreType.DMA((len(operands) + 1,)),
            ],
            compiler_params=params(SOLVE_MIB),
            name="solve_lines",
        )(*operands)
        if first:
            *small, rims = small
        other = swapped(carried)
        chips = all_chips(whole(pair_kernel, "pair", shape(2, CX, CY), carried, other, fixed, fixed_other))
        planes = (*chips, *fixed_chips, carried, other, fixed, fixed_other, solved, rims)
        if last:
            (field,) = whole(functools.partial(sweep_kernel, True), "sweep_last", (shape(rows, CY),), *planes)
            (flow,) = small
            break
        sums, *ky_sides = small
        field, lower, *edges = whole(
            functools.partial(sweep_kernel, False),
            "sweep_mid",
            (shape(2, rows, 128), shape(CX, CY), shape(8, CY), shape(8, CY)),
            *planes,
        )
        sides = from_sides(*edges)
        partials, at_slots = pl.pallas_call(
            wells_next_kernel,
            out_shape=(shape(3 * TILES, 2, 128), shape(LZ, 128)),
            in_specs=[VMEM] + [ANY] * 4,
            out_specs=(VMEM,) * 2,
            scratch_shapes=[
                pltpu.VMEM((LZ, 128), F32),
                pltpu.VMEM((1, 128), F32),
                pltpu.VMEM((1, 8), F32),
                pltpu.SMEM((1, SLOTS), jnp.int32),
                pltpu.SemaphoreType.DMA((4,)),
            ],
            compiler_params=params(),
            name="next_wells",
        )(field, live, wells, well_rate, perf_column)
    return (field.reshape(LZ, CX, CY), flow.T[None])


def solution(mesh):
    placed = (
        P("layer", "gx", "gy"),
        P("layer", "gx", "gy"),
        P("layer", "gx", "gy"),
        P("layer", "gx", "gy"),
        P("layer", None, None, "gx", "gy"),
        P("layer", "gx", "gy"),
        P("layer", ("gx", "gy")),
        P("layer", ("gx", "gy"), None),
        P("layer", ("gx", "gy")),
        P("layer", ("gx", "gy")),
        P("layer", ("gx", "gy"), None),
        P("layer", ("gx", "gy")),
    )
    return jax.shard_map(
        shards,
        mesh=mesh,
        in_specs=placed,
        out_specs=(P("layer", "gx", "gy"), P("layer", ("gx", "gy"), None)),
        check_vma=False,
    )
```

```python
import functools

import jax
import jax.numpy as jnp
from jax import lax
from jax.experimental import pallas as pl
from jax.experimental.pallas import tpu as pltpu
from jax.sharding import PartitionSpec as P

ITERS = 2
EDGE_MIB = 53.0
WELLS_MIB = 52.0
SOLVE_MIB = 52.0
LZ = 8
CX = 64
CY = 256
HALF = CX // 2
SLOTS = 48
WELLS = 256
TILES = 32
GROUPS = 8
F32 = jnp.float32
VMEM = pl.BlockSpec(memory_space=pltpu.VMEM)
SMEM = pl.BlockSpec(memory_space=pltpu.SMEM)
ANY = pl.BlockSpec(memory_space=pltpu.HBM)


def shape(*dims):
    return jax.ShapeDtypeStruct(dims, F32)


def lane_ids(rows, lanes):
    return lax.broadcasted_iota(jnp.int32, (rows, lanes), 1)


def x_edges(ref, row, out, first):
    for l in range(LZ):
        out[first + l : first + l + 1, :] = ref[l * CX + row : l * CX + row + 1, :]


def y_edges(pieces):
    lanes = lane_ids(2 * CX, 128)
    packed = jnp.zeros((2 * CX, 128), F32)
    row = 0
    for ref, column in pieces:
        start = (column // 128) * 128
        for r in range(LZ // 2):
            block = ref[r * 2 * CX : (r + 1) * 2 * CX, start : start + 128]
            value = block[:, column - start : column - start + 1]
            packed = jnp.where(lanes == row, value, packed)
            row += 1
    return packed.T


def gather_slots(split_ref, column_ref):
    lanes = lane_ids(LZ, 128)
    found = jnp.zeros((LZ, 128), F32)
    for s in range(SLOTS):
        column = column_ref[0, s]
        x = column // CY
        y = column % CY
        half = y // 128
        lane = y % 128
        block = split_ref.at[half][pl.ds(x, LZ, stride=CX), :]
        value = jnp.sum(jnp.where(lanes == lane, block, 0.0), axis=1, keepdims=True)
        found = jnp.where(lanes == s, value, found)
    return found


def well_columns(rows):
    block = jnp.concatenate(rows + [jnp.zeros((8 - len(rows), 128), F32)], axis=0)
    turned = block.T
    return [turned[:, i : i + 1] for i in range(len(rows))]


def pad_lanes(value):
    return jnp.concatenate([value, jnp.zeros((value.shape[0], 128 - value.shape[1]), value.dtype)], axis=1)


def own_tile():
    return lax.axis_index("gx") * 4 + lax.axis_index("gy")


def tile_at(step):
    return lax.rem(own_tile() + step + TILES, TILES)


def send_wells(out, wells):
    count = out.shape[0] // TILES
    for t in range(TILES):
        out[t * count] = wells


def send_y(out, lower_edge, upper_edge):
    count, rows, _ = out.shape
    count = count // TILES
    for step, edge in ((1, upper_edge), (-1, lower_edge)):
        first = tile_at(step) * count + 1
        for n in range(edge.shape[0] // rows):
            out[first + n] = edge[n * rows : (n + 1) * rows]


def from_y(spread, blocks):
    count = spread.shape[0] // TILES
    result = []
    for step in (-1, 1):
        first = tile_at(step) * count + 1
        result.append(jnp.concatenate([spread[first + n] for n in range(blocks)], axis=0))
    return result


def live_index(index_ref, count_ref):
    index = pad_lanes(index_ref[...])
    return jnp.where(lane_ids(LZ, 128) < count_ref[0, 0], index, 0.0)


def well_row(owner_ref, well_ref):
    return pad_lanes((owner_ref[...] * 8 + well_ref[...]).astype(F32))


def totals_by_well(column, well_column):
    ids = well_column[:SLOTS].astype(jnp.int32)
    halves = []
    for half in range(2):
        hit = ids == lane_ids(SLOTS, 128) + half * 128
        halves.append(jnp.sum(jnp.where(hit, column[:SLOTS], 0.0), axis=0, keepdims=True))
    return jnp.concatenate(halves, axis=0)


def own_rates(rate_ref):
    tile = own_tile()
    rate = rate_ref[...]
    tiled = jnp.concatenate([rate] * 16, axis=1)
    lanes = lane_ids(1, 128)
    halves = [jnp.where((lanes + half * 128) // 8 == tile, tiled, 0.0) for half in range(2)]
    return jnp.concatenate(halves, axis=0)


def load(copies, sem):
    started = [pltpu.make_async_copy(source, target, sem.at[n]) for n, (source, target) in enumerate(copies)]
    for copy in started:
        copy.start()
    return started


def halves_of(split, span):
    return jnp.concatenate([split[0, span, :], split[1, span, :]], axis=1)


def rows_of(side):
    core = lax.rem(lax.axis_index("layer") + side, 2)
    return pl.ds(pl.multiple_of(core * HALF, HALF), HALF)


def edges_kernel(pressure, perm_x, perm_y, inverse, xlo, xhi, y_edge, fixed, fixed_give, split, kx_lo, kx_hi, ky, sem):
    copies = load(
        [(pressure.at[:, half * 128 : half * 128 + 128], split.at[half]) for half in range(2)]
        + [(perm_x.at[:, 0:8], kx_lo), (perm_x.at[:, CX - 8 : CX], kx_hi), (perm_y, ky)]
        + [
            (inverse.at[i, j, rows_of(side)], target.at[n])
            for n, (i, j) in enumerate(((LZ - 1, 0), (0, LZ - 1), (0, 0)))
            for side, target in ((0, fixed), (1, fixed_give))
        ],
        sem,
    )
    for copy in copies[:5]:
        copy.wait()
    split_x_edges(split, xlo, xhi)
    for l in range(LZ):
        xlo[LZ + l : LZ + l + 1, :] = kx_lo[l, 0:1, :]
        xhi[LZ + l : LZ + l + 1, :] = kx_hi[l, 7:8, :]
    y_edge[...] = y_edges([(split.at[0], 0), (ky, 0), (split.at[1], 127), (ky, CY - 1)])[0:16]
    for copy in copies[5:]:
        copy.wait()


def split_x_edges(split, xlo, xhi):
    for l in range(LZ):
        for half in range(2):
            lanes = slice(half * 128, half * 128 + 128)
            xlo[l : l + 1, lanes] = split[half, l * CX : l * CX + 1, :]
            xhi[l : l + 1, lanes] = split[half, l * CX + CX - 1 : l * CX + CX, :]


def wells_first_kernel(*refs):
    (y_edge, pressure, index, owner, well, rate, column, count, *refs) = refs
    (partials, at_slots, live_out, wells_out, *refs) = refs
    (split, y_edge_v, index_v, owner_v, well_v, rate_v, column_s, count_s, sem) = refs
    copies = load(
        [(pressure.at[:, half * 128 : half * 128 + 128], split.at[half]) for half in range(2)]
        + [
            (y_edge, y_edge_v),
            (column, column_s),
            (count, count_s),
            (index, index_v),
            (owner, owner_v),
            (well, well_v),
            (rate, rate_v),
        ],
        sem,
    )
    for copy in copies:
        copy.wait()
    at = gather_slots(split, column_s)
    at_slots[...] = at
    live = live_index(index_v, count_s)
    live_out[...] = live
    weighted = jnp.sum(live * at, axis=0, keepdims=True)
    total = jnp.sum(live, axis=0, keepdims=True)
    wells = well_row(owner_v, well_v)
    wells_out[...] = wells
    weighted_c, total_c, wells_c = well_columns([weighted, total, wells])
    values = jnp.concatenate(
        [totals_by_well(weighted_c, wells_c) + own_rates(rate_v), totals_by_well(total_c, wells_c)], axis=0
    )
    send_wells(partials, values)
    send_y(partials, y_edge_v[0:8], y_edge_v[8:16])


def wells_next_kernel(split, live, wells, rate, column, partials, at_slots, live_v, wells_v, rate_v, column_s, sem):
    copies = load([(column, column_s), (rate, rate_v), (live, live_v), (wells, wells_v)], sem)
    for copy in copies:
        copy.wait()
    at = gather_slots(split, column_s)
    at_slots[...] = at
    weighted = jnp.sum(live_v[...] * at, axis=0, keepdims=True)
    weighted_c, wells_c = well_columns([weighted, wells_v[...]])
    send_wells(partials, totals_by_well(weighted_c, wells_c) + own_rates(rate_v))
    turned = y_edges([(split.at[0], 0), (split.at[1], 127)])
    send_y(partials, turned[0:4], turned[4:8])


def solve_kernel(first, inputs, *refs):
    away, refs = refs[:inputs], refs[inputs:]
    if first:
        (solved, keep, give, sums_out, kylo_out, kyhi_out, rims, *refs) = refs
    else:
        (solved, keep, give, flow_out, *refs) = refs
    held, (rhs, carried, column_s, sem) = refs[:inputs], refs[inputs:]
    (column, partials, live, wells, at_slots, *small, field, kx, ky, source, lower, inverse) = held
    held = dict(zip(range(inputs), held))
    wanted = [(away[0], column_s)] + [(away[n], held[n]) for n in range(1, inputs - 6)]
    if first:
        wanted += [(away[inputs - 6].at[:, half * 128 : half * 128 + 128], field.at[half]) for half in range(2)]
    else:
        wanted += [(away[inputs - 6].at[half], field.at[half]) for half in range(2)]
    wanted += [(away[n], held[n]) for n in range(inputs - 5, inputs)]
    copies = load(wanted, sem)
    for copy in copies[: inputs - 6]:
        copy.wait()
    gx, gy = lax.axis_index("gx"), lax.axis_index("gy")
    block = partials.shape[0] // TILES
    total = partials[0]
    for t in range(1, TILES):
        total = total + partials[block * t]
    if first:
        x_lo, x_hi = small
        kx_lo, kx_hi = x_lo, x_hi
        numerator, index_sum = total[0:2], total[2:4]
        sums_out[...] = index_sum
    else:
        x_lo, x_hi, kx_lo, kx_hi, ky_lo, ky_hi, sums = small
        numerator, index_sum = total, sums[...]
    bottom_hole = numerator / (index_sum + 1.0)
    (wells_c,) = well_columns([wells[...]])
    ids = wells_c[:SLOTS].astype(jnp.int32)
    hole = jnp.zeros((SLOTS, 128), F32)
    for half in range(2):
        hit = ids == lane_ids(SLOTS, 128) + half * 128
        hole = hole + jnp.where(hit, bottom_hole[half : half + 1], 0.0)
    hole = jnp.sum(hole, axis=1, keepdims=True)
    hole = jnp.broadcast_to(hole, (SLOTS, 128))
    hole = jnp.concatenate([hole, jnp.zeros((128 - SLOTS, 128), F32)], axis=0).T[0:1]
    flow = live[...] * (hole - at_slots[...])
    if not first:
        flow_out[...] = flow[:, :SLOTS]

    rows = lax.broadcasted_iota(jnp.int32, (CX, CY), 0)
    lanes = lane_ids(CX, CY)
    from_ylo, from_yhi = from_y(partials, 2)
    if first:
        kylo_out[...] = from_ylo
        kyhi_out[...] = from_yhi
        ylo_c = kylo_c = from_ylo.T
        yhi_c = kyhi_c = from_yhi.T
    else:
        spare = jnp.zeros((4, 128), F32)
        ylo_c = jnp.concatenate([from_ylo, spare], axis=0).T
        yhi_c = jnp.concatenate([from_yhi, spare], axis=0).T
        kylo_c = ky_lo[...].T
        kyhi_c = ky_hi[...].T

    def y_column(turned, base, l):
        s = (l % 2) * CX
        return turned[s : s + CX, base + l // 2 : base + l // 2 + 1]

    for copy in copies[inputs - 6 : inputs - 1]:
        copy.wait()
    for l in range(LZ):
        span = slice(l * CX, (l + 1) * CX)
        f = halves_of(field, span)
        k = kx[span, :]
        f_after = jnp.where(gx < 7, x_hi[l : l + 1, :], 0.0)
        k_after = kx_hi[LZ + l : LZ + l + 1, :]
        f_before = jnp.where(gx > 0, x_lo[l : l + 1, :], 0.0)
        k_before = kx_lo[LZ + l : LZ + l + 1, :]
        f_east = jnp.where(rows == CX - 1, f_after, pltpu.roll(f, CX - 1, 0))
        k_east = jnp.where(rows == CX - 1, k_after, pltpu.roll(k, CX - 1, 0))
        face = k + k_east
        west_first = (k[0:1, :] + k_before) * f_before
        lateral = face * f_east + jnp.where(rows == 0, west_first, pltpu.roll(face * f, 1, 0))
        k = ky[span, :]
        f_after = jnp.where(gy < 3, y_column(yhi_c, 0, l), 0.0)
        k_after = y_column(kyhi_c, 4, l)
        f_before = jnp.where(gy > 0, y_column(ylo_c, 0, l), 0.0)
        k_before = y_column(kylo_c, 4, l)
        f_north = jnp.where(lanes == CY - 1, f_after, pltpu.roll(f, CY - 1, 1))
        k_north = jnp.where(lanes == CY - 1, k_after, pltpu.roll(k, CY - 1, 1))
        face = k + k_north
        south_first = (k[:, 0:1] + k_before) * f_before
        lateral = lateral + face * f_north + jnp.where(lanes == 0, south_first, pltpu.roll(face * f, 1, 1))
        value = source[span, :] + 0.5 * lateral
        rhs[0, span, :] = value[:, :128]
        rhs[1, span, :] = value[:, 128:]

    lanes8 = lane_ids(LZ, 128)
    for s in range(SLOTS):
        place = column_s[0, s]
        x = place // CY
        y = place % CY
        half = y // 128
        lane = y % 128
        part = rhs.at[half]
        where = (pl.ds(x, LZ, stride=CX), slice(None))
        part[where] = part[where] + jnp.where(lanes8 == lane, flow[:, s : s + 1], 0.0)

    for copy in copies[inputs - 1 :]:
        copy.wait()

    def solve_block(b, carry):
        at = pl.multiple_of(b * 8, 8)
        right = [halves_of(rhs, pl.ds(j * CX + at, 8)) for j in range(LZ)]
        here = pl.ds(at, 8)
        for i in range(LZ):
            if first:
                rims[0, i, here, :] = inverse[i, 0, here, :]
                rims[1, i, here, :] = inverse[i, LZ - 1, here, :]
            total = inverse[i, 0, here, :] * right[0]
            for j in range(1, LZ):
                total = total + inverse[i, j, here, :] * right[j]
            solved[pl.ds(i * CX + at, 8), :] = total
            if i == 0:
                carried[1, here, :] = total
            if i == LZ - 1:
                low = lower[here, :]
                carried[0, here, :] = total + inverse[i, i, here, :] * low - low
        return carry

    lax.fori_loop(0, CX // 8, solve_block, 0)
    for side, out in ((0, keep), (1, give)):
        out[...] = carried[:, rows_of(side), :]


def by_core(body):
    core = lax.axis_index("layer") % 2
    for own in range(2):
        pl.when(core == own)(functools.partial(body, own))


def pair_fixed_kernel(mine, other, out):
    def body(own):
        top, low = (mine, other) if own == 0 else (other, mine)
        out[0] = low[0] * top[0]
        out[1] = top[1] * low[1]
        out[2] = top[2] + top[1] * (low[2] - 1.0) * top[0]

    by_core(body)


def pair_kernel(mine, other, fixed_mine, fixed_other, out):
    def body(own):
        top, low = (mine, other) if own == 0 else (other, mine)
        fixed_top, fixed_low = (fixed_mine, fixed_other) if own == 0 else (fixed_other, fixed_mine)
        out[0] = fixed_low[0] * top[0] + low[0]
        out[1] = top[1] + fixed_top[1] * (low[1] + fixed_low[2] * top[0] - top[0])

    by_core(body)


def chain_kernel(*refs):
    cds, fixed, refs = refs[:4], refs[4:8], refs[8:]
    cd_mine, cd_other, fixed_mine, fixed_other, mine, give = refs
    me = lax.axis_index("layer")

    def position(own):
        chip, even = own // 2, own % 2 == 0
        cd_top, cd_low = (cd_mine, cd_other) if even else (cd_other, cd_mine)
        fixed_top, fixed_low = (fixed_mine, fixed_other) if even else (fixed_other, fixed_mine)
        out_top, out_low = (mine, give) if even else (give, mine)

        def block(b, carry):
            here = pl.ds(pl.multiple_of(b * 8, 8), 8)
            uppers = [jnp.zeros((8, CY), F32)]
            for c in range(3):
                d = (chip - c) % 4
                uppers.append(fixed[d][0, here, :] * uppers[-1] + cds[d][0, here, :])
            low = jnp.zeros((8, CY), F32)
            for c in range(3, chip, -1):
                d = (chip - c) % 4
                step = cds[d][1, here, :] + fixed[d][2, here, :] * uppers[c] - uppers[c]
                low = fixed[d][1, here, :] * low + step
            upper = uppers[chip]
            below = fixed_top[0, here, :] * upper + cd_top[0, here, :]
            step = cd_low[1, here, :] + fixed_low[2, here, :] * below - below
            out_top[0, here, :] = upper
            out_top[1, here, :] = fixed_low[1, here, :] * low + step
            out_low[0, here, :] = below
            out_low[1, here, :] = low
            return carry

        @pl.when(me == own)
        def _():
            lax.fori_loop(0, HALF // 8, block, 0)

    for own in range(GROUPS):
        position(own)


def sweep_kernel(last, mine, other, solved, rims, *refs):
    if last:
        (field,) = refs
    else:
        split, lower, xlo, xhi = refs

    def body(own):
        for side in range(2):
            ends = mine if side == own else other

            def block(b, carry):
                there = pl.ds(pl.multiple_of(b * 8, 8), 8)
                here = pl.ds(pl.multiple_of(side * HALF + b * 8, 8), 8)
                upper, low = ends[0, there, :], ends[1, there, :]
                for i in range(LZ):
                    span = pl.ds(pl.multiple_of(i * CX + side * HALF + b * 8, 8), 8)
                    value = solved[span, :] + rims[0, i, here, :] * upper + rims[1, i, here, :] * low
                    if last:
                        field[span, :] = value
                    else:
                        split[0, span, :] = value[:, :128]
                        split[1, span, :] = value[:, 128:]
                if not last:
                    lower[here, :] = low
                return carry

            lax.fori_loop(0, HALF // 8, block, 0)

    by_core(body)
    if not last:
        split_x_edges(split, xlo, xhi)


def params(mib=8.0):
    return pltpu.CompilerParams(vmem_limit_bytes=int(mib * 1024) * 1024)


def around(n, step):
    return [(i, (i + step) % n) for i in range(n)]


def from_sides(xlo, xhi):
    return (lax.ppermute(xhi, "gx", around(8, 1)), lax.ppermute(xlo, "gx", around(8, -1)))


def swapped(value):
    return lax.ppermute(value, "layer", [(i, i ^ 1) for i in range(GROUPS)])


def all_chips(value):
    return [value] + [lax.ppermute(value, "layer", around(GROUPS, 2 * d)) for d in range(1, 4)]


def whole(kernel, name, out_shape, *operands):
    return pl.pallas_call(
        kernel,
        out_shape=out_shape,
        in_specs=[VMEM] * len(operands),
        out_specs=jax.tree.map(lambda _: VMEM, out_shape),
        compiler_params=params(),
        name=name,
    )(*operands)


def shards(
    pressure,
    source,
    perm_x,
    perm_y,
    line_inverse,
    robin_below,
    tile_count,
    perf_owner,
    perf_well,
    perf_column,
    perf_index,
    well_rate,
):
    rows = LZ * CX
    pressure = pressure.reshape(rows, CY)
    source = source.reshape(rows, CY)
    inverse = line_inverse[0]
    lower = robin_below[0]
    owner = perf_owner[0].T
    index = perf_index[0].T

    kx = perm_x.reshape(rows, CY)
    ky = perm_y.reshape(rows, CY)
    *edges, y_edge, fixed, fixed_give = pl.pallas_call(
        edges_kernel,
        out_shape=(shape(16, CY), shape(16, CY), shape(16, 128), shape(3, HALF, CY), shape(3, HALF, CY)),
        in_specs=[ANY] * 4,
        out_specs=(VMEM,) * 5,
        scratch_shapes=[
            pltpu.VMEM((2, rows, 128), F32),
            pltpu.VMEM((LZ, 8, CY), F32),
            pltpu.VMEM((LZ, 8, CY), F32),
            pltpu.VMEM((rows, CY), F32),
            pltpu.SemaphoreType.DMA((11,)),
        ],
        compiler_params=params(EDGE_MIB),
        name="first_edges",
    )(pressure, perm_x, ky, inverse)
    sides = from_sides(*edges)
    fixed_other = swapped(fixed_give)
    fixed_pair = whole(pair_fixed_kernel, "pair_fixed", shape(3, HALF, CY), fixed, fixed_other)
    fixed_chips = all_chips(fixed_pair)
    partials, at_slots, live, wells = pl.pallas_call(
        wells_first_kernel,
        out_shape=(shape(3 * TILES, 4, 128), shape(LZ, 128), shape(LZ, 128), shape(1, 128)),
        in_specs=[ANY] * 8,
        out_specs=(VMEM,) * 4,
        scratch_shapes=[
            pltpu.VMEM((2, rows, 128), F32),
            pltpu.VMEM((16, 128), F32),
            pltpu.VMEM((LZ, SLOTS), F32),
            pltpu.VMEM((1, SLOTS), jnp.int32),
            pltpu.VMEM((1, SLOTS), jnp.int32),
            pltpu.VMEM((1, 8), F32),
            pltpu.SMEM((1, SLOTS), jnp.int32),
            pltpu.SMEM((1, 1), jnp.int32),
            pltpu.SemaphoreType.DMA((9,)),
        ],
        compiler_params=params(WELLS_MIB),
        name="first_wells",
    )(y_edge, pressure, index, owner, perf_well, well_rate, perf_column, tile_count)
    field = pressure
    k_sides = sides
    ky_sides = sums = None
    for sweep_step in range(ITERS):
        first, last = sweep_step == 0, sweep_step == ITERS - 1
        if first:
            partials, fixed_pair = lax.optimization_barrier((partials, fixed_pair))
        spread = lax.all_to_all(partials, ("gx", "gy"), split_axis=0, concat_axis=0, tiled=True)
        if first:
            spread, *fixed_chips = lax.optimization_barrier((spread, *fixed_chips))
        small = sides if first else (*sides, *k_sides, *ky_sides, sums)
        operands = (perf_column, spread, live, wells, at_slots, *small, field, kx, ky, source, lower, inverse)
        held = [pltpu.VMEM(value.shape, value.dtype) for value in operands]
        held[len(operands) - 6] = pltpu.VMEM((2, rows, 128), F32)
        solved, carried, give, *small = pl.pallas_call(
            functools.partial(solve_kernel, first, len(operands)),
            out_shape=(shape(rows, CY), shape(2, HALF, CY), shape(2, HALF, CY))
            + ((shape(2, 128), shape(8, 128), shape(8, 128), shape(2, LZ, CX, CY)) if first else (shape(LZ, SLOTS),)),
            in_specs=[ANY] * len(operands),
            out_specs=(VMEM,) * (7 if first else 4),
            scratch_shapes=held
            + [
                pltpu.VMEM((2, rows, 128), F32),
                pltpu.VMEM((2, CX, CY), F32),
                pltpu.SMEM((1, SLOTS), jnp.int32),
                pltpu.SemaphoreType.DMA((len(operands) + 1,)),
            ],
            compiler_params=params(SOLVE_MIB),
            name="solve_lines",
        )(*operands)
        if first:
            *small, rims = small
        other = swapped(give)
        chips = all_chips(whole(pair_kernel, "pair", shape(2, HALF, CY), carried, other, fixed, fixed_other))
        ends, ends_give = whole(
            chain_kernel,
            "chain",
            (shape(2, HALF, CY),) * 2,
            *(*chips, *fixed_chips, carried, other, fixed, fixed_other),
        )
        planes = (ends, swapped(ends_give), solved, rims)
        if last:
            (field,) = whole(functools.partial(sweep_kernel, True), "sweep_last", (shape(rows, CY),), *planes)
            (flow,) = small
            break
        sums, *ky_sides = small
        field, lower, *edges = whole(
            functools.partial(sweep_kernel, False),
            "sweep_mid",
            (shape(2, rows, 128), shape(CX, CY), shape(8, CY), shape(8, CY)),
            *planes,
        )
        sides = from_sides(*edges)
        partials, at_slots = pl.pallas_call(
            wells_next_kernel,
            out_shape=(shape(3 * TILES, 2, 128), shape(LZ, 128)),
            in_specs=[VMEM] + [ANY] * 4,
            out_specs=(VMEM,) * 2,
            scratch_shapes=[
                pltpu.VMEM((LZ, 128), F32),
                pltpu.VMEM((1, 128), F32),
                pltpu.VMEM((1, 8), F32),
                pltpu.SMEM((1, SLOTS), jnp.int32),
                pltpu.SemaphoreType.DMA((4,)),
            ],
            compiler_params=params(),
            name="next_wells",
        )(field, live, wells, well_rate, perf_column)
    return (field.reshape(LZ, CX, CY), flow.T[None])


def solution(mesh):
    placed = (
        P("layer", "gx", "gy"),
        P("layer", "gx", "gy"),
        P("layer", "gx", "gy"),
        P("layer", "gx", "gy"),
        P("layer", None, None, "gx", "gy"),
        P("layer", "gx", "gy"),
        P("layer", ("gx", "gy")),
        P("layer", ("gx", "gy"), None),
        P("layer", ("gx", "gy")),
        P("layer", ("gx", "gy")),
        P("layer", ("gx", "gy"), None),
        P("layer", ("gx", "gy")),
    )
    return jax.shard_map(
        shards,
        mesh=mesh,
        in_specs=placed,
        out_specs=(P("layer", "gx", "gy"), P("layer", ("gx", "gy"), None)),
        check_vma=False,
    )
```

```python
import functools

import jax
import jax.numpy as jnp
from jax import lax
from jax.experimental import pallas as pl
from jax.experimental.pallas import tpu as pltpu
from jax.sharding import PartitionSpec as P

ITERS = 2
EDGE_MIB = 53.0
WELLS_MIB = 52.0
SOLVE_MIB = 52.0
LATERAL_MIB = 52.0
LZ = 8
CX = 64
CY = 256
HALF = CX // 2
SLOTS = 48
WELLS = 256
TILES = 32
GROUPS = 8
F32 = jnp.float32
VMEM = pl.BlockSpec(memory_space=pltpu.VMEM)
SMEM = pl.BlockSpec(memory_space=pltpu.SMEM)
ANY = pl.BlockSpec(memory_space=pltpu.HBM)


def shape(*dims):
    return jax.ShapeDtypeStruct(dims, F32)


def lane_ids(rows, lanes):
    return lax.broadcasted_iota(jnp.int32, (rows, lanes), 1)


def x_edges(ref, row, out, first):
    for l in range(LZ):
        out[first + l : first + l + 1, :] = ref[l * CX + row : l * CX + row + 1, :]


def y_edges(pieces):
    lanes = lane_ids(2 * CX, 128)
    packed = jnp.zeros((2 * CX, 128), F32)
    row = 0
    for ref, column in pieces:
        start = (column // 128) * 128
        for r in range(LZ // 2):
            block = ref[r * 2 * CX : (r + 1) * 2 * CX, start : start + 128]
            value = block[:, column - start : column - start + 1]
            packed = jnp.where(lanes == row, value, packed)
            row += 1
    return packed.T


def gather_slots(split_ref, column_ref):
    lanes = lane_ids(LZ, 128)
    found = jnp.zeros((LZ, 128), F32)
    for s in range(SLOTS):
        column = column_ref[0, s]
        x = column // CY
        y = column % CY
        half = y // 128
        lane = y % 128
        block = split_ref.at[half][pl.ds(x, LZ, stride=CX), :]
        value = jnp.sum(jnp.where(lanes == lane, block, 0.0), axis=1, keepdims=True)
        found = jnp.where(lanes == s, value, found)
    return found


def well_columns(rows):
    block = jnp.concatenate(rows + [jnp.zeros((8 - len(rows), 128), F32)], axis=0)
    turned = block.T
    return [turned[:, i : i + 1] for i in range(len(rows))]


def pad_lanes(value):
    return jnp.concatenate([value, jnp.zeros((value.shape[0], 128 - value.shape[1]), value.dtype)], axis=1)


def own_tile():
    return lax.axis_index("gx") * 4 + lax.axis_index("gy")


def tile_at(step):
    return lax.rem(own_tile() + step + TILES, TILES)


def send_wells(out, wells):
    count = out.shape[0] // TILES
    for t in range(TILES):
        out[t * count] = wells


def send_y(out, lower_edge, upper_edge):
    count, rows, _ = out.shape
    count = count // TILES
    for step, edge in ((1, upper_edge), (-1, lower_edge)):
        first = tile_at(step) * count + 1
        for n in range(edge.shape[0] // rows):
            out[first + n] = edge[n * rows : (n + 1) * rows]


def from_y(spread, blocks):
    count = spread.shape[0] // TILES
    result = []
    for step in (-1, 1):
        first = tile_at(step) * count + 1
        result.append(jnp.concatenate([spread[first + n] for n in range(blocks)], axis=0))
    return result


def live_index(index_ref, count_ref):
    index = pad_lanes(index_ref[...])
    return jnp.where(lane_ids(LZ, 128) < count_ref[0, 0], index, 0.0)


def well_row(owner_ref, well_ref):
    return pad_lanes((owner_ref[...] * 8 + well_ref[...]).astype(F32))


def totals_by_well(column, well_column):
    ids = well_column[:SLOTS].astype(jnp.int32)
    halves = []
    for half in range(2):
        hit = ids == lane_ids(SLOTS, 128) + half * 128
        halves.append(jnp.sum(jnp.where(hit, column[:SLOTS], 0.0), axis=0, keepdims=True))
    return jnp.concatenate(halves, axis=0)


def own_rates(rate_ref):
    tile = own_tile()
    rate = rate_ref[...]
    tiled = jnp.concatenate([rate] * 16, axis=1)
    lanes = lane_ids(1, 128)
    halves = [jnp.where((lanes + half * 128) // 8 == tile, tiled, 0.0) for half in range(2)]
    return jnp.concatenate(halves, axis=0)


def load(copies, sem):
    started = [pltpu.make_async_copy(source, target, sem.at[n]) for n, (source, target) in enumerate(copies)]
    for copy in started:
        copy.start()
    return started


def halves_of(split, span):
    return jnp.concatenate([split[0, span, :], split[1, span, :]], axis=1)


def rows_of(side):
    core = lax.rem(lax.axis_index("layer") + side, 2)
    return pl.ds(pl.multiple_of(core * HALF, HALF), HALF)


def edges_kernel(pressure, perm_x, perm_y, inverse, xlo, xhi, y_edge, fixed, fixed_give, split, kx_lo, kx_hi, ky, sem):
    copies = load(
        [(pressure.at[:, half * 128 : half * 128 + 128], split.at[half]) for half in range(2)]
        + [(perm_x.at[:, 0:8], kx_lo), (perm_x.at[:, CX - 8 : CX], kx_hi), (perm_y, ky)]
        + [
            (inverse.at[i, j, rows_of(side)], target.at[n])
            for n, (i, j) in enumerate(((LZ - 1, 0), (0, LZ - 1), (0, 0)))
            for side, target in ((0, fixed), (1, fixed_give))
        ],
        sem,
    )
    for copy in copies[:5]:
        copy.wait()
    split_x_edges(split, xlo, xhi)
    for l in range(LZ):
        xlo[LZ + l : LZ + l + 1, :] = kx_lo[l, 0:1, :]
        xhi[LZ + l : LZ + l + 1, :] = kx_hi[l, 7:8, :]
    y_edge[...] = y_edges([(split.at[0], 0), (ky, 0), (split.at[1], 127), (ky, CY - 1)])[0:16]
    for copy in copies[5:]:
        copy.wait()


def split_x_edges(split, xlo, xhi):
    for l in range(LZ):
        for half in range(2):
            lanes = slice(half * 128, half * 128 + 128)
            xlo[l : l + 1, lanes] = split[half, l * CX : l * CX + 1, :]
            xhi[l : l + 1, lanes] = split[half, l * CX + CX - 1 : l * CX + CX, :]


def wells_first_kernel(*refs):
    (y_edge, pressure, index, owner, well, rate, column, count, *refs) = refs
    (partials, at_slots, live_out, wells_out, *refs) = refs
    (split, y_edge_v, index_v, owner_v, well_v, rate_v, column_s, count_s, sem) = refs
    copies = load(
        [(pressure.at[:, half * 128 : half * 128 + 128], split.at[half]) for half in range(2)]
        + [
            (y_edge, y_edge_v),
            (column, column_s),
            (count, count_s),
            (index, index_v),
            (owner, owner_v),
            (well, well_v),
            (rate, rate_v),
        ],
        sem,
    )
    for copy in copies:
        copy.wait()
    at = gather_slots(split, column_s)
    at_slots[...] = at
    live = live_index(index_v, count_s)
    live_out[...] = live
    weighted = jnp.sum(live * at, axis=0, keepdims=True)
    total = jnp.sum(live, axis=0, keepdims=True)
    wells = well_row(owner_v, well_v)
    wells_out[...] = wells
    weighted_c, total_c, wells_c = well_columns([weighted, total, wells])
    values = jnp.concatenate(
        [totals_by_well(weighted_c, wells_c) + own_rates(rate_v), totals_by_well(total_c, wells_c)], axis=0
    )
    send_wells(partials, values)
    send_y(partials, y_edge_v[0:8], y_edge_v[8:16])


def wells_next_kernel(split, live, wells, rate, column, partials, at_slots, live_v, wells_v, rate_v, column_s, sem):
    copies = load([(column, column_s), (rate, rate_v), (live, live_v), (wells, wells_v)], sem)
    for copy in copies:
        copy.wait()
    at = gather_slots(split, column_s)
    at_slots[...] = at
    weighted = jnp.sum(live_v[...] * at, axis=0, keepdims=True)
    weighted_c, wells_c = well_columns([weighted, wells_v[...]])
    send_wells(partials, totals_by_well(weighted_c, wells_c) + own_rates(rate_v))
    turned = y_edges([(split.at[0], 0), (split.at[1], 127)])
    send_y(partials, turned[0:4], turned[4:8])


def lateral_kernel(first, field, kx, ky, source, rhs, field_v, kx_v, ky_v, source_v, sem):
    if first:
        wanted = [(field.at[:, half * 128 : half * 128 + 128], field_v.at[half]) for half in range(2)]
    else:
        wanted = [(field.at[half], field_v.at[half]) for half in range(2)]
    for copy in load(wanted + [(kx, kx_v), (ky, ky_v), (source, source_v)], sem):
        copy.wait()
    rows = lax.broadcasted_iota(jnp.int32, (CX, CY), 0)
    lanes = lane_ids(CX, CY)
    for l in range(LZ):
        span = slice(l * CX, (l + 1) * CX)
        f = halves_of(field_v, span)
        k = kx_v[span, :]
        face = k + pltpu.roll(k, CX - 1, 0)
        lateral = face * jnp.where(rows == CX - 1, 0.0, pltpu.roll(f, CX - 1, 0))
        lateral = lateral + jnp.where(rows == 0, 0.0, pltpu.roll(face * f, 1, 0))
        k = ky_v[span, :]
        face = k + pltpu.roll(k, CY - 1, 1)
        lateral = lateral + face * jnp.where(lanes == CY - 1, 0.0, pltpu.roll(f, CY - 1, 1))
        lateral = lateral + jnp.where(lanes == 0, 0.0, pltpu.roll(face * f, 1, 1))
        value = source_v[span, :] + 0.5 * lateral
        rhs[0, span, :] = value[:, :128]
        rhs[1, span, :] = value[:, 128:]


def solve_kernel(first, inputs, *refs):
    away, refs = refs[:inputs], refs[inputs:]
    if first:
        (solved, keep, give, sums_out, kylo_out, kyhi_out, rims, *refs) = refs
    else:
        (solved, keep, give, flow_out, *refs) = refs
    held, (carried, column_s, sem) = refs[:inputs], refs[inputs:]
    (column, partials, live, wells, at_slots, y_own, x_own_lo, x_own_hi, *small, rhs, lower, inverse) = held
    copies = load([(away[0], column_s)] + [(away[n], held[n]) for n in range(1, inputs)], sem)
    for copy in copies[: inputs - 3]:
        copy.wait()
    gx, gy = lax.axis_index("gx"), lax.axis_index("gy")
    block = partials.shape[0] // TILES
    total = partials[0]
    for t in range(1, TILES):
        total = total + partials[block * t]
    from_ylo, from_yhi = from_y(partials, 2)
    if first:
        x_lo, x_hi = small
        kx_lo, kx_hi = x_lo, x_hi
        ky_lo, ky_hi = from_ylo[4:8], from_yhi[4:8]
        kylo_out[...] = from_ylo
        kyhi_out[...] = from_yhi
        numerator, index_sum = total[0:2], total[2:4]
        sums_out[...] = index_sum
    else:
        x_lo, x_hi, kx_lo, kx_hi, ky_lo, ky_hi, sums = small
        ky_lo, ky_hi = ky_lo[4:8], ky_hi[4:8]
        numerator, index_sum = total, sums[...]
    bottom_hole = numerator / (index_sum + 1.0)
    (wells_c,) = well_columns([wells[...]])
    ids = wells_c[:SLOTS].astype(jnp.int32)
    hole = jnp.zeros((SLOTS, 128), F32)
    for half in range(2):
        hit = ids == lane_ids(SLOTS, 128) + half * 128
        hole = hole + jnp.where(hit, bottom_hole[half : half + 1], 0.0)
    hole = jnp.sum(hole, axis=1, keepdims=True)
    hole = jnp.broadcast_to(hole, (SLOTS, 128))
    hole = jnp.concatenate([hole, jnp.zeros((128 - SLOTS, 128), F32)], axis=0).T[0:1]
    flow = live[...] * (hole - at_slots[...])
    if not first:
        flow_out[...] = flow[:, :SLOTS]

    for copy in copies[inputs - 3 : inputs - 2]:
        copy.wait()
    add = jnp.concatenate(
        [
            jnp.where(gy > 0, 0.5 * (y_own[4:8] + ky_lo) * from_ylo[0:4], 0.0),
            jnp.where(gy < 3, 0.5 * (y_own[12:16] + ky_hi) * from_yhi[0:4], 0.0),
        ],
        axis=0,
    ).T
    lanes = lane_ids(CX, 128)
    for l in range(LZ):
        span = slice(l * CX, (l + 1) * CX)
        part = slice((l % 2) * CX, (l % 2) * CX + CX)
        for half, lane in ((0, 0), (1, 127)):
            value = add[part, half * 4 + l // 2 : half * 4 + l // 2 + 1]
            rhs[half, span, :] = rhs[half, span, :] + jnp.where(lanes == lane, value, 0.0)
    sides = (
        (0, jnp.where(gx > 0, 0.5 * (x_own_lo[LZ : 2 * LZ] + kx_lo[LZ : 2 * LZ]) * x_lo[0:LZ], 0.0)),
        (CX - 1, jnp.where(gx < 7, 0.5 * (x_own_hi[LZ : 2 * LZ] + kx_hi[LZ : 2 * LZ]) * x_hi[0:LZ], 0.0)),
    )
    for row, value in sides:
        for half in range(2):
            part = rhs.at[half]
            where = (pl.ds(row, LZ, stride=CX), slice(None))
            part[where] = part[where] + value[:, half * 128 : half * 128 + 128]

    lanes8 = lane_ids(LZ, 128)
    for s in range(SLOTS):
        place = column_s[0, s]
        x = place // CY
        y = place % CY
        half = y // 128
        lane = y % 128
        part = rhs.at[half]
        where = (pl.ds(x, LZ, stride=CX), slice(None))
        part[where] = part[where] + jnp.where(lanes8 == lane, flow[:, s : s + 1], 0.0)

    for copy in copies[inputs - 2 :]:
        copy.wait()

    def solve_block(b, carry):
        at = pl.multiple_of(b * 8, 8)
        right = [halves_of(rhs, pl.ds(j * CX + at, 8)) for j in range(LZ)]
        here = pl.ds(at, 8)
        for i in range(LZ):
            if first:
                rims[0, i, here, :] = inverse[i, 0, here, :]
                rims[1, i, here, :] = inverse[i, LZ - 1, here, :]
            total = inverse[i, 0, here, :] * right[0]
            for j in range(1, LZ):
                total = total + inverse[i, j, here, :] * right[j]
            solved[pl.ds(i * CX + at, 8), :] = total
            if i == 0:
                carried[1, here, :] = total
            if i == LZ - 1:
                low = lower[here, :]
                carried[0, here, :] = total + inverse[i, i, here, :] * low - low
        return carry

    lax.fori_loop(0, CX // 8, solve_block, 0)
    for side, out in ((0, keep), (1, give)):
        out[...] = carried[:, rows_of(side), :]


def by_core(body):
    core = lax.axis_index("layer") % 2
    for own in range(2):
        pl.when(core == own)(functools.partial(body, own))


def pair_fixed_kernel(mine, other, out):
    def body(own):
        top, low = (mine, other) if own == 0 else (other, mine)
        out[0] = low[0] * top[0]
        out[1] = top[1] * low[1]
        out[2] = top[2] + top[1] * (low[2] - 1.0) * top[0]

    by_core(body)


def pair_kernel(mine, other, fixed_mine, fixed_other, out):
    def body(own):
        top, low = (mine, other) if own == 0 else (other, mine)
        fixed_top, fixed_low = (fixed_mine, fixed_other) if own == 0 else (fixed_other, fixed_mine)
        out[0] = fixed_low[0] * top[0] + low[0]
        out[1] = top[1] + fixed_top[1] * (low[1] + fixed_low[2] * top[0] - top[0])

    by_core(body)


def chain_kernel(*refs):
    cds, fixed, refs = refs[:4], refs[4:8], refs[8:]
    cd_mine, cd_other, fixed_mine, fixed_other, mine, give = refs
    me = lax.axis_index("layer")

    def position(own):
        chip, even = own // 2, own % 2 == 0
        cd_top, cd_low = (cd_mine, cd_other) if even else (cd_other, cd_mine)
        fixed_top, fixed_low = (fixed_mine, fixed_other) if even else (fixed_other, fixed_mine)
        out_top, out_low = (mine, give) if even else (give, mine)

        def block(b, carry):
            here = pl.ds(pl.multiple_of(b * 8, 8), 8)
            uppers = [jnp.zeros((8, CY), F32)]
            for c in range(3):
                d = (chip - c) % 4
                uppers.append(fixed[d][0, here, :] * uppers[-1] + cds[d][0, here, :])
            low = jnp.zeros((8, CY), F32)
            for c in range(3, chip, -1):
                d = (chip - c) % 4
                step = cds[d][1, here, :] + fixed[d][2, here, :] * uppers[c] - uppers[c]
                low = fixed[d][1, here, :] * low + step
            upper = uppers[chip]
            below = fixed_top[0, here, :] * upper + cd_top[0, here, :]
            step = cd_low[1, here, :] + fixed_low[2, here, :] * below - below
            out_top[0, here, :] = upper
            out_top[1, here, :] = fixed_low[1, here, :] * low + step
            out_low[0, here, :] = below
            out_low[1, here, :] = low
            return carry

        @pl.when(me == own)
        def _():
            lax.fori_loop(0, HALF // 8, block, 0)

    for own in range(GROUPS):
        position(own)


def sweep_kernel(last, mine, other, solved, rims, *refs):
    if last:
        (field,) = refs
    else:
        split, lower, xlo, xhi = refs

    def body(own):
        for side in range(2):
            ends = mine if side == own else other

            def block(b, carry):
                there = pl.ds(pl.multiple_of(b * 8, 8), 8)
                here = pl.ds(pl.multiple_of(side * HALF + b * 8, 8), 8)
                upper, low = ends[0, there, :], ends[1, there, :]
                for i in range(LZ):
                    span = pl.ds(pl.multiple_of(i * CX + side * HALF + b * 8, 8), 8)
                    value = solved[span, :] + rims[0, i, here, :] * upper + rims[1, i, here, :] * low
                    if last:
                        field[span, :] = value
                    else:
                        split[0, span, :] = value[:, :128]
                        split[1, span, :] = value[:, 128:]
                if not last:
                    lower[here, :] = low
                return carry

            lax.fori_loop(0, HALF // 8, block, 0)

    by_core(body)
    if not last:
        split_x_edges(split, xlo, xhi)


def params(mib=8.0):
    return pltpu.CompilerParams(vmem_limit_bytes=int(mib * 1024) * 1024)


def around(n, step):
    return [(i, (i + step) % n) for i in range(n)]


def from_sides(xlo, xhi):
    return (lax.ppermute(xhi, "gx", around(8, 1)), lax.ppermute(xlo, "gx", around(8, -1)))


def swapped(value):
    return lax.ppermute(value, "layer", [(i, i ^ 1) for i in range(GROUPS)])


def all_chips(value):
    return [value] + [lax.ppermute(value, "layer", around(GROUPS, 2 * d)) for d in range(1, 4)]


def whole(kernel, name, out_shape, *operands):
    return pl.pallas_call(
        kernel,
        out_shape=out_shape,
        in_specs=[VMEM] * len(operands),
        out_specs=jax.tree.map(lambda _: VMEM, out_shape),
        compiler_params=params(),
        name=name,
    )(*operands)


def shards(
    pressure,
    source,
    perm_x,
    perm_y,
    line_inverse,
    robin_below,
    tile_count,
    perf_owner,
    perf_well,
    perf_column,
    perf_index,
    well_rate,
):
    rows = LZ * CX
    pressure = pressure.reshape(rows, CY)
    source = source.reshape(rows, CY)
    inverse = line_inverse[0]
    lower = robin_below[0]
    owner = perf_owner[0].T
    index = perf_index[0].T

    kx = perm_x.reshape(rows, CY)
    ky = perm_y.reshape(rows, CY)
    *edges, y_edge, fixed, fixed_give = pl.pallas_call(
        edges_kernel,
        out_shape=(shape(16, CY), shape(16, CY), shape(16, 128), shape(3, HALF, CY), shape(3, HALF, CY)),
        in_specs=[ANY] * 4,
        out_specs=(VMEM,) * 5,
        scratch_shapes=[
            pltpu.VMEM((2, rows, 128), F32),
            pltpu.VMEM((LZ, 8, CY), F32),
            pltpu.VMEM((LZ, 8, CY), F32),
            pltpu.VMEM((rows, CY), F32),
            pltpu.SemaphoreType.DMA((11,)),
        ],
        compiler_params=params(EDGE_MIB),
        name="first_edges",
    )(pressure, perm_x, ky, inverse)
    sides = from_sides(*edges)
    fixed_other = swapped(fixed_give)
    fixed_pair = whole(pair_fixed_kernel, "pair_fixed", shape(3, HALF, CY), fixed, fixed_other)
    fixed_chips = all_chips(fixed_pair)
    partials, at_slots, live, wells = pl.pallas_call(
        wells_first_kernel,
        out_shape=(shape(3 * TILES, 4, 128), shape(LZ, 128), shape(LZ, 128), shape(1, 128)),
        in_specs=[ANY] * 8,
        out_specs=(VMEM,) * 4,
        scratch_shapes=[
            pltpu.VMEM((2, rows, 128), F32),
            pltpu.VMEM((16, 128), F32),
            pltpu.VMEM((LZ, SLOTS), F32),
            pltpu.VMEM((1, SLOTS), jnp.int32),
            pltpu.VMEM((1, SLOTS), jnp.int32),
            pltpu.VMEM((1, 8), F32),
            pltpu.SMEM((1, SLOTS), jnp.int32),
            pltpu.SMEM((1, 1), jnp.int32),
            pltpu.SemaphoreType.DMA((9,)),
        ],
        compiler_params=params(WELLS_MIB),
        name="first_wells",
    )(y_edge, pressure, index, owner, perf_well, well_rate, perf_column, tile_count)
    field = pressure
    k_sides = sides
    own_edges = (y_edge, *edges)
    ky_sides = sums = None
    for sweep_step in range(ITERS):
        first, last = sweep_step == 0, sweep_step == ITERS - 1
        if first:
            partials, fixed_pair = lax.optimization_barrier((partials, fixed_pair))
        spread = lax.all_to_all(partials, ("gx", "gy"), split_axis=0, concat_axis=0, tiled=True)
        if first:
            spread, *fixed_chips = lax.optimization_barrier((spread, *fixed_chips))
        small = sides if first else (*sides, *k_sides, *ky_sides, sums)
        rhs = pl.pallas_call(
            functools.partial(lateral_kernel, first),
            out_shape=shape(2, rows, 128),
            in_specs=[ANY] * 4,
            out_specs=VMEM,
            scratch_shapes=[pltpu.VMEM((2, rows, 128), F32)]
            + [pltpu.VMEM((rows, CY), F32)] * 3
            + [pltpu.SemaphoreType.DMA((5,))],
            compiler_params=params(LATERAL_MIB),
            cost_estimate=pl.CostEstimate(
                flops=17 * rows * CY, bytes_accessed=5 * 4 * rows * CY, transcendentals=0
            ),
            name="lateral",
        )(field, kx, ky, source)
        operands = (perf_column, spread, live, wells, at_slots, *own_edges, *small, rhs, lower, inverse)
        held = [pltpu.VMEM(value.shape, value.dtype) for value in operands]
        solved, carried, give, *small = pl.pallas_call(
            functools.partial(solve_kernel, first, len(operands)),
            out_shape=(shape(rows, CY), shape(2, HALF, CY), shape(2, HALF, CY))
            + ((shape(2, 128), shape(8, 128), shape(8, 128), shape(2, LZ, CX, CY)) if first else (shape(LZ, SLOTS),)),
            in_specs=[ANY] * len(operands),
            out_specs=(VMEM,) * (7 if first else 4),
            scratch_shapes=held
            + [
                pltpu.VMEM((2, CX, CY), F32),
                pltpu.SMEM((1, SLOTS), jnp.int32),
                pltpu.SemaphoreType.DMA((len(operands),)),
            ],
            compiler_params=params(SOLVE_MIB),
            name="solve_lines",
        )(*operands)
        if first:
            *small, rims = small
        other = swapped(give)
        chips = all_chips(whole(pair_kernel, "pair", shape(2, HALF, CY), carried, other, fixed, fixed_other))
        ends, ends_give = whole(
            chain_kernel,
            "chain",
            (shape(2, HALF, CY),) * 2,
            *(*chips, *fixed_chips, carried, other, fixed, fixed_other),
        )
        planes = (ends, swapped(ends_give), solved, rims)
        if last:
            (field,) = whole(functools.partial(sweep_kernel, True), "sweep_last", (shape(rows, CY),), *planes)
            (flow,) = small
            break
        sums, *ky_sides = small
        field, lower, *edges = whole(
            functools.partial(sweep_kernel, False),
            "sweep_mid",
            (shape(2, rows, 128), shape(CX, CY), shape(8, CY), shape(8, CY)),
            *planes,
        )
        sides = from_sides(*edges)
        partials, at_slots = pl.pallas_call(
            wells_next_kernel,
            out_shape=(shape(3 * TILES, 2, 128), shape(LZ, 128)),
            in_specs=[VMEM] + [ANY] * 4,
            out_specs=(VMEM,) * 2,
            scratch_shapes=[
                pltpu.VMEM((LZ, 128), F32),
                pltpu.VMEM((1, 128), F32),
                pltpu.VMEM((1, 8), F32),
                pltpu.SMEM((1, SLOTS), jnp.int32),
                pltpu.SemaphoreType.DMA((4,)),
            ],
            compiler_params=params(),
            name="next_wells",
        )(field, live, wells, well_rate, perf_column)
    return (field.reshape(LZ, CX, CY), flow.T[None])


def solution(mesh):
    placed = (
        P("layer", "gx", "gy"),
        P("layer", "gx", "gy"),
        P("layer", "gx", "gy"),
        P("layer", "gx", "gy"),
        P("layer", None, None, "gx", "gy"),
        P("layer", "gx", "gy"),
        P("layer", ("gx", "gy")),
        P("layer", ("gx", "gy"), None),
        P("layer", ("gx", "gy")),
        P("layer", ("gx", "gy")),
        P("layer", ("gx", "gy"), None),
        P("layer", ("gx", "gy")),
    )
    return jax.shard_map(
        shards,
        mesh=mesh,
        in_specs=placed,
        out_specs=(P("layer", "gx", "gy"), P("layer", ("gx", "gy"), None)),
        check_vma=False,
    )
```

```python
import functools

import jax
import jax.numpy as jnp
from jax import lax
from jax.experimental import pallas as pl
from jax.experimental.pallas import tpu as pltpu
from jax.sharding import PartitionSpec as P

ITERS = 2
EDGE_MIB = 53.5
WELLS_MIB = 52.0
SOLVE_MIB = 52.0
LATERAL_MIB = 52.0
LZ = 8
CX = 64
CY = 256
HALF = CX // 2
SLOTS = 48
WELLS = 256
TILES = 32
GROUPS = 8
PARTS = 4
F32 = jnp.float32
VMEM = pl.BlockSpec(memory_space=pltpu.VMEM)
SMEM = pl.BlockSpec(memory_space=pltpu.SMEM)
ANY = pl.BlockSpec(memory_space=pltpu.HBM)


def shape(*dims):
    return jax.ShapeDtypeStruct(dims, F32)


def lane_ids(rows, lanes):
    return lax.broadcasted_iota(jnp.int32, (rows, lanes), 1)


def x_edges(ref, row, out, first):
    for l in range(LZ):
        out[first + l : first + l + 1, :] = ref[l * CX + row : l * CX + row + 1, :]


def y_edges(pieces):
    lanes = lane_ids(2 * CX, 128)
    packed = jnp.zeros((2 * CX, 128), F32)
    row = 0
    for ref, column in pieces:
        start = (column // 128) * 128
        for r in range(LZ // 2):
            block = ref[r * 2 * CX : (r + 1) * 2 * CX, start : start + 128]
            value = block[:, column - start : column - start + 1]
            packed = jnp.where(lanes == row, value, packed)
            row += 1
    return packed.T


def gather_slots(split_ref, column_ref):
    lanes = lane_ids(LZ, 128)
    found = jnp.zeros((LZ, 128), F32)
    for s in range(SLOTS):
        column = column_ref[0, s]
        x = column // CY
        y = column % CY
        half = y // 128
        lane = y % 128
        block = split_ref.at[half][pl.ds(x, LZ, stride=CX), :]
        value = jnp.sum(jnp.where(lanes == lane, block, 0.0), axis=1, keepdims=True)
        found = jnp.where(lanes == s, value, found)
    return found


def well_columns(rows):
    block = jnp.concatenate(rows + [jnp.zeros((8 - len(rows), 128), F32)], axis=0)
    turned = block.T
    return [turned[:, i : i + 1] for i in range(len(rows))]


def pad_lanes(value):
    return jnp.concatenate([value, jnp.zeros((value.shape[0], 128 - value.shape[1]), value.dtype)], axis=1)


def own_tile():
    return lax.axis_index("gx") * 4 + lax.axis_index("gy")


def tile_at(step):
    return lax.rem(own_tile() + step + TILES, TILES)


def send_wells(out, wells):
    count = out.shape[0] // TILES
    for t in range(TILES):
        out[t * count] = wells


def send_y(out, lower_edge, upper_edge):
    count, rows, _ = out.shape
    count = count // TILES
    for step, edge in ((1, upper_edge), (-1, lower_edge)):
        first = tile_at(step) * count + 1
        for n in range(edge.shape[0] // rows):
            out[first + n] = edge[n * rows : (n + 1) * rows]


def from_y(spread, blocks):
    count = spread.shape[0] // TILES
    result = []
    for step in (-1, 1):
        first = tile_at(step) * count + 1
        result.append(jnp.concatenate([spread[first + n] for n in range(blocks)], axis=0))
    return result


def live_index(index_ref, count_ref):
    index = pad_lanes(index_ref[...])
    return jnp.where(lane_ids(LZ, 128) < count_ref[0, 0], index, 0.0)


def well_row(owner_ref, well_ref):
    return pad_lanes((owner_ref[...] * 8 + well_ref[...]).astype(F32))


def totals_by_well(column, well_column):
    ids = well_column[:SLOTS].astype(jnp.int32)
    halves = []
    for half in range(2):
        hit = ids == lane_ids(SLOTS, 128) + half * 128
        halves.append(jnp.sum(jnp.where(hit, column[:SLOTS], 0.0), axis=0, keepdims=True))
    return jnp.concatenate(halves, axis=0)


def own_rates(rate_ref):
    tile = own_tile()
    rate = rate_ref[...]
    tiled = jnp.concatenate([rate] * 16, axis=1)
    lanes = lane_ids(1, 128)
    halves = [jnp.where((lanes + half * 128) // 8 == tile, tiled, 0.0) for half in range(2)]
    return jnp.concatenate(halves, axis=0)


def load(copies, sem):
    started = [pltpu.make_async_copy(source, target, sem.at[n]) for n, (source, target) in enumerate(copies)]
    for copy in started:
        copy.start()
    return started


def halves_of(split, span):
    return jnp.concatenate([split[0, span, :], split[1, span, :]], axis=1)


def rows_of(side):
    core = lax.rem(lax.axis_index("layer") + side, 2)
    return pl.ds(pl.multiple_of(core * HALF, HALF), HALF)


def edges_kernel(pressure, perm_x, perm_y, inverse, xlo, xhi, y_edge, fixed, fixed_give, split, kx_lo, kx_hi, ky, sem):
    copies = load(
        [(pressure.at[:, half * 128 : half * 128 + 128], split.at[half]) for half in range(2)]
        + [(perm_x.at[:, 0:8], kx_lo), (perm_x.at[:, CX - 8 : CX], kx_hi), (perm_y, ky)]
        + [
            (inverse.at[i, j, rows_of(side)], target.at[n])
            for n, (i, j) in enumerate(((LZ - 1, 0), (0, LZ - 1), (0, 0)))
            for side, target in ((0, fixed), (1, fixed_give))
        ],
        sem,
    )
    for copy in copies[:5]:
        copy.wait()
    split_x_edges(split, xlo, xhi)
    for l in range(LZ):
        xlo[LZ + l : LZ + l + 1, :] = kx_lo[l, 0:1, :]
        xhi[LZ + l : LZ + l + 1, :] = kx_hi[l, 7:8, :]
    y_edge[...] = y_edges([(split.at[0], 0), (ky, 0), (split.at[1], 127), (ky, CY - 1)])[0:16]
    for copy in copies[5:]:
        copy.wait()


def split_x_edges(split, xlo, xhi):
    for l in range(LZ):
        for half in range(2):
            lanes = slice(half * 128, half * 128 + 128)
            xlo[l : l + 1, lanes] = split[half, l * CX : l * CX + 1, :]
            xhi[l : l + 1, lanes] = split[half, l * CX + CX - 1 : l * CX + CX, :]


def wells_first_kernel(*refs):
    (y_edge, pressure, index, owner, well, rate, column, count, *refs) = refs
    (partials, at_slots, live_out, wells_out, *refs) = refs
    (split, y_edge_v, index_v, owner_v, well_v, rate_v, column_s, count_s, sem) = refs
    copies = load(
        [(pressure.at[:, half * 128 : half * 128 + 128], split.at[half]) for half in range(2)]
        + [
            (y_edge, y_edge_v),
            (column, column_s),
            (count, count_s),
            (index, index_v),
            (owner, owner_v),
            (well, well_v),
            (rate, rate_v),
        ],
        sem,
    )
    for copy in copies:
        copy.wait()
    at = gather_slots(split, column_s)
    at_slots[...] = at
    live = live_index(index_v, count_s)
    live_out[...] = live
    weighted = jnp.sum(live * at, axis=0, keepdims=True)
    total = jnp.sum(live, axis=0, keepdims=True)
    wells = well_row(owner_v, well_v)
    wells_out[...] = wells
    weighted_c, total_c, wells_c = well_columns([weighted, total, wells])
    values = jnp.concatenate(
        [totals_by_well(weighted_c, wells_c) + own_rates(rate_v), totals_by_well(total_c, wells_c)], axis=0
    )
    send_wells(partials, values)
    send_y(partials, y_edge_v[0:8], y_edge_v[8:16])


def wells_next_kernel(split, live, wells, rate, column, partials, at_slots, live_v, wells_v, rate_v, column_s, sem):
    copies = load([(column, column_s), (rate, rate_v), (live, live_v), (wells, wells_v)], sem)
    turned = y_edges([(split.at[0], 0), (split.at[1], 127)])
    send_y(partials, turned[0:4], turned[4:8])
    for copy in copies:
        copy.wait()
    at = gather_slots(split, column_s)
    at_slots[...] = at
    weighted = jnp.sum(live_v[...] * at, axis=0, keepdims=True)
    weighted_c, wells_c = well_columns([weighted, wells_v[...]])
    send_wells(partials, totals_by_well(weighted_c, wells_c) + own_rates(rate_v))


def lateral_kernel(first, field, kx, ky, source, rhs, field_v, kx_v, ky_v, source_v, sem):
    if first:
        wanted = [(field.at[:, half * 128 : half * 128 + 128], field_v.at[half]) for half in range(2)]
    else:
        wanted = [(field.at[half], field_v.at[half]) for half in range(2)]
    for copy in load(wanted + [(kx, kx_v), (ky, ky_v), (source, source_v)], sem):
        copy.wait()
    rows = lax.broadcasted_iota(jnp.int32, (CX, CY), 0)
    lanes = lane_ids(CX, CY)
    for l in range(LZ):
        span = slice(l * CX, (l + 1) * CX)
        f = halves_of(field_v, span)
        k = kx_v[span, :]
        face = k + pltpu.roll(k, CX - 1, 0)
        lateral = face * jnp.where(rows == CX - 1, 0.0, pltpu.roll(f, CX - 1, 0))
        lateral = lateral + jnp.where(rows == 0, 0.0, pltpu.roll(face * f, 1, 0))
        k = ky_v[span, :]
        face = k + pltpu.roll(k, CY - 1, 1)
        lateral = lateral + face * jnp.where(lanes == CY - 1, 0.0, pltpu.roll(f, CY - 1, 1))
        lateral = lateral + jnp.where(lanes == 0, 0.0, pltpu.roll(face * f, 1, 1))
        value = source_v[span, :] + 0.5 * lateral
        rhs[0, span, :] = value[:, :128]
        rhs[1, span, :] = value[:, 128:]


def solve_kernel(first, inputs, *refs):
    away, refs = refs[:inputs], refs[inputs:]
    if first:
        (solved, keep, give, sums_out, kylo_out, kyhi_out, rims, *refs) = refs
    else:
        (solved, keep, give, flow_out, *refs) = refs
    held, (carried, column_s, sem) = refs[:inputs], refs[inputs:]
    (column, partials, live, wells, at_slots, y_own, x_own_lo, x_own_hi, *small, rhs, lower, inverse) = held
    parts = [slice(n * CX // PARTS, (n + 1) * CX // PARTS) for n in range(PARTS)]
    copies = load(
        [(away[0], column_s)]
        + [(away[n], held[n]) for n in range(1, inputs - 1)]
        + [(away[inputs - 1].at[:, :, part], inverse.at[:, :, part]) for part in parts],
        sem,
    )
    for copy in copies[: inputs - 3]:
        copy.wait()
    gx, gy = lax.axis_index("gx"), lax.axis_index("gy")
    block = partials.shape[0] // TILES
    total = partials[0]
    for t in range(1, TILES):
        total = total + partials[block * t]
    from_ylo, from_yhi = from_y(partials, 2)
    if first:
        x_lo, x_hi = small
        kx_lo, kx_hi = x_lo, x_hi
        ky_lo, ky_hi = from_ylo[4:8], from_yhi[4:8]
        kylo_out[...] = from_ylo
        kyhi_out[...] = from_yhi
        numerator, index_sum = total[0:2], total[2:4]
        sums_out[...] = index_sum
    else:
        x_lo, x_hi, kx_lo, kx_hi, ky_lo, ky_hi, sums = small
        ky_lo, ky_hi = ky_lo[4:8], ky_hi[4:8]
        numerator, index_sum = total, sums[...]
    bottom_hole = numerator / (index_sum + 1.0)
    (wells_c,) = well_columns([wells[...]])
    ids = wells_c[:SLOTS].astype(jnp.int32)
    hole = jnp.zeros((SLOTS, 128), F32)
    for half in range(2):
        hit = ids == lane_ids(SLOTS, 128) + half * 128
        hole = hole + jnp.where(hit, bottom_hole[half : half + 1], 0.0)
    hole = jnp.sum(hole, axis=1, keepdims=True)
    hole = jnp.broadcast_to(hole, (SLOTS, 128))
    hole = jnp.concatenate([hole, jnp.zeros((128 - SLOTS, 128), F32)], axis=0).T[0:1]
    flow = live[...] * (hole - at_slots[...])
    if not first:
        flow_out[...] = flow[:, :SLOTS]

    for copy in copies[inputs - 3 : inputs - 2]:
        copy.wait()
    add = jnp.concatenate(
        [
            jnp.where(gy > 0, 0.5 * (y_own[4:8] + ky_lo) * from_ylo[0:4], 0.0),
            jnp.where(gy < 3, 0.5 * (y_own[12:16] + ky_hi) * from_yhi[0:4], 0.0),
        ],
        axis=0,
    ).T
    lanes = lane_ids(CX, 128)
    for l in range(LZ):
        span = slice(l * CX, (l + 1) * CX)
        part = slice((l % 2) * CX, (l % 2) * CX + CX)
        for half, lane in ((0, 0), (1, 127)):
            value = add[part, half * 4 + l // 2 : half * 4 + l // 2 + 1]
            rhs[half, span, :] = rhs[half, span, :] + jnp.where(lanes == lane, value, 0.0)
    sides = (
        (0, jnp.where(gx > 0, 0.5 * (x_own_lo[LZ : 2 * LZ] + kx_lo[LZ : 2 * LZ]) * x_lo[0:LZ], 0.0)),
        (CX - 1, jnp.where(gx < 7, 0.5 * (x_own_hi[LZ : 2 * LZ] + kx_hi[LZ : 2 * LZ]) * x_hi[0:LZ], 0.0)),
    )
    for row, value in sides:
        for half in range(2):
            part = rhs.at[half]
            where = (pl.ds(row, LZ, stride=CX), slice(None))
            part[where] = part[where] + value[:, half * 128 : half * 128 + 128]

    lanes8 = lane_ids(LZ, 128)
    for s in range(SLOTS):
        place = column_s[0, s]
        x = place // CY
        y = place % CY
        half = y // 128
        lane = y % 128
        part = rhs.at[half]
        where = (pl.ds(x, LZ, stride=CX), slice(None))
        part[where] = part[where] + jnp.where(lanes8 == lane, flow[:, s : s + 1], 0.0)

    copies[inputs - 2].wait()

    def solve_block(b, carry):
        at = pl.multiple_of(b * 8, 8)
        right = [halves_of(rhs, pl.ds(j * CX + at, 8)) for j in range(LZ)]
        here = pl.ds(at, 8)
        for i in range(LZ):
            if first:
                rims[0, i, here, :] = inverse[i, 0, here, :]
                rims[1, i, here, :] = inverse[i, LZ - 1, here, :]
            total = inverse[i, 0, here, :] * right[0]
            for j in range(1, LZ):
                total = total + inverse[i, j, here, :] * right[j]
            solved[pl.ds(i * CX + at, 8), :] = total
            if i == 0:
                carried[1, here, :] = total
            if i == LZ - 1:
                low = lower[here, :]
                carried[0, here, :] = total + inverse[i, i, here, :] * low - low
        return carry

    for n in range(PARTS):
        copies[inputs - 1 + n].wait()
        lax.fori_loop(n * (CX // 8) // PARTS, (n + 1) * (CX // 8) // PARTS, solve_block, 0)
    for side, out in ((0, keep), (1, give)):
        out[...] = carried[:, rows_of(side), :]


def by_core(body):
    core = lax.axis_index("layer") % 2
    for own in range(2):
        pl.when(core == own)(functools.partial(body, own))


def pair_fixed_kernel(mine, other, out):
    def body(own):
        top, low = (mine, other) if own == 0 else (other, mine)
        out[0] = low[0] * top[0]
        out[1] = top[1] * low[1]
        out[2] = top[2] + top[1] * (low[2] - 1.0) * top[0]

    by_core(body)


def pair_kernel(mine, other, fixed_mine, fixed_other, out):
    def body(own):
        top, low = (mine, other) if own == 0 else (other, mine)
        fixed_top, fixed_low = (fixed_mine, fixed_other) if own == 0 else (fixed_other, fixed_mine)
        out[0] = fixed_low[0] * top[0] + low[0]
        out[1] = top[1] + fixed_top[1] * (low[1] + fixed_low[2] * top[0] - top[0])

    by_core(body)


def chain_kernel(*refs):
    cds, fixed, refs = refs[:4], refs[4:8], refs[8:]
    cd_mine, cd_other, fixed_mine, fixed_other, mine, give = refs
    me = lax.axis_index("layer")

    def position(own):
        chip, even = own // 2, own % 2 == 0
        cd_top, cd_low = (cd_mine, cd_other) if even else (cd_other, cd_mine)
        fixed_top, fixed_low = (fixed_mine, fixed_other) if even else (fixed_other, fixed_mine)
        out_top, out_low = (mine, give) if even else (give, mine)

        def block(b, carry):
            here = pl.ds(pl.multiple_of(b * 8, 8), 8)
            uppers = [jnp.zeros((8, CY), F32)]
            for c in range(3):
                d = (chip - c) % 4
                uppers.append(fixed[d][0, here, :] * uppers[-1] + cds[d][0, here, :])
            low = jnp.zeros((8, CY), F32)
            for c in range(3, chip, -1):
                d = (chip - c) % 4
                step = cds[d][1, here, :] + fixed[d][2, here, :] * uppers[c] - uppers[c]
                low = fixed[d][1, here, :] * low + step
            upper = uppers[chip]
            below = fixed_top[0, here, :] * upper + cd_top[0, here, :]
            step = cd_low[1, here, :] + fixed_low[2, here, :] * below - below
            out_top[0, here, :] = upper
            out_top[1, here, :] = fixed_low[1, here, :] * low + step
            out_low[0, here, :] = below
            out_low[1, here, :] = low
            return carry

        @pl.when(me == own)
        def _():
            lax.fori_loop(0, HALF // 8, block, 0)

    for own in range(GROUPS):
        position(own)


def sweep_kernel(last, mine, other, solved, rims, *refs):
    if last:
        (field,) = refs
    else:
        split, lower, xlo, xhi = refs

    def body(own):
        for side in range(2):
            ends = mine if side == own else other

            def block(b, carry):
                there = pl.ds(pl.multiple_of(b * 8, 8), 8)
                here = pl.ds(pl.multiple_of(side * HALF + b * 8, 8), 8)
                upper, low = ends[0, there, :], ends[1, there, :]
                for i in range(LZ):
                    span = pl.ds(pl.multiple_of(i * CX + side * HALF + b * 8, 8), 8)
                    value = solved[span, :] + rims[0, i, here, :] * upper + rims[1, i, here, :] * low
                    if last:
                        field[span, :] = value
                    else:
                        split[0, span, :] = value[:, :128]
                        split[1, span, :] = value[:, 128:]
                if not last:
                    lower[here, :] = low
                return carry

            lax.fori_loop(0, HALF // 8, block, 0)

    by_core(body)
    if not last:
        split_x_edges(split, xlo, xhi)


def params(mib=8.0):
    return pltpu.CompilerParams(vmem_limit_bytes=int(mib * 1024) * 1024)


def around(n, step):
    return [(i, (i + step) % n) for i in range(n)]


def from_sides(xlo, xhi):
    return (lax.ppermute(xhi, "gx", around(8, 1)), lax.ppermute(xlo, "gx", around(8, -1)))


def swapped(value):
    return lax.ppermute(value, "layer", [(i, i ^ 1) for i in range(GROUPS)])


def all_chips(value):
    return [value] + [lax.ppermute(value, "layer", around(GROUPS, 2 * d)) for d in range(1, 4)]


def whole(kernel, name, out_shape, *operands):
    return pl.pallas_call(
        kernel,
        out_shape=out_shape,
        in_specs=[VMEM] * len(operands),
        out_specs=jax.tree.map(lambda _: VMEM, out_shape),
        compiler_params=params(),
        name=name,
    )(*operands)


def shards(
    pressure,
    source,
    perm_x,
    perm_y,
    line_inverse,
    robin_below,
    tile_count,
    perf_owner,
    perf_well,
    perf_column,
    perf_index,
    well_rate,
):
    rows = LZ * CX
    pressure = pressure.reshape(rows, CY)
    source = source.reshape(rows, CY)
    inverse = line_inverse[0]
    lower = robin_below[0]
    owner = perf_owner[0].T
    index = perf_index[0].T

    kx = perm_x.reshape(rows, CY)
    ky = perm_y.reshape(rows, CY)
    *edges, y_edge, fixed, fixed_give = pl.pallas_call(
        edges_kernel,
        out_shape=(shape(16, CY), shape(16, CY), shape(16, 128), shape(3, HALF, CY), shape(3, HALF, CY)),
        in_specs=[ANY] * 4,
        out_specs=(VMEM,) * 5,
        scratch_shapes=[
            pltpu.VMEM((2, rows, 128), F32),
            pltpu.VMEM((LZ, 8, CY), F32),
            pltpu.VMEM((LZ, 8, CY), F32),
            pltpu.VMEM((rows, CY), F32),
            pltpu.SemaphoreType.DMA((11,)),
        ],
        compiler_params=params(EDGE_MIB),
        name="first_edges",
    )(pressure, perm_x, ky, inverse)
    sides = from_sides(*edges)
    fixed_other = swapped(fixed_give)
    fixed_pair = whole(pair_fixed_kernel, "pair_fixed", shape(3, HALF, CY), fixed, fixed_other)
    fixed_chips = all_chips(fixed_pair)
    partials, at_slots, live, wells = pl.pallas_call(
        wells_first_kernel,
        out_shape=(shape(3 * TILES, 4, 128), shape(LZ, 128), shape(LZ, 128), shape(1, 128)),
        in_specs=[ANY] * 8,
        out_specs=(VMEM,) * 4,
        scratch_shapes=[
            pltpu.VMEM((2, rows, 128), F32),
            pltpu.VMEM((16, 128), F32),
            pltpu.VMEM((LZ, SLOTS), F32),
            pltpu.VMEM((1, SLOTS), jnp.int32),
            pltpu.VMEM((1, SLOTS), jnp.int32),
            pltpu.VMEM((1, 8), F32),
            pltpu.SMEM((1, SLOTS), jnp.int32),
            pltpu.SMEM((1, 1), jnp.int32),
            pltpu.SemaphoreType.DMA((9,)),
        ],
        compiler_params=params(WELLS_MIB),
        name="first_wells",
    )(y_edge, pressure, index, owner, perf_well, well_rate, perf_column, tile_count)
    field = pressure
    k_sides = sides
    own_edges = (y_edge, *edges)
    ky_sides = sums = None
    for sweep_step in range(ITERS):
        first, last = sweep_step == 0, sweep_step == ITERS - 1
        if first:
            partials, fixed_pair = lax.optimization_barrier((partials, fixed_pair))
        spread = lax.all_to_all(partials, ("gx", "gy"), split_axis=0, concat_axis=0, tiled=True)
        if first:
            spread, *fixed_chips = lax.optimization_barrier((spread, *fixed_chips))
        small = sides if first else (*sides, *k_sides, *ky_sides, sums)
        rhs = pl.pallas_call(
            functools.partial(lateral_kernel, first),
            out_shape=shape(2, rows, 128),
            in_specs=[ANY] * 4,
            out_specs=VMEM,
            scratch_shapes=[pltpu.VMEM((2, rows, 128), F32)]
            + [pltpu.VMEM((rows, CY), F32)] * 3
            + [pltpu.SemaphoreType.DMA((5,))],
            compiler_params=params(LATERAL_MIB),
            cost_estimate=pl.CostEstimate(
                flops=17 * rows * CY, bytes_accessed=5 * 4 * rows * CY, transcendentals=0
            ),
            name="lateral",
        )(field, kx, ky, source)
        operands = (perf_column, spread, live, wells, at_slots, *own_edges, *small, rhs, lower, inverse)
        held = [pltpu.VMEM(value.shape, value.dtype) for value in operands]
        solved, carried, give, *small = pl.pallas_call(
            functools.partial(solve_kernel, first, len(operands)),
            out_shape=(shape(rows, CY), shape(2, HALF, CY), shape(2, HALF, CY))
            + ((shape(2, 128), shape(8, 128), shape(8, 128), shape(2, LZ, CX, CY)) if first else (shape(LZ, SLOTS),)),
            in_specs=[ANY] * len(operands),
            out_specs=(VMEM,) * (7 if first else 4),
            scratch_shapes=held
            + [
                pltpu.VMEM((2, CX, CY), F32),
                pltpu.SMEM((1, SLOTS), jnp.int32),
                pltpu.SemaphoreType.DMA((len(operands) + PARTS - 1,)),
            ],
            compiler_params=params(SOLVE_MIB),
            name="solve_lines",
        )(*operands)
        if first:
            *small, rims = small
        other = swapped(give)
        chips = all_chips(whole(pair_kernel, "pair", shape(2, HALF, CY), carried, other, fixed, fixed_other))
        ends, ends_give = whole(
            chain_kernel,
            "chain",
            (shape(2, HALF, CY),) * 2,
            *(*chips, *fixed_chips, carried, other, fixed, fixed_other),
        )
        planes = (ends, swapped(ends_give), solved, rims)
        if last:
            (field,) = whole(functools.partial(sweep_kernel, True), "sweep_last", (shape(rows, CY),), *planes)
            (flow,) = small
            break
        sums, *ky_sides = small
        field, lower, *edges = whole(
            functools.partial(sweep_kernel, False),
            "sweep_mid",
            (shape(2, rows, 128), shape(CX, CY), shape(8, CY), shape(8, CY)),
            *planes,
        )
        sides = from_sides(*edges)
        partials, at_slots = pl.pallas_call(
            wells_next_kernel,
            out_shape=(shape(3 * TILES, 2, 128), shape(LZ, 128)),
            in_specs=[VMEM] + [ANY] * 4,
            out_specs=(VMEM,) * 2,
            scratch_shapes=[
                pltpu.VMEM((LZ, 128), F32),
                pltpu.VMEM((1, 128), F32),
                pltpu.VMEM((1, 8), F32),
                pltpu.SMEM((1, SLOTS), jnp.int32),
                pltpu.SemaphoreType.DMA((4,)),
            ],
            compiler_params=params(),
            name="next_wells",
        )(field, live, wells, well_rate, perf_column)
    return (field.reshape(LZ, CX, CY), flow.T[None])


def solution(mesh):
    placed = (
        P("layer", "gx", "gy"),
        P("layer", "gx", "gy"),
        P("layer", "gx", "gy"),
        P("layer", "gx", "gy"),
        P("layer", None, None, "gx", "gy"),
        P("layer", "gx", "gy"),
        P("layer", ("gx", "gy")),
        P("layer", ("gx", "gy"), None),
        P("layer", ("gx", "gy")),
        P("layer", ("gx", "gy")),
        P("layer", ("gx", "gy"), None),
        P("layer", ("gx", "gy")),
    )
    return jax.shard_map(
        shards,
        mesh=mesh,
        in_specs=placed,
        out_specs=(P("layer", "gx", "gy"), P("layer", ("gx", "gy"), None)),
        check_vma=False,
    )
```

```python
import functools

import jax
import jax.numpy as jnp
from jax import lax
from jax.experimental import pallas as pl
from jax.experimental.pallas import tpu as pltpu
from jax.sharding import PartitionSpec as P

ITERS = 2
EDGE_MIB = 53.5
WELLS_MIB = 52.0
SOLVE_MIB = 52.0
LATERAL_MIB = 52.0
LZ = 8
CX = 64
CY = 256
HALF = CX // 2
SLOTS = 48
WELLS = 256
TILES = 32
GROUPS = 8
PARTS = 8
F32 = jnp.float32
VMEM = pl.BlockSpec(memory_space=pltpu.VMEM)
SMEM = pl.BlockSpec(memory_space=pltpu.SMEM)
ANY = pl.BlockSpec(memory_space=pltpu.HBM)


def shape(*dims):
    return jax.ShapeDtypeStruct(dims, F32)


def lane_ids(rows, lanes):
    return lax.broadcasted_iota(jnp.int32, (rows, lanes), 1)


def x_edges(ref, row, out, first):
    for l in range(LZ):
        out[first + l : first + l + 1, :] = ref[l * CX + row : l * CX + row + 1, :]


def y_edges(pieces):
    lanes = lane_ids(2 * CX, 128)
    packed = jnp.zeros((2 * CX, 128), F32)
    row = 0
    for ref, column in pieces:
        start = (column // 128) * 128
        for r in range(LZ // 2):
            block = ref[r * 2 * CX : (r + 1) * 2 * CX, start : start + 128]
            value = block[:, column - start : column - start + 1]
            packed = jnp.where(lanes == row, value, packed)
            row += 1
    return packed.T


def gather_slots(split_ref, column_ref):
    lanes = lane_ids(LZ, 128)
    found = jnp.zeros((LZ, 128), F32)
    for s in range(SLOTS):
        column = column_ref[0, s]
        x = column // CY
        y = column % CY
        half = y // 128
        lane = y % 128
        block = split_ref.at[half][pl.ds(x, LZ, stride=CX), :]
        value = jnp.sum(jnp.where(lanes == lane, block, 0.0), axis=1, keepdims=True)
        found = jnp.where(lanes == s, value, found)
    return found


def well_columns(rows):
    block = jnp.concatenate(rows + [jnp.zeros((8 - len(rows), 128), F32)], axis=0)
    turned = block.T
    return [turned[:, i : i + 1] for i in range(len(rows))]


def pad_lanes(value):
    return jnp.concatenate([value, jnp.zeros((value.shape[0], 128 - value.shape[1]), value.dtype)], axis=1)


def own_tile():
    return lax.axis_index("gx") * 4 + lax.axis_index("gy")


def tile_at(step):
    return lax.rem(own_tile() + step + TILES, TILES)


def send_wells(out, wells):
    count = out.shape[0] // TILES
    for t in range(TILES):
        out[t * count] = wells


def send_y(out, lower_edge, upper_edge):
    count, rows, _ = out.shape
    count = count // TILES
    for step, edge in ((1, upper_edge), (-1, lower_edge)):
        first = tile_at(step) * count + 1
        for n in range(edge.shape[0] // rows):
            out[first + n] = edge[n * rows : (n + 1) * rows]


def from_y(spread, blocks):
    count = spread.shape[0] // TILES
    result = []
    for step in (-1, 1):
        first = tile_at(step) * count + 1
        result.append(jnp.concatenate([spread[first + n] for n in range(blocks)], axis=0))
    return result


def live_index(index_ref, count_ref):
    index = pad_lanes(index_ref[...])
    return jnp.where(lane_ids(LZ, 128) < count_ref[0, 0], index, 0.0)


def well_row(owner_ref, well_ref):
    return pad_lanes((owner_ref[...] * 8 + well_ref[...]).astype(F32))


def totals_by_well(column, well_column):
    ids = well_column[:SLOTS].astype(jnp.int32)
    halves = []
    for half in range(2):
        hit = ids == lane_ids(SLOTS, 128) + half * 128
        halves.append(jnp.sum(jnp.where(hit, column[:SLOTS], 0.0), axis=0, keepdims=True))
    return jnp.concatenate(halves, axis=0)


def own_rates(rate_ref):
    tile = own_tile()
    rate = rate_ref[...]
    tiled = jnp.concatenate([rate] * 16, axis=1)
    lanes = lane_ids(1, 128)
    halves = [jnp.where((lanes + half * 128) // 8 == tile, tiled, 0.0) for half in range(2)]
    return jnp.concatenate(halves, axis=0)


def load(copies, sem):
    started = [pltpu.make_async_copy(source, target, sem.at[n]) for n, (source, target) in enumerate(copies)]
    for copy in started:
        copy.start()
    return started


def halves_of(split, span):
    return jnp.concatenate([split[0, span, :], split[1, span, :]], axis=1)


def rows_of(side):
    core = lax.rem(lax.axis_index("layer") + side, 2)
    return pl.ds(pl.multiple_of(core * HALF, HALF), HALF)


def edges_kernel(pressure, perm_x, perm_y, inverse, xlo, xhi, y_edge, fixed, fixed_give, split, kx_lo, kx_hi, ky, sem):
    copies = load(
        [(pressure.at[:, half * 128 : half * 128 + 128], split.at[half]) for half in range(2)]
        + [(perm_x.at[:, 0:8], kx_lo), (perm_x.at[:, CX - 8 : CX], kx_hi), (perm_y, ky)]
        + [
            (inverse.at[i, j, rows_of(side)], target.at[n])
            for n, (i, j) in enumerate(((LZ - 1, 0), (0, LZ - 1), (0, 0)))
            for side, target in ((0, fixed), (1, fixed_give))
        ],
        sem,
    )
    for copy in copies[:5]:
        copy.wait()
    split_x_edges(split, xlo, xhi)
    for l in range(LZ):
        xlo[LZ + l : LZ + l + 1, :] = kx_lo[l, 0:1, :]
        xhi[LZ + l : LZ + l + 1, :] = kx_hi[l, 7:8, :]
    y_edge[...] = y_edges([(split.at[0], 0), (ky, 0), (split.at[1], 127), (ky, CY - 1)])[0:16]
    for copy in copies[5:]:
        copy.wait()


def split_x_edges(split, xlo, xhi):
    for l in range(LZ):
        for half in range(2):
            lanes = slice(half * 128, half * 128 + 128)
            xlo[l : l + 1, lanes] = split[half, l * CX : l * CX + 1, :]
            xhi[l : l + 1, lanes] = split[half, l * CX + CX - 1 : l * CX + CX, :]


def wells_first_kernel(*refs):
    (y_edge, pressure, index, owner, well, rate, column, count, *refs) = refs
    (partials, at_slots, live_out, wells_out, *refs) = refs
    (split, y_edge_v, index_v, owner_v, well_v, rate_v, column_s, count_s, sem) = refs
    copies = load(
        [(pressure.at[:, half * 128 : half * 128 + 128], split.at[half]) for half in range(2)]
        + [
            (y_edge, y_edge_v),
            (column, column_s),
            (count, count_s),
            (index, index_v),
            (owner, owner_v),
            (well, well_v),
            (rate, rate_v),
        ],
        sem,
    )
    copies[2].wait()
    send_y(partials, y_edge_v[0:8], y_edge_v[8:16])
    for copy in copies[:2] + copies[3:]:
        copy.wait()
    at = gather_slots(split, column_s)
    at_slots[...] = at
    live = live_index(index_v, count_s)
    live_out[...] = live
    weighted = jnp.sum(live * at, axis=0, keepdims=True)
    total = jnp.sum(live, axis=0, keepdims=True)
    wells = well_row(owner_v, well_v)
    wells_out[...] = wells
    weighted_c, total_c, wells_c = well_columns([weighted, total, wells])
    values = jnp.concatenate(
        [totals_by_well(weighted_c, wells_c) + own_rates(rate_v), totals_by_well(total_c, wells_c)], axis=0
    )
    send_wells(partials, values)


def wells_next_kernel(split, live, wells, rate, column, partials, at_slots, live_v, wells_v, rate_v, column_s, sem):
    copies = load([(column, column_s), (rate, rate_v), (live, live_v), (wells, wells_v)], sem)
    turned = y_edges([(split.at[0], 0), (split.at[1], 127)])
    send_y(partials, turned[0:4], turned[4:8])
    for copy in copies:
        copy.wait()
    at = gather_slots(split, column_s)
    at_slots[...] = at
    weighted = jnp.sum(live_v[...] * at, axis=0, keepdims=True)
    weighted_c, wells_c = well_columns([weighted, wells_v[...]])
    send_wells(partials, totals_by_well(weighted_c, wells_c) + own_rates(rate_v))


def lateral_kernel(first, field, kx, ky, source, rhs, field_v, kx_v, ky_v, source_v, sem):
    if first:
        wanted = [(field.at[:, half * 128 : half * 128 + 128], field_v.at[half]) for half in range(2)]
    else:
        wanted = [(field.at[half], field_v.at[half]) for half in range(2)]
    for copy in load(wanted + [(kx, kx_v), (ky, ky_v), (source, source_v)], sem):
        copy.wait()
    rows = lax.broadcasted_iota(jnp.int32, (CX, CY), 0)
    lanes = lane_ids(CX, CY)
    for l in range(LZ):
        span = slice(l * CX, (l + 1) * CX)
        f = halves_of(field_v, span)
        k = kx_v[span, :]
        face = k + pltpu.roll(k, CX - 1, 0)
        lateral = face * jnp.where(rows == CX - 1, 0.0, pltpu.roll(f, CX - 1, 0))
        lateral = lateral + jnp.where(rows == 0, 0.0, pltpu.roll(face * f, 1, 0))
        k = ky_v[span, :]
        face = k + pltpu.roll(k, CY - 1, 1)
        lateral = lateral + face * jnp.where(lanes == CY - 1, 0.0, pltpu.roll(f, CY - 1, 1))
        lateral = lateral + jnp.where(lanes == 0, 0.0, pltpu.roll(face * f, 1, 1))
        value = source_v[span, :] + 0.5 * lateral
        rhs[0, span, :] = value[:, :128]
        rhs[1, span, :] = value[:, 128:]


def solve_kernel(first, inputs, *refs):
    away, refs = refs[:inputs], refs[inputs:]
    if first:
        (solved, keep, give, sums_out, kylo_out, kyhi_out, rims, *refs) = refs
    else:
        (solved, keep, give, flow_out, *refs) = refs
    held, (carried, column_s, sem) = refs[:inputs], refs[inputs:]
    (column, partials, live, wells, at_slots, y_own, x_own_lo, x_own_hi, *small, rhs, lower, inverse) = held
    parts = [slice(n * CX // PARTS, (n + 1) * CX // PARTS) for n in range(PARTS)]
    copies = load(
        [(away[0], column_s)]
        + [(away[n], held[n]) for n in range(1, inputs - 1)]
        + [(away[inputs - 1].at[:, :, part], inverse.at[:, :, part]) for part in parts],
        sem,
    )
    for copy in copies[: inputs - 3]:
        copy.wait()
    gx, gy = lax.axis_index("gx"), lax.axis_index("gy")
    block = partials.shape[0] // TILES
    total = partials[0]
    for t in range(1, TILES):
        total = total + partials[block * t]
    from_ylo, from_yhi = from_y(partials, 2)
    if first:
        x_lo, x_hi = small
        kx_lo, kx_hi = x_lo, x_hi
        ky_lo, ky_hi = from_ylo[4:8], from_yhi[4:8]
        kylo_out[...] = from_ylo
        kyhi_out[...] = from_yhi
        numerator, index_sum = total[0:2], total[2:4]
        sums_out[...] = index_sum
    else:
        x_lo, x_hi, kx_lo, kx_hi, ky_lo, ky_hi, sums = small
        ky_lo, ky_hi = ky_lo[4:8], ky_hi[4:8]
        numerator, index_sum = total, sums[...]
    bottom_hole = numerator / (index_sum + 1.0)
    (wells_c,) = well_columns([wells[...]])
    ids = wells_c[:SLOTS].astype(jnp.int32)
    hole = jnp.zeros((SLOTS, 128), F32)
    for half in range(2):
        hit = ids == lane_ids(SLOTS, 128) + half * 128
        hole = hole + jnp.where(hit, bottom_hole[half : half + 1], 0.0)
    hole = jnp.sum(hole, axis=1, keepdims=True)
    hole = jnp.broadcast_to(hole, (SLOTS, 128))
    hole = jnp.concatenate([hole, jnp.zeros((128 - SLOTS, 128), F32)], axis=0).T[0:1]
    flow = live[...] * (hole - at_slots[...])
    if not first:
        flow_out[...] = flow[:, :SLOTS]

    for copy in copies[inputs - 3 : inputs - 2]:
        copy.wait()
    add = jnp.concatenate(
        [
            jnp.where(gy > 0, 0.5 * (y_own[4:8] + ky_lo) * from_ylo[0:4], 0.0),
            jnp.where(gy < 3, 0.5 * (y_own[12:16] + ky_hi) * from_yhi[0:4], 0.0),
        ],
        axis=0,
    ).T
    lanes = lane_ids(CX, 128)
    for l in range(LZ):
        span = slice(l * CX, (l + 1) * CX)
        part = slice((l % 2) * CX, (l % 2) * CX + CX)
        for half, lane in ((0, 0), (1, 127)):
            value = add[part, half * 4 + l // 2 : half * 4 + l // 2 + 1]
            rhs[half, span, :] = rhs[half, span, :] + jnp.where(lanes == lane, value, 0.0)
    sides = (
        (0, jnp.where(gx > 0, 0.5 * (x_own_lo[LZ : 2 * LZ] + kx_lo[LZ : 2 * LZ]) * x_lo[0:LZ], 0.0)),
        (CX - 1, jnp.where(gx < 7, 0.5 * (x_own_hi[LZ : 2 * LZ] + kx_hi[LZ : 2 * LZ]) * x_hi[0:LZ], 0.0)),
    )
    for row, value in sides:
        for half in range(2):
            part = rhs.at[half]
            where = (pl.ds(row, LZ, stride=CX), slice(None))
            part[where] = part[where] + value[:, half * 128 : half * 128 + 128]

    lanes8 = lane_ids(LZ, 128)
    for s in range(SLOTS):
        place = column_s[0, s]
        x = place // CY
        y = place % CY
        half = y // 128
        lane = y % 128
        part = rhs.at[half]
        where = (pl.ds(x, LZ, stride=CX), slice(None))
        part[where] = part[where] + jnp.where(lanes8 == lane, flow[:, s : s + 1], 0.0)

    copies[inputs - 2].wait()

    def solve_block(b, carry):
        at = pl.multiple_of(b * 8, 8)
        right = [halves_of(rhs, pl.ds(j * CX + at, 8)) for j in range(LZ)]
        here = pl.ds(at, 8)
        for i in range(LZ):
            if first:
                rims[0, i, here, :] = inverse[i, 0, here, :]
                rims[1, i, here, :] = inverse[i, LZ - 1, here, :]
            total = inverse[i, 0, here, :] * right[0]
            for j in range(1, LZ):
                total = total + inverse[i, j, here, :] * right[j]
            solved[pl.ds(i * CX + at, 8), :] = total
            if i == 0:
                carried[1, here, :] = total
            if i == LZ - 1:
                low = lower[here, :]
                carried[0, here, :] = total + inverse[i, i, here, :] * low - low
        return carry

    for n in range(PARTS):
        copies[inputs - 1 + n].wait()
        lax.fori_loop(n * (CX // 8) // PARTS, (n + 1) * (CX // 8) // PARTS, solve_block, 0)
    for side, out in ((0, keep), (1, give)):
        out[...] = carried[:, rows_of(side), :]


def by_core(body):
    core = lax.axis_index("layer") % 2
    for own in range(2):
        pl.when(core == own)(functools.partial(body, own))


def pair_fixed_kernel(mine, other, out):
    def body(own):
        top, low = (mine, other) if own == 0 else (other, mine)
        out[0] = low[0] * top[0]
        out[1] = top[1] * low[1]
        out[2] = top[2] + top[1] * (low[2] - 1.0) * top[0]

    by_core(body)


def pair_kernel(mine, other, fixed_mine, fixed_other, out):
    def body(own):
        top, low = (mine, other) if own == 0 else (other, mine)
        fixed_top, fixed_low = (fixed_mine, fixed_other) if own == 0 else (fixed_other, fixed_mine)
        out[0] = fixed_low[0] * top[0] + low[0]
        out[1] = top[1] + fixed_top[1] * (low[1] + fixed_low[2] * top[0] - top[0])

    by_core(body)


def chain_kernel(*refs):
    cds, fixed, refs = refs[:4], refs[4:8], refs[8:]
    cd_mine, cd_other, fixed_mine, fixed_other, mine, give = refs
    me = lax.axis_index("layer")

    def position(own):
        chip, even = own // 2, own % 2 == 0
        cd_top, cd_low = (cd_mine, cd_other) if even else (cd_other, cd_mine)
        fixed_top, fixed_low = (fixed_mine, fixed_other) if even else (fixed_other, fixed_mine)
        out_top, out_low = (mine, give) if even else (give, mine)

        def block(b, carry):
            here = pl.ds(pl.multiple_of(b * 8, 8), 8)
            uppers = [jnp.zeros((8, CY), F32)]
            for c in range(3):
                d = (chip - c) % 4
                uppers.append(fixed[d][0, here, :] * uppers[-1] + cds[d][0, here, :])
            low = jnp.zeros((8, CY), F32)
            for c in range(3, chip, -1):
                d = (chip - c) % 4
                step = cds[d][1, here, :] + fixed[d][2, here, :] * uppers[c] - uppers[c]
                low = fixed[d][1, here, :] * low + step
            upper = uppers[chip]
            below = fixed_top[0, here, :] * upper + cd_top[0, here, :]
            step = cd_low[1, here, :] + fixed_low[2, here, :] * below - below
            out_top[0, here, :] = upper
            out_top[1, here, :] = fixed_low[1, here, :] * low + step
            out_low[0, here, :] = below
            out_low[1, here, :] = low
            return carry

        @pl.when(me == own)
        def _():
            lax.fori_loop(0, HALF // 8, block, 0)

    for own in range(GROUPS):
        position(own)


def sweep_kernel(last, mine, other, solved, rims, *refs):
    if last:
        (field,) = refs
    else:
        split, lower, xlo, xhi = refs

    def body(own):
        for side in range(2):
            ends = mine if side == own else other

            def block(b, carry):
                there = pl.ds(pl.multiple_of(b * 8, 8), 8)
                here = pl.ds(pl.multiple_of(side * HALF + b * 8, 8), 8)
                upper, low = ends[0, there, :], ends[1, there, :]
                for i in range(LZ):
                    span = pl.ds(pl.multiple_of(i * CX + side * HALF + b * 8, 8), 8)
                    value = solved[span, :] + rims[0, i, here, :] * upper + rims[1, i, here, :] * low
                    if last:
                        field[span, :] = value
                    else:
                        split[0, span, :] = value[:, :128]
                        split[1, span, :] = value[:, 128:]
                if not last:
                    lower[here, :] = low
                return carry

            lax.fori_loop(0, HALF // 8, block, 0)

    by_core(body)
    if not last:
        split_x_edges(split, xlo, xhi)


def params(mib=8.0):
    return pltpu.CompilerParams(vmem_limit_bytes=int(mib * 1024) * 1024)


def around(n, step):
    return [(i, (i + step) % n) for i in range(n)]


def from_sides(xlo, xhi):
    return (lax.ppermute(xhi, "gx", around(8, 1)), lax.ppermute(xlo, "gx", around(8, -1)))


def swapped(value):
    return lax.ppermute(value, "layer", [(i, i ^ 1) for i in range(GROUPS)])


def all_chips(value):
    return [value] + [lax.ppermute(value, "layer", around(GROUPS, 2 * d)) for d in range(1, 4)]


def whole(kernel, name, out_shape, *operands):
    return pl.pallas_call(
        kernel,
        out_shape=out_shape,
        in_specs=[VMEM] * len(operands),
        out_specs=jax.tree.map(lambda _: VMEM, out_shape),
        compiler_params=params(),
        name=name,
    )(*operands)


def shards(
    pressure,
    source,
    perm_x,
    perm_y,
    line_inverse,
    robin_below,
    tile_count,
    perf_owner,
    perf_well,
    perf_column,
    perf_index,
    well_rate,
):
    rows = LZ * CX
    pressure = pressure.reshape(rows, CY)
    source = source.reshape(rows, CY)
    inverse = line_inverse[0]
    lower = robin_below[0]
    owner = perf_owner[0].T
    index = perf_index[0].T

    kx = perm_x.reshape(rows, CY)
    ky = perm_y.reshape(rows, CY)
    *edges, y_edge, fixed, fixed_give = pl.pallas_call(
        edges_kernel,
        out_shape=(shape(16, CY), shape(16, CY), shape(16, 128), shape(3, HALF, CY), shape(3, HALF, CY)),
        in_specs=[ANY] * 4,
        out_specs=(VMEM,) * 5,
        scratch_shapes=[
            pltpu.VMEM((2, rows, 128), F32),
            pltpu.VMEM((LZ, 8, CY), F32),
            pltpu.VMEM((LZ, 8, CY), F32),
            pltpu.VMEM((rows, CY), F32),
            pltpu.SemaphoreType.DMA((11,)),
        ],
        compiler_params=params(EDGE_MIB),
        name="first_edges",
    )(pressure, perm_x, ky, inverse)
    sides = from_sides(*edges)
    fixed_other = swapped(fixed_give)
    fixed_pair = whole(pair_fixed_kernel, "pair_fixed", shape(3, HALF, CY), fixed, fixed_other)
    fixed_chips = all_chips(fixed_pair)
    partials, at_slots, live, wells = pl.pallas_call(
        wells_first_kernel,
        out_shape=(shape(3 * TILES, 4, 128), shape(LZ, 128), shape(LZ, 128), shape(1, 128)),
        in_specs=[ANY] * 8,
        out_specs=(VMEM,) * 4,
        scratch_shapes=[
            pltpu.VMEM((2, rows, 128), F32),
            pltpu.VMEM((16, 128), F32),
            pltpu.VMEM((LZ, SLOTS), F32),
            pltpu.VMEM((1, SLOTS), jnp.int32),
            pltpu.VMEM((1, SLOTS), jnp.int32),
            pltpu.VMEM((1, 8), F32),
            pltpu.SMEM((1, SLOTS), jnp.int32),
            pltpu.SMEM((1, 1), jnp.int32),
            pltpu.SemaphoreType.DMA((9,)),
        ],
        compiler_params=params(WELLS_MIB),
        name="first_wells",
    )(y_edge, pressure, index, owner, perf_well, well_rate, perf_column, tile_count)
    field = pressure
    k_sides = sides
    own_edges = (y_edge, *edges)
    ky_sides = sums = None
    for sweep_step in range(ITERS):
        first, last = sweep_step == 0, sweep_step == ITERS - 1
        if first:
            partials, fixed_pair = lax.optimization_barrier((partials, fixed_pair))
        spread = lax.all_to_all(partials, ("gx", "gy"), split_axis=0, concat_axis=0, tiled=True)
        if first:
            spread, *fixed_chips = lax.optimization_barrier((spread, *fixed_chips))
        small = sides if first else (*sides, *k_sides, *ky_sides, sums)
        rhs = pl.pallas_call(
            functools.partial(lateral_kernel, first),
            out_shape=shape(2, rows, 128),
            in_specs=[ANY] * 4,
            out_specs=VMEM,
            scratch_shapes=[pltpu.VMEM((2, rows, 128), F32)]
            + [pltpu.VMEM((rows, CY), F32)] * 3
            + [pltpu.SemaphoreType.DMA((5,))],
            compiler_params=params(LATERAL_MIB),
            cost_estimate=pl.CostEstimate(
                flops=17 * rows * CY, bytes_accessed=5 * 4 * rows * CY, transcendentals=0
            ),
            name="lateral",
        )(field, kx, ky, source)
        operands = (perf_column, spread, live, wells, at_slots, *own_edges, *small, rhs, lower, inverse)
        held = [pltpu.VMEM(value.shape, value.dtype) for value in operands]
        solved, carried, give, *small = pl.pallas_call(
            functools.partial(solve_kernel, first, len(operands)),
            out_shape=(shape(rows, CY), shape(2, HALF, CY), shape(2, HALF, CY))
            + ((shape(2, 128), shape(8, 128), shape(8, 128), shape(2, LZ, CX, CY)) if first else (shape(LZ, SLOTS),)),
            in_specs=[ANY] * len(operands),
            out_specs=(VMEM,) * (7 if first else 4),
            scratch_shapes=held
            + [
                pltpu.VMEM((2, CX, CY), F32),
                pltpu.SMEM((1, SLOTS), jnp.int32),
                pltpu.SemaphoreType.DMA((len(operands) + PARTS - 1,)),
            ],
            compiler_params=params(SOLVE_MIB),
            name="solve_lines",
        )(*operands)
        if first:
            *small, rims = small
        other = swapped(give)
        chips = all_chips(whole(pair_kernel, "pair", shape(2, HALF, CY), carried, other, fixed, fixed_other))
        ends, ends_give = whole(
            chain_kernel,
            "chain",
            (shape(2, HALF, CY),) * 2,
            *(*chips, *fixed_chips, carried, other, fixed, fixed_other),
        )
        planes = (ends, swapped(ends_give), solved, rims)
        if last:
            (field,) = whole(functools.partial(sweep_kernel, True), "sweep_last", (shape(rows, CY),), *planes)
            (flow,) = small
            break
        sums, *ky_sides = small
        field, lower, *edges = whole(
            functools.partial(sweep_kernel, False),
            "sweep_mid",
            (shape(2, rows, 128), shape(CX, CY), shape(8, CY), shape(8, CY)),
            *planes,
        )
        sides = from_sides(*edges)
        partials, at_slots = pl.pallas_call(
            wells_next_kernel,
            out_shape=(shape(3 * TILES, 2, 128), shape(LZ, 128)),
            in_specs=[VMEM] + [ANY] * 4,
            out_specs=(VMEM,) * 2,
            scratch_shapes=[
                pltpu.VMEM((LZ, 128), F32),
                pltpu.VMEM((1, 128), F32),
                pltpu.VMEM((1, 8), F32),
                pltpu.SMEM((1, SLOTS), jnp.int32),
                pltpu.SemaphoreType.DMA((4,)),
            ],
            compiler_params=params(),
            name="next_wells",
        )(field, live, wells, well_rate, perf_column)
    return (field.reshape(LZ, CX, CY), flow.T[None])


def solution(mesh):
    placed = (
        P("layer", "gx", "gy"),
        P("layer", "gx", "gy"),
        P("layer", "gx", "gy"),
        P("layer", "gx", "gy"),
        P("layer", None, None, "gx", "gy"),
        P("layer", "gx", "gy"),
        P("layer", ("gx", "gy")),
        P("layer", ("gx", "gy"), None),
        P("layer", ("gx", "gy")),
        P("layer", ("gx", "gy")),
        P("layer", ("gx", "gy"), None),
        P("layer", ("gx", "gy")),
    )
    return jax.shard_map(
        shards,
        mesh=mesh,
        in_specs=placed,
        out_specs=(P("layer", "gx", "gy"), P("layer", ("gx", "gy"), None)),
        check_vma=False,
    )
```
